512 devices in a mesh: gx: 8 (over z), gy: 8 (over y), gz: 8 (over x, core).
Axes of the slice: x: 4, y: 8, z: 8, core: 2. Of those that a mesh axis runs over, the one named last changes fastest.
Arguments:
- source_term: float32 [128, 256, 1024], P('gx', 'gy', 'gz'), may hold values from -4 to 4
- conductivity: float32 [128, 256, 1024], P('gx', 'gy', 'gz'), may hold values from 0.5 to 8
Outputs:
- solution: float32 [128, 256, 1024], P('gx', 'gy', 'gz')
The draws below stay inside these ranges and needn't reach their ends.
All inputs are finite; a program needn't handle non-finite values.
Results may differ from the reference program's by a relative error of at most 0.0003.
Values sent between devices are 32-bit elements; how exact they have to be, the bound alone decides.
A program may use at most 128 MiB of HBM per device.

```python
import math
import jax
import jax.numpy as jnp
from jax import lax

SWEEPS = 2
BOTTOM = 16
NX = 128
NY = 256
NZ = 1024


def draw_source_term(key, part):
    key = jax.random.fold_in(key, 11)
    return jnp.clip(jax.random.normal(key, (NX, NY, NZ), jnp.float32), -4.0, 4.0)


def block_scale(key, dims, cuts, low, high):
    def one(position, blocks):
        draws = jax.random.uniform(jax.random.fold_in(jax.random.fold_in(key, 6), position), (blocks,), jnp.float32, low / len(cuts), high / len(cuts))
        return jnp.repeat(jnp.exp(draws), dims[position] // blocks).reshape((-1,) + (1,) * (len(dims) - position - 1))

    gain = one(*cuts[0])
    for cut in cuts[1:]:
        gain = gain * one(*cut)
    return gain


def setup_inputs(seed: int = 0) -> dict:
    arg_keys = jax.random.split(jax.random.key(seed), 3)
    source_term = draw_source_term(jax.random.fold_in(arg_keys[2], 71), 0)
    conductivity = jnp.clip(jnp.exp(math.log(8.0) - 2.7725887 * jax.random.uniform(arg_keys[1], (NX, NY, NZ), jnp.float32) ** block_scale(arg_keys[1], (NX, NY, NZ), ((0, 8), (1, 8), (2, 8)), -0.2, 0.2)), 0.5, 8.0)
    return {"source_term": source_term, "conductivity": conductivity}


def coefficients(padded, factor):
    centre = padded[1:-1, 1:-1, 1:-1]
    lower_x = factor * 0.5 * (centre + padded[:-2, 1:-1, 1:-1])
    upper_x = factor * 0.5 * (centre + padded[2:, 1:-1, 1:-1])
    lower_y = factor * 0.5 * (centre + padded[1:-1, :-2, 1:-1])
    upper_y = factor * 0.5 * (centre + padded[1:-1, 2:, 1:-1])
    lower_z = factor * 0.5 * (centre + padded[1:-1, 1:-1, :-2])
    upper_z = factor * 0.5 * (centre + padded[1:-1, 1:-1, 2:])
    diagonal = lower_x + upper_x + lower_y + upper_y + lower_z + upper_z
    return (lower_x, upper_x, lower_y, upper_y, lower_z, upper_z, diagonal)


def neighbours(stencil, padded):
    summed = stencil[0] * padded[:-2, 1:-1, 1:-1] + stencil[1] * padded[2:, 1:-1, 1:-1]
    summed = summed + stencil[2] * padded[1:-1, :-2, 1:-1] + stencil[3] * padded[1:-1, 2:, 1:-1]
    summed = summed + stencil[4] * padded[1:-1, 1:-1, :-2] + stencil[5] * padded[1:-1, 1:-1, 2:]
    return summed


def coarsen(values):
    size_x, size_y, size_z = values.shape
    blocks = values.reshape(size_x // 2, 2, size_y // 2, 2, size_z // 2, 2)
    return jnp.mean(blocks, axis=(1, 3, 5))


def prolong(values):
    return jnp.repeat(jnp.repeat(jnp.repeat(values, 2, axis=0), 2, axis=1), 2, axis=2)


def parity(extent, starts, margin):
    summed = jnp.zeros(extent, jnp.int32)
    for axis_no in range(3):
        summed = summed + lax.broadcasted_iota(jnp.int32, extent, axis_no) + (starts[axis_no] - margin)
    return summed % 2 == 0


def pad_zero(values, width):
    return jnp.pad(values, width)


def relaxation(iterate, source, stencil, red_cells, padder):
    for colour_mask in (red_cells, jnp.logical_not(red_cells)):
        padded = padder(iterate, 1)
        updated = (source + neighbours(stencil, padded)) / stencil[6]
        iterate = jnp.where(colour_mask, updated, iterate)
    return iterate


def reference(source_term, conductivity):
    conduct_levels = [conductivity]
    for level_no in range(4):
        conduct_levels.append(coarsen(conduct_levels[-1]))
    stencils = [coefficients(jnp.pad(conduct_grid, 1), 0.25 ** level_no) for level_no, conduct_grid in enumerate(conduct_levels)]
    colours = [parity(conduct_grid.shape, (0, 0, 0), 0) for conduct_grid in conduct_levels]
    sources = [source_term]
    states = []
    for level_no in range(4):
        iterate = jnp.zeros_like(sources[level_no])
        for sweep_no in range(SWEEPS):
            iterate = relaxation(iterate, sources[level_no], stencils[level_no], colours[level_no], pad_zero)
        stencil = stencils[level_no]
        residual = sources[level_no] - (stencil[6] * iterate - neighbours(stencil, pad_zero(iterate, 1)))
        states.append(iterate)
        sources.append(coarsen(residual))

    def bottom_sweep(sweep_no, current):
        return relaxation(current, sources[4], stencils[4], colours[4], pad_zero)

    iterate = lax.fori_loop(0, BOTTOM, bottom_sweep, jnp.zeros_like(sources[4]))
    for level_no in (3, 2, 1, 0):
        iterate = states[level_no] + prolong(iterate)
        for sweep_no in range(SWEEPS):
            iterate = relaxation(iterate, sources[level_no], stencils[level_no], colours[level_no], pad_zero)
    return iterate
```

```python
import functools

import jax
import jax.numpy as jnp
from jax import lax
from jax.experimental import pallas as pl
from jax.experimental.pallas import tpu as pltpu
from jax.sharding import PartitionSpec as P

MESH = pl.DeviceIdType.MESH
AXES = ("gx", "gy", "gz")
N = 8
BOTTOM = 16
F32 = jnp.float32


def iota(shape, axis):
    return lax.broadcasted_iota(jnp.int32, shape, axis)


def dot(a, b):
    return lax.dot_general(
        a, b, (((1,), (0,)), ((), ())),
        precision=lax.Precision.HIGHEST, preferred_element_type=F32,
    )


def rotate(a, shift, axis):
    shift = shift % a.shape[axis]
    return a if shift == 0 else pltpu.roll(a, shift, axis)


class Level:
    def __init__(self, refs, h, scale, closed):
        (self.f, self.k, self.wx, self.wy, self.wz, self.ir, self.ib, self.d, self.ur, self.ub) = refs
        self.planes, self.rows, self.lanes = self.ur.shape
        self.h, self.scale, self.closed = (h, scale, closed)

    def prepare(self, lo, hi):
        shape = (self.rows, self.lanes)
        hs = 0.5 * self.scale

        def body(p, carry):
            k = self.k[p]
            below, above = self.k[p - 1], self.k[p + 1]
            kyl, kyu = rotate(k, 1, 0), rotate(k, -1, 0)
            kzl, kzu = rotate(k, 1, 1), rotate(k, -1, 1)
            wy, wz = hs * (k + kyl), hs * (k + kzl)
            if self.closed:
                row, lane = iota(shape, 0), iota(shape, 1)
                kyl = jnp.where(row == 0, 0.0, kyl)
                kyu = jnp.where(row == self.rows - 1, 0.0, kyu)
                kzl = jnp.where(lane == 0, 0.0, kzl)
                kzu = jnp.where(lane == self.lanes - 1, 0.0, kzu)
                wy = jnp.where(row == 0, 0.0, wy)
                wz = jnp.where(lane == 0, 0.0, wz)
            diag = hs * (6.0 * k + below + above + kyl + kyu + kzl + kzu)
            inside = k > 0.0
            inv = jnp.where(inside, 1.0 / jnp.where(inside, diag, 1.0), 0.0)
            odd = (iota(shape, 0) + iota(shape, 1) + (p - self.h)) & 1
            red = jnp.where(odd == 0, inv, 0.0)
            self.wx[p] = hs * (k + below)
            self.wy[p] = wy
            self.wz[p] = wz
            self.ir[p] = red
            self.ib[p] = inv - red
            self.d[p] = diag
            return carry

        lax.fori_loop(lo, hi, body, 0)
        self.wx[hi] = hs * (self.k[hi] + self.k[hi - 1])

    def around(self, plane, p):
        u, wy, wz = plane(p), self.wy[p], self.wz[p]
        total = self.wx[p] * plane(p - 1) + self.wx[p + 1] * plane(p + 1)
        total = total + (wy * rotate(u, 1, 0) + rotate(wy * u, -1, 0))
        return total + (wz * rotate(u, 1, 1) + rotate(wz * u, -1, 1))

    def first(self, lo, hi):
        def body(p, carry):
            self.ur[p] = self.ir[p] * self.f[p]
            return carry

        lax.fori_loop(lo, hi, body, 0)

    def half(self, target, inverse, other, lo, hi):
        def body(p, carry):
            target[p] = inverse[p] * (self.f[p] + self.around(lambda q: other[q], p))
            return carry

        lax.fori_loop(lo, hi, body, 0, unroll=2)

    def red(self, lo, hi, black):
        self.half(self.ur, self.ir, black, lo, hi)

    def black(self, lo, hi, black):
        self.half(black, self.ib, self.ur, lo, hi)

    def residual_pairs(self, first, count, rows, out):
        def one(p):
            u = self.ur[p] + self.ub[p]
            applied = self.d[p] * u - self.around(lambda q: self.ur[q] + self.ub[q], p)
            return (self.f[p] - applied)[rows[0] : rows[1], 0:128]

        def body(i, carry):
            out[i] = one(first + 2 * i) + one(first + 2 * i + 1)
            return carry

        lax.fori_loop(0, count, body, 0)


def row_pairs(ref, count):
    return ref[pl.ds(0, count, 2), :] + ref[pl.ds(1, count, 2), :]


def kernel(f_hbm, k_hbm, out_ref, *scratch):
    names = list(SCRATCH)
    s = dict(zip(names, scratch))
    ix, iy, iz = (lax.axis_index(a) for a in AXES)
    me = (ix, iy, iz)

    def device(off):
        return tuple(lax.rem(me[a] + (off[a] + N), N) for a in range(3))

    send, recv, dummy = s["send"], s["recv"], s["dummy"]
    sent = {}

    def push(src, dst, sem, off):
        pltpu.make_async_remote_copy(
            src_ref=src, dst_ref=dst, send_sem=send.at[sem], recv_sem=recv.at[sem],
            device_id=device(off), device_id_type=MESH,
        ).start()
        size = 1
        for d in src.shape:
            size *= d
        sent[sem] = sent.get(sem, 0) + size // 1024

    def wait(sems, sem):
        view = dummy.at[pl.ds(0, sent[sem])]
        pltpu.make_async_copy(view, view, sems.at[sem]).wait()

    fk0, fk1, fk2, fk3 = s["fk0"], s["fk1"], s["fk2"], s["fk3"]

    def level(no, fk, h, closed):
        refs = [fk.at[0], fk.at[1]] + [s[f"{n}{no}"] for n in ("wx", "wy", "wz", "ir", "ib", "d", "ur", "ub")]
        return Level(refs, h, 0.25**no, closed)

    l0, l1 = level(0, fk0, 5, False), level(1, fk1, 6, False)
    l2, l3 = level(2, fk2, 8, False), level(3, fk3, 4, True)

    own0 = [fk0.at[a, pl.ds(5, 16), pl.ds(8, 32), pl.ds(0, 128)] for a in range(2)]
    loads = [pltpu.make_async_copy(r, own0[a], s["load"].at[a]) for a, r in enumerate((f_hbm, k_hbm))]
    for c in loads:
        c.start()
    near = [(a, b, c) for a in (-1, 0, 1) for b in (-1, 0, 1) for c in (-1, 0, 1) if (a, b, c) != (0, 0, 0)]
    wide = [(a, b, c) for a in (-2, -1, 0, 1, 2) for b in (-1, 0, 1) for c in (-1, 0, 1) if (a, b, c) != (0, 0, 0)]
    lines = []
    for a in range(3):
        for d in range(1, N):
            lines.append(tuple((d if d <= 4 else d - N) if b == a else 0 for b in range(3)))
    partners = wide + [o for o in lines if o not in wide]
    barrier = pltpu.get_barrier_semaphore()
    for off in partners:
        pl.semaphore_signal(barrier, inc=1, device_id=device(off), device_id_type=MESH)
    for c in loads:
        c.wait()
    pl.semaphore_wait(barrier, len(partners))

    def pack(own, zp, planes, length):
        left = right = None
        for p in range(planes):
            v = own(p)
            group = iota(v.shape, 1) // 8 == p
            a, b = rotate(v, 8 * p, 1), rotate(v, 8 * p - (length - 8), 1)
            left = a if p == 0 else jnp.where(group, a, left)
            right = b if p == 0 else jnp.where(group, b, right)
        zp[0], zp[1] = left, right

    def slabs(src, dst, h, nx, ny, lead, sem):
        for sx in (-1, 0, 1):
            xs = {1: (h + nx - h, h, 0), -1: (h, h, h + nx), 0: (h, nx, h)}[sx]
            for sy in (-1, 0, 1):
                if (sx, sy) == (0, 0):
                    continue
                ys = {1: (8 + ny - 8, 8, 0), -1: (8, 8, 8 + ny), 0: (8, ny, 8)}[sy]
                a = lead + (pl.ds(xs[0], xs[1]), pl.ds(ys[0], ys[1]), pl.ds(0, 128))
                b = lead + (pl.ds(xs[2], xs[1]), pl.ds(ys[2], ys[1]), pl.ds(0, 128))
                push(src.at[a], dst.at[b], sem, (sx, sy, 0))

    def edges(zp, zr, ny, lead, sem):
        for sz in (-1, 1):
            side = 1 if sz == 1 else 0
            for sx in (-1, 0, 1):
                for sy in (-1, 0, 1):
                    ys = {1: (ny - 8, 8, 0), -1: (0, 8, 8 + ny), 0: (0, ny, 8)}[sy]
                    a = (side,) + lead + (pl.ds(ys[0], ys[1]),)
                    b = (1 - side, 1 - sx) + lead + (pl.ds(ys[2], ys[1]),)
                    push(zp.at[a], zr.at[b], sem, (sx, sy, sz))

    def ghost(zr, lead, p, h, nx, base):
        slot, q = (0, nx - h + p) if p < h else (1, p - h) if p < h + nx else (2, p - h - nx)
        right = rotate(zr[(1, slot) + lead], base - 8 * q, 1)
        left = rotate(zr[(0, slot) + lead], 120 - 8 * q, 1)
        lane = iota(right.shape, 1)
        return jnp.where((lane >= base) & (lane < base + 8), right, jnp.where(lane >= 120, left, 0.0))

    def flag(condition):
        return jnp.where(condition, 1.0, 0.0)

    def inside_yz(rows, ny, own_lanes, right_end, lanes):
        row, lane = iota((rows, lanes), 0), iota((rows, lanes), 1)
        in_y = ((row >= 8) | (iy > 0)) & ((row < 8 + ny) | (iy < N - 1))
        in_z = (lane < own_lanes) | ((lane < right_end) & (iz < N - 1)) | ((lane >= right_end) & (iz > 0))
        return jnp.where(in_y & in_z, 1.0, 0.0)

    def inside_x(p, h, nx):
        return flag(ix > 0) if p < h else flag(ix < N - 1) if p >= h + nx else 1.0

    for a in range(2):
        pack(lambda p, a=a: fk0[a, 5 + p, 8:40, 0:128], s["zp0"].at[:, a], 16, 128)
    slabs(fk0, fk0, 5, 16, 32, (slice(None),), 0)
    edges(s["zp0"], s["zr0"], 32, (slice(None),), 1)

    lane_r, lane_c = iota((128, 128), 0), iota((128, 128), 1)
    halve1 = jnp.where((lane_r // 2 == lane_c), 0.125, 0.0)
    halve2 = jnp.where((lane_r // 2 == lane_c) & (lane_c < 32), 0.125, 0.0)

    pair0, pair1, pair2, pair3 = s["pair0"], s["pair1"], s["pair2"], s["pair3"]

    def coarse1():
        flat = pair0.reshape(256, 128)
        return dot(row_pairs(flat, 128), halve1).reshape(8, 16, 128)

    def coarse2():
        flat = pair1.reshape(64, 128)
        return dot(row_pairs(flat, 32), halve2).reshape(4, 8, 128)

    def packed2(value):
        total = value[0]
        for q in range(1, 4):
            total = total + rotate(value[q], 32 * q, 1)
        return total

    row8, col8 = iota((8, 8), 0), iota((8, 8), 1)

    def coarse3():
        place_rows = jnp.where(row8 == 4 * lax.rem(iy, 2) + col8 // 2, 1.0, 0.0)
        total = None
        for dx in range(2):
            group = lax.rem(2 * ix + dx, 8)
            place = jnp.where((lane_r < 32) & (lane_c == 16 * group + lane_r // 2), 0.125, 0.0)
            part = dot(dot(place_rows, pair2[dx]), place)
            total = part if total is None else total + part
        return total

    def gather(tile, g1, g2, g3, sem):
        g1[ix] = tile
        for d in range(1, N):
            push(g1.at[ix], g1.at[ix], sem, (d, 0, 0))
        yield
        wait(recv, sem)
        g2[iy, 0] = g1[0] + g1[1] + g1[2] + g1[3]
        g2[iy, 1] = g1[4] + g1[5] + g1[6] + g1[7]
        for d in range(1, N):
            push(g2.at[iy], g2.at[iy], sem + 1, (0, d, 0))
        yield
        wait(recv, sem + 1)
        for o in range(4):
            for h in range(2):
                g3[iz, h, o] = g2[2 * o, h] + g2[2 * o + 1, h]
        for d in range(1, N):
            push(g3.at[iz], g3.at[iz], sem + 2, (0, 0, d))
        yield
        wait(recv, sem + 2)

    def unpack3(g3, out):
        group = iota((32, 128), 1) // 16
        for h in range(2):
            blocks = [g3[j, h].reshape(32, 128) for j in range(8)]
            for g in range(8):
                total = rotate(blocks[0], 16 * (0 - g), 1)
                for j in range(1, 8):
                    total = jnp.where(group == j, rotate(blocks[j], 16 * (j - g), 1), total)
                out[4 + 8 * h + g] = total

    for i in range(8):
        pair0[i] = fk0[1, 5 + 2 * i, 8:40, 0:128] + fk0[1, 6 + 2 * i, 8:40, 0:128]
    k1_own = coarse1()
    fk1[1, 6:14, 8:24, :] = k1_own
    for i in range(4):
        pair1[i] = k1_own[2 * i] + k1_own[2 * i + 1]
    k2_own = coarse2()
    s["r2"][2, 1, 1, 1] = packed2(k2_own)
    for i in range(2):
        pair2[i] = k2_own[2 * i] + k2_own[2 * i + 1]
    k_gather = gather(coarse3(), s["gk1"], s["gk2"], s["gk3"], 10)
    next(k_gather)

    for lev in (l0, l1, l2):
        for ref in (lev.ur, lev.ub):
            for p in (0, lev.planes - 1):
                ref[p] = jnp.zeros((lev.rows, lev.lanes), F32)
    for p in (0, 1, 2, 3, 20, 21, 22, 23):
        for ref in (l3.ur, l3.ub, fk3.at[0], fk3.at[1]):
            ref[p] = jnp.zeros((32, 128), F32)

    wait(recv, 0)
    wait(recv, 1)
    wait(send, 0)
    myz0 = inside_yz(48, 32, 128, 192, 256)
    for p in range(26):
        for a in range(2):
            g = ghost(s["zr0"], (a,), p, 5, 16, 0)
            if a == 1:
                sx = inside_x(p, 5, 16)
                fk0[1, p, :, 0:128] = fk0[1, p, :, 0:128] * (myz0[:, 0:128] * sx)
                g = g * (myz0[:, 128:256] * sx)
            fk0[a, p, :, 128:256] = g
    l0.prepare(1, 25)
    next(k_gather)
    l0.first(1, 25)
    zero0 = jnp.zeros((48, 256), F32)
    l0.black(2, 24, l0.ub)
    l0.ub[1] = zero0
    l0.ub[24] = zero0
    l0.red(3, 23, l0.ub)
    l0.black(4, 22, l0.ub)
    next(k_gather)
    l0.residual_pairs(5, 8, (8, 40), pair0)
    f1_own = coarse1()
    fk1[0, 6:14, 8:24, :] = f1_own

    for a in range(2):
        pack(lambda p, a=a: fk1[a, 6 + p, 8:24, :], s["zp1"].at[:, a], 8, 64)
    slabs(fk1, fk1, 6, 8, 16, (slice(None),), 2)
    edges(s["zp1"], s["zr1"], 16, (slice(None),), 3)
    pack(lambda p: l0.ub[5 + p, 8:40, 0:128], s["zpu0"], 16, 128)
    slabs(l0.ub, s["v0"], 5, 16, 32, (), 4)
    edges(s["zpu0"], s["zru0"], 32, (), 5)
    s["v0"][5:21, 8:40, 0:128] = l0.ub[5:21, 8:40, 0:128]

    wait(recv, 2)
    wait(recv, 3)
    wait(send, 2)
    myz1 = inside_yz(32, 16, 64, 96, 128)
    lane32 = iota((32, 128), 1)
    for p in range(20):
        for a in range(2):
            v = jnp.where(lane32 < 64, fk1[a, p], ghost(s["zr1"], (a,), p, 6, 8, 64))
            if a == 1:
                v = v * (myz1 * inside_x(p, 6, 8))
            fk1[a, p] = v
    l1.prepare(1, 19)
    l1.first(2, 18)
    l1.black(3, 17, l1.ub)
    l1.ub[2] = jnp.zeros((32, 128), F32)
    l1.ub[17] = jnp.zeros((32, 128), F32)
    l1.red(4, 16, l1.ub)
    l1.black(5, 15, l1.ub)
    l1.residual_pairs(6, 4, (8, 24), pair1)
    s["r2"][2, 1, 1, 0] = packed2(coarse2())

    r2 = s["r2"]
    for off in wide:
        push(r2.at[2, 1, 1], r2.at[2 - off[0], 1 - off[1], 1 - off[2]], 6, off)
    pack(lambda p: l1.ub[6 + p, 8:24, :], s["zpu1"], 8, 64)
    slabs(l1.ub, s["v1"], 6, 8, 16, (), 7)
    edges(s["zpu1"], s["zru1"], 16, (), 8)
    s["v1"][6:14, 8:24, :] = l1.ub[6:14, 8:24, :]

    for _ in k_gather:
        pass
    unpack3(s["gk3"], fk3.at[1])
    l3.prepare(4, 20)

    wait(recv, 6)
    lane8 = iota((8, 128), 1)

    def unpack2(block, p, by):
        b, q = divmod(p, 4)
        own = rotate(block(b, by, 1), -32 * q, 1)
        right = rotate(block(b, by, 2), 32 * (1 - q), 1)
        left = rotate(block(b, by, 0), 32 * (3 - q), 1)
        v = jnp.where(lane8 < 32, own, jnp.where(lane8 < 64, right, jnp.where(lane8 >= 96, left, 0.0)))
        return v

    row24, lane24 = iota((24, 128), 0), iota((24, 128), 1)
    in_y = ((row24 >= 8) | (iy > 0)) & ((row24 < 16) | (iy < N - 1))
    in_z = (lane24 < 32) | ((lane24 < 64) & (iz < N - 1)) | ((lane24 >= 96) & (iz > 0))
    myz2 = jnp.where(in_y & in_z, 1.0, 0.0)
    for p in range(20):
        b = p // 4
        sx = [flag(ix > 1), flag(ix > 0), 1.0, flag(ix < N - 1), flag(ix < N - 2)][b]
        for a in range(2):
            for by in range(3):
                v = unpack2(lambda i, j, k, a=a: r2[i, j, k, a], p, by)
                if a == 1:
                    v = v * (myz2[8 * by : 8 * by + 8] * sx)
                fk2[a, p, 8 * by : 8 * by + 8, :] = v
    l2.prepare(1, 19)
    l2.first(4, 16)
    l2.black(5, 15, l2.ub)
    l2.ub[4] = jnp.zeros((24, 128), F32)
    l2.ub[15] = jnp.zeros((24, 128), F32)
    l2.red(6, 14, l2.ub)
    l2.black(7, 13, l2.ub)
    l2.residual_pairs(8, 2, (8, 16), pair2)
    f_gather = gather(coarse3(), s["gf1"], s["gf2"], s["gf3"], 13)
    next(f_gather)
    ru2 = s["ru2"]
    total = l2.ub[8, 8:16, :]
    total = jnp.where(lane8 < 32, total, 0.0)
    for q in range(1, 4):
        total = total + rotate(jnp.where(lane8 < 32, l2.ub[8 + q, 8:16, :], 0.0), 32 * q, 1)
    ru2[2, 1, 1] = total
    for off in wide:
        push(ru2.at[2, 1, 1], ru2.at[2 - off[0], 1 - off[1], 1 - off[2]], 9, off)
    pair3_flat = pair3.reshape(8 * 32, 128)

    def coarse4():
        rows = row_pairs(pair3_flat, 128).reshape(8, 16, 128)
        out = None
        for h in range(2):
            place = jnp.where(lane_c == 64 * h + lane_r // 2, 0.125, 0.0)
            part = dot(rows[4 * h : 4 * h + 4].reshape(64, 128), place)
            out = part if out is None else out + part
        return out.reshape(4, 16, 128)

    for i in range(8):
        pair3[i] = fk3[1, 4 + 2 * i] + fk3[1, 5 + 2 * i]
    k4 = coarse4()
    shape4 = (4, 16, 128)
    row4, lane4 = iota(shape4, 1), iota(shape4, 2)
    z4 = lane4 & 63

    def cat(parts):
        return jnp.concatenate(parts, axis=0)

    def x_below(v):
        return cat([rotate(v[3], 64, 1)[None], v[0:3]])

    def x_above(v):
        return cat([v[1:4], rotate(v[0], 64, 1)[None]])

    def roll3(v, shift, axis):
        flat = [rotate(v[i], shift, axis)[None] for i in range(4)]
        return cat(flat)

    plane4 = iota(shape4, 0)
    first_x = (plane4 == 0) & (lane4 < 64)
    last_x = (plane4 == 3) & (lane4 >= 64)
    hs4 = 0.5 * 0.25**4
    kxl, kxu = jnp.where(first_x, 0.0, x_below(k4)), jnp.where(last_x, 0.0, x_above(k4))
    kyl = jnp.where(row4 == 0, 0.0, roll3(k4, 1, 0))
    kyu = jnp.where(row4 == 15, 0.0, roll3(k4, -1, 0))
    kzl = jnp.where(z4 == 0, 0.0, roll3(k4, 1, 1))
    kzu = jnp.where(z4 == 63, 0.0, roll3(k4, -1, 1))
    w4 = s["w4"]
    inv4 = 1.0 / (hs4 * (6.0 * k4 + kxl + kxu + kyl + kyu + kzl + kzu))
    odd4 = (plane4 + row4 + lane4) & 1
    w4[0] = jnp.where(first_x, 0.0, hs4 * (k4 + kxl))
    w4[1] = jnp.where(last_x, 0.0, hs4 * (k4 + kxu))
    w4[2] = jnp.where(row4 == 0, 0.0, hs4 * (k4 + kyl))
    w4[3] = jnp.where(row4 == 15, 0.0, hs4 * (k4 + kyu))
    w4[4] = jnp.where(z4 == 0, 0.0, hs4 * (k4 + kzl))
    w4[5] = jnp.where(z4 == 63, 0.0, hs4 * (k4 + kzu))
    w4[6] = jnp.where(odd4 == 0, inv4, 0.0)
    w4[7] = jnp.where(odd4 == 1, inv4, 0.0)

    for _ in f_gather:
        pass
    unpack3(s["gf3"], fk3.at[0])
    l3.first(4, 20)
    l3.black(4, 20, l3.ub)
    l3.red(4, 20, l3.ub)
    l3.black(4, 20, l3.ub)
    l3.residual_pairs(4, 8, (0, 32), pair3)
    f4 = coarse4()
    w4[8] = f4

    def around4(v):
        total = w4[0] * x_below(v) + w4[1] * x_above(v)
        total = total + (w4[2] * roll3(v, 1, 0) + w4[3] * roll3(v, -1, 0))
        return total + (w4[4] * roll3(v, 1, 1) + w4[5] * roll3(v, -1, 1))

    def bottom(i, carry):
        black = carry[1]
        red = w4[6] * (w4[8] + around4(black))
        black = w4[7] * (w4[8] + around4(red))
        return (red, black)

    zero4 = jnp.zeros(shape4, F32)
    red4, black4 = lax.fori_loop(0, BOTTOM, bottom, (zero4, zero4))
    u4 = red4 + black4

    for h in range(2):
        place = jnp.where(lane_r == 64 * h + lane_c // 2, 1.0, 0.0)
        wide4 = dot(u4.reshape(64, 128), place)
        flat = pair3_flat
        flat[pl.ds(128 * h, 64, 2), :] = wide4
        flat[pl.ds(128 * h + 1, 64, 2), :] = wide4

    def add(lev, black, p, corr):
        black[p] = jnp.where(lev.ib[p] > 0.0, black[p] + corr, 0.0)

    for i in range(8):
        corr = pair3[i]
        add(l3, l3.ub, 4 + 2 * i, corr)
        add(l3, l3.ub, 5 + 2 * i, corr)
    for _ in range(2):
        l3.red(4, 20, l3.ub)
        l3.black(4, 20, l3.ub)

    wait(recv, 9)
    v2 = s["v2"]
    for p in range(20):
        for by in range(3):
            v2[p, 8 * by : 8 * by + 8, :] = unpack2(lambda i, j, k: ru2[i, j, k], p, by)
    zoff = jnp.where(lane_c < 64, lane_c, lane_c - 128)
    source_lane = 16 * iz + ((zoff + 128) // 2 - 64)
    spread_z = jnp.where((lane_r == source_lane) & ((lane_c < 64) | (lane_c >= 96)), 1.0, 0.0)
    spread_y = jnp.where(iota((24, 32), 1) == 4 * iy - 4 + iota((24, 32), 0) // 2, 1.0, 0.0)
    for j in range(10):
        p3 = 2 * ix + j
        u3 = l3.ur[p3] + l3.ub[p3]
        corr = dot(spread_y, dot(u3, spread_z))
        add(l2, v2, 2 * j, corr) if j > 0 else None
        add(l2, v2, 2 * j + 1, corr)
    l2.red(2, 18, v2)
    l2.black(3, 17, v2)
    l2.red(4, 16, v2)
    l2.black(5, 15, v2)

    wait(recv, 7)
    wait(recv, 8)
    v1 = s["v1"]
    for p in range(20):
        v1[p] = jnp.where(lane32 < 64, v1[p], ghost(s["zru1"], (), p, 6, 8, 64))
    spread1 = jnp.where(lane_r == jnp.where(lane_c >= 96, 64 + lane_c // 2, lane_c // 2), 1.0, 0.0)
    up1 = s["up1"]
    coarse = (l2.ur[5:15] + v2[5:15]).reshape(240, 128)
    up1[...] = dot(coarse, spread1).reshape(10, 24, 128)
    tall1 = s["tall1"]
    for j in range(10):
        part = up1[j, 4:20, :]
        tall1[pl.ds(0, 16, 2), :] = part
        tall1[pl.ds(1, 16, 2), :] = part
        corr = tall1[...]
        for p in (2 * j, 2 * j + 1):
            if 0 < p < 19:
                add(l1, v1, p, corr)
    l1.red(1, 19, v1)
    l1.black(2, 18, v1)
    l1.red(3, 17, v1)
    l1.black(4, 16, v1)

    wait(recv, 4)
    wait(recv, 5)
    v0 = s["v0"]
    for p in range(1, 25):
        v0[p, :, 128:256] = ghost(s["zru0"], (), p, 5, 16, 0)
    spread0 = jnp.where(iota((128, 256), 0) == iota((128, 256), 1) // 2, 1.0, 0.0)
    up0 = s["up0"]
    coarse = (l1.ur[4:16] + v1[4:16]).reshape(384, 128)
    up0[...] = dot(coarse, spread0).reshape(12, 32, 256)
    tall0 = s["tall0"]
    for j in range(12):
        for t in range(2):
            part = up0[j, 4:28, 128 * t : 128 * t + 128]
            tall0[t, pl.ds(0, 24, 2), :] = part
            tall0[t, pl.ds(1, 24, 2), :] = part
        for t in range(2):
            corr = tall0[t]
            for p in (1 + 2 * j, 2 + 2 * j):
                lanes = slice(128 * t, 128 * t + 128)
                v0[p, :, lanes] = jnp.where(l0.ib[p, :, lanes] > 0.0, v0[p, :, lanes] + corr, 0.0)
    l0.red(2, 24, v0)
    l0.black(3, 23, v0)
    l0.red(4, 22, v0)
    l0.black(5, 21, v0)
    out_ref[...] = l0.ur[5:21, 8:40, 0:128] + v0[5:21, 8:40, 0:128]
    for sem in sorted(sent):
        if sem not in (0, 2):
            wait(send, sem)


def vmem(*shape):
    return pltpu.VMEM(shape, F32)


def scratch_shapes():
    shapes = {}
    for no, shape in enumerate([(26, 48, 256), (20, 32, 128), (20, 24, 128), (24, 32, 128)]):
        shapes[f"fk{no}"] = vmem(2, *shape)
        for name in ("wx", "wy", "wz", "ir", "ib", "d", "ur", "ub"):
            shapes[f"{name}{no}"] = vmem(*shape)
        if no < 3:
            shapes[f"v{no}"] = vmem(*shape)
    shapes["zp0"], shapes["zr0"] = vmem(2, 2, 32, 128), vmem(2, 3, 2, 48, 128)
    shapes["zpu0"], shapes["zru0"] = vmem(2, 32, 128), vmem(2, 3, 48, 128)
    shapes["zp1"], shapes["zr1"] = vmem(2, 2, 16, 128), vmem(2, 3, 2, 32, 128)
    shapes["zpu1"], shapes["zru1"] = vmem(2, 16, 128), vmem(2, 3, 32, 128)
    shapes["r2"], shapes["ru2"] = vmem(5, 3, 3, 2, 8, 128), vmem(5, 3, 3, 8, 128)
    for name in "kf":
        shapes[f"g{name}1"] = vmem(8, 8, 128)
        shapes[f"g{name}2"] = vmem(8, 2, 8, 128)
        shapes[f"g{name}3"] = vmem(8, 2, 4, 8, 128)
    shapes["pair0"], shapes["pair1"] = vmem(8, 32, 128), vmem(4, 16, 128)
    shapes["pair2"], shapes["pair3"] = vmem(2, 8, 128), vmem(8, 32, 128)
    shapes["w4"] = vmem(9, 4, 16, 128)
    shapes["up0"], shapes["tall0"] = vmem(12, 32, 256), vmem(2, 48, 128)
    shapes["up1"], shapes["tall1"] = vmem(10, 24, 128), vmem(32, 128)
    shapes["dummy"] = vmem(256, 8, 128)
    shapes["send"] = pltpu.SemaphoreType.DMA((16,))
    shapes["recv"] = pltpu.SemaphoreType.DMA((16,))
    shapes["load"] = pltpu.SemaphoreType.DMA((2,))
    return shapes


SCRATCH = scratch_shapes()


def on_device(source_term, conductivity):
    return pl.pallas_call(
        kernel,
        out_shape=jax.ShapeDtypeStruct((16, 32, 128), F32),
        in_specs=[pl.BlockSpec(memory_space=pl.ANY)] * 2,
        out_specs=pl.BlockSpec(memory_space=pltpu.VMEM),
        scratch_shapes=list(SCRATCH.values()),
        compiler_params=pltpu.CompilerParams(
            collective_id=0, has_side_effects=True, vmem_limit_bytes=48 * 2**20
        ),
        name="vcycle",
    )(source_term, conductivity)


def solution(mesh):
    spec = P("gx", "gy", "gz")
    return jax.shard_map(
        on_device, mesh=mesh, in_specs=(spec, spec), out_specs=spec, check_vma=False
    )
```

```python
import functools

import jax
import jax.numpy as jnp
from jax import lax
from jax.experimental import pallas as pl
from jax.experimental.pallas import tpu as pltpu
from jax.sharding import PartitionSpec as P

MESH = pl.DeviceIdType.MESH
AXES = ("gx", "gy", "gz")
N = 8
BOTTOM = 16
F32 = jnp.float32


def iota(shape, axis):
    return lax.broadcasted_iota(jnp.int32, shape, axis)


def halves(a):
    high = a.astype(jnp.bfloat16)
    return high, (a - high.astype(F32)).astype(jnp.bfloat16)


def product(a, b):
    return lax.dot_general(a, b, (((1,), (0,)), ((), ())), preferred_element_type=F32)


def spread(a, b):
    high, low = halves(a)
    b = b.astype(jnp.bfloat16)
    return product(high, b) + product(low, b)


def select_rows(a, b):
    high, low = halves(b)
    a = a.astype(jnp.bfloat16)
    return product(a, high) + product(a, low)


def rotate(a, shift, axis):
    shift = shift % a.shape[axis]
    return a if shift == 0 else pltpu.roll(a, shift, axis)


class Level:
    def __init__(self, s, no, fk, scale, closed, block):
        self.f, self.k = fk.at[0], fk.at[1]
        self.xin, self.dr, self.db = s[f"xin{no}"], s[f"dr{no}"], s[f"db{no}"]
        self.v = {"r": s[f"vr{no}"], "b": s[f"vb{no}"]}
        self.xo, self.y, self.z, self.i, self.g = (
            {c: s[f"{n}{c}{no}"] for c in "rb"} for n in ("xo", "wy", "wz", "inv", "src")
        )
        self.pairs, self.rows, self.lanes = self.xin.shape
        self.scale, self.closed, self.block = (scale, closed, block)

    def even(self):
        shape = (self.rows, self.lanes)
        return (iota(shape, 0) + iota(shape, 1)) & 1 == 0

    def loop(self, lo, hi, body):
        block = min(self.block, hi - lo)
        if block == hi - lo:
            for j in range(lo, hi):
                body(j)
            return

        def step(i, carry):
            for t in range(block):
                body(lo + i * block + t)
            return carry

        lax.fori_loop(0, (hi - lo) // block, step, 0)
        for j in range(lo + (hi - lo) // block * block, hi):
            body(j)

    def prepare(self, lo, hi, sources=True):
        shape = (self.rows, self.lanes)
        hs = 0.5 * self.scale

        def one(p):
            k = self.k[p]
            kyl, kyu = rotate(k, 1, 0), rotate(k, -1, 0)
            kzl, kzu = rotate(k, 1, 1), rotate(k, -1, 1)
            wy, wz = hs * (k + kyl), hs * (k + kzl)
            if self.closed:
                row, lane = iota(shape, 0), iota(shape, 1)
                kyl = jnp.where(row == 0, 0.0, kyl)
                kyu = jnp.where(row == self.rows - 1, 0.0, kyu)
                kzl = jnp.where(lane == 0, 0.0, kzl)
                kzu = jnp.where(lane == self.lanes - 1, 0.0, kzu)
                wy = jnp.where(row == 0, 0.0, wy)
                wz = jnp.where(lane == 0, 0.0, wz)
            diag = hs * (6.0 * k + self.k[p - 1] + self.k[p + 1] + kyl + kyu + kzl + kzu)
            inside = k > 0.0
            inv = jnp.where(inside, 1.0 / jnp.where(inside, diag, 1.0), 0.0)
            return wy, wz, inv, diag

        def body(j):
            even = self.even()
            p = 2 * j - 1
            first, second = one(p), one(p + 1)
            below = hs * (self.k[p] + self.k[p - 1])
            above = hs * (self.k[p + 2] + self.k[p + 1])
            self.xin[j] = hs * (self.k[p] + self.k[p + 1])
            self.xo["r"][j] = jnp.where(even, below, above)
            self.xo["b"][j] = jnp.where(even, above, below)
            for ref, n in ((self.y, 0), (self.z, 1), (self.i, 2)):
                ref["r"][j] = jnp.where(even, first[n], second[n])
                ref["b"][j] = jnp.where(even, second[n], first[n])
            self.dr[j] = jnp.where(even, first[3], second[3])
            self.db[j] = jnp.where(even, second[3], first[3])

        self.loop(lo, hi, body)

    def sources(self, lo, hi):
        def body(j):
            even = self.even()
            a, b = self.f[2 * j - 1], self.f[2 * j]
            red = jnp.where(even, a, b)
            self.g["r"][j] = red
            self.g["b"][j] = jnp.where(even, b, a)
            self.v["r"][j] = self.i["r"][j] * red

        self.loop(lo, hi, body)

    def around(self, colour, other, j):
        far = "b" if colour == "r" else "r"
        u, before, after = other[j], other[j - 1], other[j + 1]
        if colour == "b":
            before, after = after, before
        total = self.xin[j] * u + self.xo[colour][j] * jnp.where(self.even(), before, after)
        total = total + (self.y[colour][j] * rotate(u, 1, 0) + rotate(self.y[far][j] * u, -1, 0))
        return total + (self.z[colour][j] * rotate(u, 1, 1) + rotate(self.z[far][j] * u, -1, 1))

    def half(self, colour, black, lo, hi):
        target, other = (self.v["r"], black) if colour == "r" else (black, self.v["r"])

        def body(j):
            target[j] = self.i[colour][j] * (self.g[colour][j] + self.around(colour, other, j))

        self.loop(lo, hi, body)

    def sweep(self, black, red_range, black_range):
        self.half("r", black, *red_range)
        self.half("b", black, *black_range)

    def residual(self, lo, hi, rows, out):
        def body(j):
            r, b = self.v["r"], self.v["b"]
            red = self.g["r"][j] - (self.dr[j] * r[j] - self.around("r", b, j))
            black = self.g["b"][j] - (self.db[j] * b[j] - self.around("b", r, j))
            out[j - lo] = (red + black)[rows[0] : rows[1], 0:128]

        self.loop(lo, hi, body)

    def correct(self, black, j, value):
        black[j] = jnp.where(self.i["b"][j] > 0.0, black[j] + value, 0.0)

    def planes(self, black, j):
        r, b, even = self.v["r"][j], black[j], self.even()
        return jnp.where(even, r, b), jnp.where(even, b, r)


def row_pairs(ref, count):
    return ref[pl.ds(0, count, 2), :] + ref[pl.ds(1, count, 2), :]


def kernel(f_hbm, k_hbm, out_ref, *scratch):
    names = list(SCRATCH)
    s = dict(zip(names, scratch))
    ix, iy, iz = (lax.axis_index(a) for a in AXES)
    me = (ix, iy, iz)

    def device(off):
        return tuple(lax.rem(me[a] + (off[a] + N), N) for a in range(3))

    send, recv, dummy = s["send"], s["recv"], s["dummy"]
    sent = {}

    def push(src, dst, sem, off):
        pltpu.make_async_remote_copy(
            src_ref=src, dst_ref=dst, send_sem=send.at[sem], recv_sem=recv.at[sem],
            device_id=device(off), device_id_type=MESH,
        ).start()
        size = 1
        for d in src.shape:
            size *= d
        sent[sem] = sent.get(sem, 0) + size // 1024

    def wait(sems, sem):
        view = dummy.at[pl.ds(0, sent[sem])]
        pltpu.make_async_copy(view, view, sems.at[sem]).wait()

    fk0, fk1, fk2, fk3 = s["fk0"], s["fk1"], s["fk2"], s["fk3"]

    l0, l1 = Level(s, 0, fk0, 1.0, False, 2), Level(s, 1, fk1, 0.25, False, 12)
    l2, l3 = Level(s, 2, fk2, 0.25**2, False, 12), Level(s, 3, fk3, 0.25**3, True, 12)

    own0 = [fk0.at[a, pl.ds(5, 16), pl.ds(8, 32), pl.ds(0, 128)] for a in range(2)]
    loads = [pltpu.make_async_copy(r, own0[a], s["load"].at[a]) for a, r in enumerate((f_hbm, k_hbm))]
    for c in loads:
        c.start()
    near = [(a, b, c) for a in (-1, 0, 1) for b in (-1, 0, 1) for c in (-1, 0, 1) if (a, b, c) != (0, 0, 0)]
    wide = [(a, b, c) for a in (-2, -1, 0, 1, 2) for b in (-1, 0, 1) for c in (-1, 0, 1) if (a, b, c) != (0, 0, 0)]
    lines = []
    for a in range(3):
        for d in range(1, N):
            lines.append(tuple((d if d <= 4 else d - N) if b == a else 0 for b in range(3)))
    partners = wide + [o for o in lines if o not in wide]
    barrier = pltpu.get_barrier_semaphore()
    for off in partners:
        pl.semaphore_signal(barrier, inc=1, device_id=device(off), device_id_type=MESH)
    for c in loads:
        c.wait()
    pl.semaphore_wait(barrier, len(partners))

    def pack(own, zp, planes, length):
        left = right = None
        for p in range(planes):
            v = own(p)
            group = iota(v.shape, 1) // 8 == p
            a, b = rotate(v, 8 * p, 1), rotate(v, 8 * p - (length - 8), 1)
            left = a if p == 0 else jnp.where(group, a, left)
            right = b if p == 0 else jnp.where(group, b, right)
        zp[0], zp[1] = left, right

    def slabs(src, dst, start, nx, w, ny, lead, sem, corners=None):
        for sx in (-1, 0, 1):
            for sy in (-1, 0, 1):
                if (sx, sy) == (0, 0):
                    continue
                xs = {1: (start + nx - w, w, start - w), -1: (start, w, start + nx), 0: (start, nx, start)}[sx]
                ys = {1: (8 + ny - 8, 8, 0), -1: (8, 8, 8 + ny), 0: (8, ny, 8)}[sy]
                a = lead + (pl.ds(xs[0], xs[1]), pl.ds(ys[0], ys[1]), pl.ds(0, 128))
                b = lead + (pl.ds(xs[2], xs[1]), pl.ds(ys[2], ys[1]), pl.ds(0, 128))
                push(src.at[a], dst.at[b], sem, (sx, sy, 0))

    def edges(zp, zr, ny, lead, sem, columns=(-1, 0, 1)):
        for sz in (-1, 1):
            side = 1 if sz == 1 else 0
            for sx in columns:
                for sy in (-1, 0, 1):
                    ys = {1: (ny - 8, 8, 0), -1: (0, 8, 8 + ny), 0: (0, ny, 8)}[sy]
                    a = (side,) + lead + (pl.ds(ys[0], ys[1]),)
                    b = (1 - side, 1 - sx) + lead + (pl.ds(ys[2], ys[1]),)
                    push(zp.at[a], zr.at[b], sem, (sx, sy, sz))

    def place(right, left, base):
        lane = iota(right.shape, 1)
        return jnp.where((lane >= base) & (lane < base + 8), right, jnp.where(lane >= 120, left, 0.0))

    def slot(p, start, nx):
        return (0, p - start + nx) if p < start else (1, p - start) if p < start + nx else (2, p - start - nx)

    def ghost(zr, lead, p, start, nx, base):
        b, q = slot(p, start, nx)
        right = rotate(zr[(1, b) + lead], base - 8 * q, 1)
        left = rotate(zr[(0, b) + lead], 120 - 8 * q, 1)
        return place(right, left, base)

    def flag(condition):
        return jnp.where(condition, 1.0, 0.0)

    def inside_yz(rows, ny, own_lanes, right_end, lanes):
        row, lane = iota((rows, lanes), 0), iota((rows, lanes), 1)
        in_y = ((row >= 8) | (iy > 0)) & ((row < 8 + ny) | (iy < N - 1))
        in_z = (lane < own_lanes) | ((lane < right_end) & (iz < N - 1)) | ((lane >= right_end) & (iz > 0))
        return jnp.where(in_y & in_z, 1.0, 0.0)

    def inside_x(p, h, nx):
        return flag(ix > 0) if p < h else flag(ix < N - 1) if p >= h + nx else 1.0

    zp0, ze0, zr0, zs0 = s["zp0"], s["ze0"], s["zr0"], s["zs0"]
    for a in range(2):
        pack(lambda p, a=a: fk0[a, 5 + p, 8:40, 0:128], zp0.at[:, a], 16, 128)
    slabs(fk0, fk0, 5, 16, 4, 32, (slice(None),), 0)
    for sx, a, b in ((1, 16 + 0, 0), (-1, 9, 25)):
        push(fk0.at[1, a, pl.ds(8, 32), pl.ds(0, 128)], fk0.at[1, b, pl.ds(8, 32), pl.ds(0, 128)], 0, (sx, 0, 0))
    edges(zp0, zr0, 32, (slice(None),), 1, (0,))
    lane32 = iota((32, 128), 1)
    for side in range(2):
        fs, ks = zp0[side, 0], zp0[side, 1]
        v = jnp.where(lane32 < 32, fs, rotate(fs, -64, 1))
        ze0[side] = jnp.where(lane32 < 64, v, jnp.where(lane32 < 96, rotate(ks, 64, 1), ks))
    edges(ze0, zs0, 32, (), 1, (-1, 1))

    def ghost0(a, p):
        b, q = slot(p, 5, 16)
        if b == 1:
            return ghost(zr0, (a,), p, 5, 16, 0)
        if not 0 < p < 25:
            return jnp.zeros((48, 128), F32)
        at = 64 * a + (8 * q if b == 2 else 32 + 8 * (q - 12))
        return place(rotate(zs0[1, b], -at, 1), rotate(zs0[0, b], 120 - at, 1), 0)

    lane_r, lane_c = iota((128, 128), 0), iota((128, 128), 1)
    halve1 = jnp.where((lane_r // 2 == lane_c), 0.125, 0.0)
    halve2 = jnp.where((lane_r // 2 == lane_c) & (lane_c < 32), 0.125, 0.0)

    pair0, pair1, pair2, pair3 = s["pair0"], s["pair1"], s["pair2"], s["pair3"]

    def coarse1():
        flat = pair0.reshape(256, 128)
        return spread(row_pairs(flat, 128), halve1).reshape(8, 16, 128)

    def coarse2():
        flat = pair1.reshape(64, 128)
        return spread(row_pairs(flat, 32), halve2).reshape(4, 8, 128)

    def packed2(value):
        total = value[0]
        for q in range(1, 4):
            total = total + rotate(value[q], 32 * q, 1)
        return total

    row8, col8 = iota((8, 8), 0), iota((8, 8), 1)

    def coarse3():
        place_rows = jnp.where(row8 == 4 * lax.rem(iy, 2) + col8 // 2, 1.0, 0.0)
        total = None
        for dx in range(2):
            group = lax.rem(2 * ix + dx, 8)
            into = jnp.where((lane_r < 32) & (lane_c == 16 * group + lane_r // 2), 0.125, 0.0)
            part = spread(select_rows(place_rows, pair2[dx]), into)
            total = part if total is None else total + part
        return total

    def gather(tile, g1, g2, g3, sem):
        g1[ix] = tile
        for d in range(1, N):
            push(g1.at[ix], g1.at[ix], sem, (d, 0, 0))
        yield
        wait(recv, sem)
        g2[iy, 0] = g1[0] + g1[1] + g1[2] + g1[3]
        g2[iy, 1] = g1[4] + g1[5] + g1[6] + g1[7]
        for d in range(1, N):
            push(g2.at[iy], g2.at[iy], sem + 1, (0, d, 0))
        yield
        wait(recv, sem + 1)
        for o in range(4):
            for h in range(2):
                g3[iz, h, o] = g2[2 * o, h] + g2[2 * o + 1, h]
        for d in range(1, N):
            push(g3.at[iz], g3.at[iz], sem + 2, (0, 0, d))
        yield
        wait(recv, sem + 2)

    def unpack3(g3, out):
        group = iota((32, 128), 1) // 16
        for h in range(2):
            blocks = [g3[j, h].reshape(32, 128) for j in range(8)]
            for g in range(8):
                total = rotate(blocks[0], 16 * (0 - g), 1)
                for j in range(1, 8):
                    total = jnp.where(group == j, rotate(blocks[j], 16 * (j - g), 1), total)
                out[1 + 8 * h + g] = total

    for i in range(8):
        pair0[i] = fk0[1, 5 + 2 * i, 8:40, 0:128] + fk0[1, 6 + 2 * i, 8:40, 0:128]
    k1_own = coarse1()
    fk1[1, 7:15, 8:24, :] = k1_own
    for i in range(4):
        pair1[i] = k1_own[2 * i] + k1_own[2 * i + 1]
    k2_own = coarse2()
    rk2 = s["rk2"]
    rk2[2, 1, 1] = packed2(k2_own)
    for i in range(2):
        pair2[i] = k2_own[2 * i] + k2_own[2 * i + 1]
    k_gather = gather(coarse3(), s["gk1"], s["gk2"], s["gk3"], 10)
    pack(lambda p: fk1[1, 7 + p, 8:24, :], s["zk1"], 8, 64)

    for lev, last in ((l0, 13), (l1, 11), (l2, 11), (l3, 9)):
        for colour in "rb":
            for j in (0, last):
                lev.v[colour][j] = jnp.zeros((lev.rows, lev.lanes), F32)
    for j in (0, 13):
        s["v0"][j] = jnp.zeros((48, 256), F32)
    for j in (0, 11):
        s["v1"][j] = jnp.zeros((32, 128), F32)
        s["v2"][j] = jnp.zeros((24, 128), F32)
    for p in (0, 21):
        fk1[1, p] = jnp.zeros((32, 128), F32)
        fk2[1, p] = jnp.zeros((24, 128), F32)
    for p in (1, 20):
        fk1[0, p] = jnp.zeros((32, 128), F32)
    for p in (0, 17):
        fk3[1, p] = jnp.zeros((32, 128), F32)
    u3 = s["u3"]
    for p in (0, 1, 2, 3, 20, 21, 22, 23):
        u3[p] = jnp.zeros((32, 128), F32)

    wait(recv, 0)
    wait(recv, 1)
    wait(send, 0)
    slabs(fk1, fk1, 7, 8, 6, 16, (1,), 2)
    edges(s["zk1"], s["zrk1"], 16, (), 3)
    for off in wide:
        push(rk2.at[2, 1, 1], rk2.at[2 - off[0], 1 - off[1], 1 - off[2]], 16, off)
    next(k_gather)
    myz0 = inside_yz(48, 32, 128, 192, 256)
    row48 = iota((48, 128), 0)
    for p in range(26):
        for a in range(2):
            g = ghost0(a, p)
            if a == 1:
                sx = inside_x(p, 5, 16)
                main = fk0[1, p, :, 0:128] * (myz0[:, 0:128] * sx)
                if not 0 < p < 25:
                    main = jnp.where((row48 >= 8) & (row48 < 40), main, 0.0)
                fk0[1, p, :, 0:128] = main
                g = g * (myz0[:, 128:256] * sx)
            fk0[a, p, :, 128:256] = g
    l0.prepare(1, 13)
    l0.sources(1, 13)
    l0.half("b", l0.v["b"], 1, 13)
    l0.sweep(l0.v["b"], (2, 12), (2, 12))
    l0.residual(3, 11, (8, 40), pair0)
    f1_own = coarse1()
    fk1[0, 7:15, 8:24, :] = f1_own

    pack(lambda p: fk1[0, 7 + p, 8:24, :], s["zf1"], 8, 64)
    slabs(fk1, fk1, 7, 8, 5, 16, (0,), 4)
    edges(s["zf1"], s["zrf1"], 16, (), 5)
    wait(recv, 2)
    wait(recv, 3)
    wait(send, 2)
    myz1 = inside_yz(32, 16, 64, 96, 128)
    for p in range(1, 21):
        v = jnp.where(lane32 < 64, fk1[1, p], ghost(s["zrk1"], (), p, 7, 8, 64))
        fk1[1, p] = v * (myz1 * inside_x(p, 7, 8))
    l1.prepare(1, 11)
    next(k_gather)

    lane8 = iota((8, 128), 1)

    def unpack2(block, b, q, by):
        own = rotate(block(b, by, 1), -32 * q, 1)
        right = rotate(block(b, by, 2), 32 * (1 - q), 1)
        left = rotate(block(b, by, 0), 32 * (3 - q), 1)
        return jnp.where(lane8 < 32, own, jnp.where(lane8 < 64, right, jnp.where(lane8 >= 96, left, 0.0)))

    row24, lane24 = iota((24, 128), 0), iota((24, 128), 1)
    in_y = ((row24 >= 8) | (iy > 0)) & ((row24 < 16) | (iy < N - 1))
    in_z = (lane24 < 32) | ((lane24 < 64) & (iz < N - 1)) | ((lane24 >= 96) & (iz > 0))
    myz2 = jnp.where(in_y & in_z, 1.0, 0.0)
    wait(recv, 16)
    for p in range(20):
        b, q = divmod(p, 4)
        sx = [flag(ix > 1), flag(ix > 0), 1.0, flag(ix < N - 1), flag(ix < N - 2)][b]
        for by in range(3):
            v = unpack2(lambda i, j, k: rk2[i, j, k], b, q, by)
            fk2[1, 1 + p, 8 * by : 8 * by + 8, :] = v * (myz2[8 * by : 8 * by + 8] * sx)
    l2.prepare(1, 11)

    wait(recv, 4)
    wait(recv, 5)
    wait(send, 4)
    for p in range(2, 20):
        fk1[0, p] = jnp.where(lane32 < 64, fk1[0, p], ghost(s["zrf1"], (), p, 7, 8, 64))
    l1.sources(1, 11)
    l1.half("b", l1.v["b"], 2, 10)
    l1.sweep(l1.v["b"], (3, 9), (3, 9))
    l1.residual(4, 8, (8, 24), pair1)
    rf2 = s["rf2"]
    rf2[2, 1, 1] = packed2(coarse2())

    for off in wide:
        push(rf2.at[2, 1, 1], rf2.at[2 - off[0], 1 - off[1], 1 - off[2]], 6, off)
    wait(recv, 6)
    next(k_gather)
    for p in range(20):
        b, q = divmod(p, 4)
        for by in range(3):
            fk2[0, 1 + p, 8 * by : 8 * by + 8, :] = unpack2(lambda i, j, k: rf2[i, j, k], b, q, by)
    l2.sources(1, 11)
    l2.half("b", l2.v["b"], 3, 9)
    l2.sweep(l2.v["b"], (4, 8), (4, 8))
    l2.residual(5, 7, (8, 16), pair2)
    f_gather = gather(coarse3(), s["gf1"], s["gf2"], s["gf3"], 13)
    next(f_gather)
    next(f_gather)
    for _ in k_gather:
        pass
    unpack3(s["gk3"], fk3.at[1])
    l3.prepare(1, 9)
    next(f_gather)
    pair3_flat = pair3.reshape(8 * 32, 128)

    def coarse4():
        rows = row_pairs(pair3_flat, 128).reshape(8, 16, 128)
        out = None
        for h in range(2):
            into = jnp.where(lane_c == 64 * h + lane_r // 2, 0.125, 0.0)
            part = spread(rows[4 * h : 4 * h + 4].reshape(64, 128), into)
            out = part if out is None else out + part
        return out.reshape(4, 16, 128)

    for i in range(8):
        pair3[i] = fk3[1, 1 + 2 * i] + fk3[1, 2 + 2 * i]
    k4 = coarse4()
    shape4 = (4, 16, 128)
    row4, lane4 = iota(shape4, 1), iota(shape4, 2)
    z4 = lane4 & 63

    def cat(parts):
        return jnp.concatenate(parts, axis=0)

    def x_below(v):
        return cat([rotate(v[3], 64, 1)[None], v[0:3]])

    def x_above(v):
        return cat([v[1:4], rotate(v[0], 64, 1)[None]])

    def roll3(v, shift, axis):
        flat = [rotate(v[i], shift, axis)[None] for i in range(4)]
        return cat(flat)

    plane4 = iota(shape4, 0)
    first_x = (plane4 == 0) & (lane4 < 64)
    last_x = (plane4 == 3) & (lane4 >= 64)
    hs4 = 0.5 * 0.25**4
    kxl, kxu = jnp.where(first_x, 0.0, x_below(k4)), jnp.where(last_x, 0.0, x_above(k4))
    kyl = jnp.where(row4 == 0, 0.0, roll3(k4, 1, 0))
    kyu = jnp.where(row4 == 15, 0.0, roll3(k4, -1, 0))
    kzl = jnp.where(z4 == 0, 0.0, roll3(k4, 1, 1))
    kzu = jnp.where(z4 == 63, 0.0, roll3(k4, -1, 1))
    w4 = s["w4"]
    inv4 = 1.0 / (hs4 * (6.0 * k4 + kxl + kxu + kyl + kyu + kzl + kzu))
    odd4 = (plane4 + row4 + lane4) & 1
    w4[0] = jnp.where(first_x, 0.0, hs4 * (k4 + kxl))
    w4[1] = jnp.where(last_x, 0.0, hs4 * (k4 + kxu))
    w4[2] = jnp.where(row4 == 0, 0.0, hs4 * (k4 + kyl))
    w4[3] = jnp.where(row4 == 15, 0.0, hs4 * (k4 + kyu))
    w4[4] = jnp.where(z4 == 0, 0.0, hs4 * (k4 + kzl))
    w4[5] = jnp.where(z4 == 63, 0.0, hs4 * (k4 + kzu))
    w4[6] = jnp.where(odd4 == 0, inv4, 0.0)
    w4[7] = jnp.where(odd4 == 1, inv4, 0.0)

    for _ in f_gather:
        pass
    ru2 = s["ru2"]
    total = jnp.where(lane8 < 32, l2.v["b"][5, 8:16, :], 0.0)
    ru2[2, 1, 1] = total + rotate(jnp.where(lane8 < 32, l2.v["b"][6, 8:16, :], 0.0), 32, 1)
    for off in wide:
        push(ru2.at[2, 1, 1], ru2.at[2 - off[0], 1 - off[1], 1 - off[2]], 9, off)
    pack(lambda p: l1.v["b"][4 + p, 8:24, :], s["zpu1"], 4, 64)
    slabs(l1.v["b"], s["v1"], 4, 4, 3, 16, (), 7)
    edges(s["zpu1"], s["zru1"], 16, (), 8)
    s["v1"][4:8, 8:24, :] = l1.v["b"][4:8, 8:24, :]
    pack(lambda p: l0.v["b"][3 + p, 8:40, 0:128], s["zpu0"], 8, 128)
    slabs(l0.v["b"], s["v0"], 3, 8, 2, 32, (), 17)
    edges(s["zpu0"], s["zru0"], 32, (), 18)
    s["v0"][3:11, 8:40, 0:128] = l0.v["b"][3:11, 8:40, 0:128]

    unpack3(s["gf3"], fk3.at[0])
    l3.sources(1, 9)
    l3.half("b", l3.v["b"], 1, 9)
    l3.sweep(l3.v["b"], (1, 9), (1, 9))
    l3.residual(1, 9, (0, 32), pair3)
    f4 = coarse4()
    w4[8] = f4

    def around4(v):
        total = w4[0] * x_below(v) + w4[1] * x_above(v)
        total = total + (w4[2] * roll3(v, 1, 0) + w4[3] * roll3(v, -1, 0))
        return total + (w4[4] * roll3(v, 1, 1) + w4[5] * roll3(v, -1, 1))

    def bottom(i, carry):
        black = carry[1]
        red = w4[6] * (w4[8] + around4(black))
        black = w4[7] * (w4[8] + around4(red))
        return (red, black)

    zero4 = jnp.zeros(shape4, F32)
    red4, black4 = lax.fori_loop(0, BOTTOM, bottom, (zero4, zero4))
    u4 = red4 + black4

    for h in range(2):
        into = jnp.where(lane_r == 64 * h + lane_c // 2, 1.0, 0.0)
        wide4 = spread(u4.reshape(64, 128), into)
        pair3_flat[pl.ds(128 * h, 64, 2), :] = wide4
        pair3_flat[pl.ds(128 * h + 1, 64, 2), :] = wide4
    v3 = l3.v["b"]
    for j in range(1, 9):
        l3.correct(v3, j, pair3[j - 1])
    for _ in range(2):
        l3.sweep(v3, (1, 9), (1, 9))
    for j in range(1, 9):
        u3[2 + 2 * j], u3[3 + 2 * j] = l3.planes(v3, j)

    v2 = s["v2"]
    zoff = jnp.where(lane_c < 64, lane_c, lane_c - 128)
    source_lane = 16 * iz + ((zoff + 128) // 2 - 64)
    spread_z = jnp.where((lane_r == source_lane) & ((lane_c < 64) | (lane_c >= 96)), 1.0, 0.0)
    spread_y = jnp.where(iota((24, 32), 1) == 4 * iy - 4 + iota((24, 32), 0) // 2, 1.0, 0.0)
    stretched = spread(u3[pl.ds(2 * ix, 10)].reshape(320, 128), spread_z)
    side_by_side = jnp.concatenate([stretched[32 * j : 32 * j + 32] for j in range(10)], axis=1)
    corr2 = select_rows(spread_y, side_by_side)
    wait(recv, 9)
    for j in range(1, 11):
        b, q = divmod(j - 1, 2)
        for by in range(3):
            v2[j, 8 * by : 8 * by + 8, :] = unpack2(lambda i, j, k: ru2[i, j, k], b, q, by)
        l2.correct(v2, j, corr2[:, 128 * (j - 1) : 128 * j])
    l2.sweep(v2, (2, 10), (2, 10))
    l2.sweep(v2, (3, 9), (3, 9))

    spread1 = jnp.where(lane_r == jnp.where(lane_c >= 96, 64 + lane_c // 2, lane_c // 2), 1.0, 0.0)
    up1 = s["up1"]
    coarse = []
    for j in range(3, 9):
        coarse += list(l2.planes(v2, j))
    up1[...] = spread(jnp.concatenate(coarse[1:11], axis=0), spread1).reshape(10, 24, 128)
    tall1 = s["tall1"]
    wait(recv, 7)
    wait(recv, 8)
    v1 = s["v1"]
    for j in range(1, 11):
        v1[j] = jnp.where(lane32 < 64, v1[j], ghost(s["zru1"], (), j, 4, 4, 64))
        part = up1[j - 1, 4:20, :]
        tall1[j - 1, pl.ds(0, 16, 2), :] = part
        tall1[j - 1, pl.ds(1, 16, 2), :] = part
        l1.correct(v1, j, tall1[j - 1])
    l1.sweep(v1, (1, 11), (2, 10))
    l1.sweep(v1, (2, 10), (3, 9))

    spread0 = jnp.where(iota((128, 256), 0) == iota((128, 256), 1) // 2, 1.0, 0.0)
    up0, tall0 = s["up0"], s["tall0"]
    coarse = []
    for j in range(3, 9):
        coarse += list(l1.planes(v1, j))
    up0[...] = spread(jnp.concatenate(coarse, axis=0), spread0).reshape(12, 32, 256)
    wait(recv, 17)
    wait(recv, 18)
    v0 = s["v0"]
    for j in range(1, 13):
        v0[j, :, 128:256] = ghost(s["zru0"], (), j, 3, 8, 0)
        for t in range(2):
            lanes = slice(128 * t, 128 * t + 128)
            part = up0[j - 1, 4:28, lanes]
            tall0[j - 1, t, pl.ds(0, 24, 2), :] = part
            tall0[j - 1, t, pl.ds(1, 24, 2), :] = part
            black = l0.i["b"][j, :, lanes] > 0.0
            v0[j, :, lanes] = jnp.where(black, v0[j, :, lanes] + tall0[j - 1, t], 0.0)
    l0.sweep(v0, (1, 13), (2, 12))
    l0.sweep(v0, (2, 12), (3, 11))
    for j in range(3, 11):
        a, b = l0.planes(v0, j)
        out_ref[2 * j - 6] = a[8:40, 0:128]
        out_ref[2 * j - 5] = b[8:40, 0:128]
    for sem in sorted(sent):
        if sem not in (0, 2, 4):
            wait(send, sem)


def vmem(*shape):
    return pltpu.VMEM(shape, F32)


def scratch_shapes():
    shapes = {}
    sizes = [(26, 12, 48, 256), (22, 10, 32, 128), (22, 10, 24, 128), (18, 8, 32, 128)]
    for no, (planes, pairs, rows, lanes) in enumerate(sizes):
        shapes[f"fk{no}"] = vmem(2, planes, rows, lanes)
        names = ["xin", "dr", "db"] + [n + c for n in ("v", "xo", "wy", "wz", "inv", "src") for c in "rb"]
        for name in names + (["v"] if no < 3 else []):
            shapes[f"{name}{no}"] = vmem(pairs + 2, rows, lanes)
    shapes["zp0"], shapes["zr0"] = vmem(2, 2, 32, 128), vmem(2, 3, 2, 48, 128)
    shapes["ze0"], shapes["zs0"] = vmem(2, 32, 128), vmem(2, 3, 48, 128)
    shapes["zpu0"], shapes["zru0"] = vmem(2, 32, 128), vmem(2, 3, 48, 128)
    for name in ("k1", "f1", "pu1"):
        shapes["z" + name] = vmem(2, 16, 128)
    for name in ("zrk1", "zrf1", "zru1"):
        shapes[name] = vmem(2, 3, 32, 128)
    for name in ("rk2", "rf2", "ru2"):
        shapes[name] = vmem(5, 3, 3, 8, 128)
    for name in "kf":
        shapes[f"g{name}1"] = vmem(8, 8, 128)
        shapes[f"g{name}2"] = vmem(8, 2, 8, 128)
        shapes[f"g{name}3"] = vmem(8, 2, 4, 8, 128)
    shapes["pair0"], shapes["pair1"] = vmem(8, 32, 128), vmem(4, 16, 128)
    shapes["pair2"], shapes["pair3"] = vmem(2, 8, 128), vmem(8, 32, 128)
    shapes["w4"], shapes["u3"] = vmem(9, 4, 16, 128), vmem(24, 32, 128)
    shapes["up0"], shapes["tall0"] = vmem(12, 32, 256), vmem(12, 2, 48, 128)
    shapes["up1"], shapes["tall1"] = vmem(10, 24, 128), vmem(10, 32, 128)
    shapes["dummy"] = vmem(256, 8, 128)
    shapes["send"] = pltpu.SemaphoreType.DMA((20,))
    shapes["recv"] = pltpu.SemaphoreType.DMA((20,))
    shapes["load"] = pltpu.SemaphoreType.DMA((2,))
    return shapes


SCRATCH = scratch_shapes()


def on_device(source_term, conductivity):
    return pl.pallas_call(
        kernel,
        out_shape=jax.ShapeDtypeStruct((16, 32, 128), F32),
        in_specs=[pl.BlockSpec(memory_space=pl.ANY)] * 2,
        out_specs=pl.BlockSpec(memory_space=pltpu.VMEM),
        scratch_shapes=list(SCRATCH.values()),
        compiler_params=pltpu.CompilerParams(
            collective_id=0, has_side_effects=True, vmem_limit_bytes=60 * 2**20
        ),
        name="vcycle",
    )(source_term, conductivity)


def solution(mesh):
    spec = P("gx", "gy", "gz")
    return jax.shard_map(
        on_device, mesh=mesh, in_specs=(spec, spec), out_specs=spec, check_vma=False
    )
```

```python
import functools

import jax
import jax.numpy as jnp
from jax import lax
from jax.experimental import pallas as pl
from jax.experimental.pallas import tpu as pltpu
from jax.sharding import PartitionSpec as P

MESH = pl.DeviceIdType.MESH
AXES = ("gx", "gy", "gz")
N = 8
BOTTOM = 16
F32 = jnp.float32


def iota(shape, axis):
    return lax.broadcasted_iota(jnp.int32, shape, axis)


def halves(a):
    high = a.astype(jnp.bfloat16)
    return high, (a - high.astype(F32)).astype(jnp.bfloat16)


def product(a, b):
    return lax.dot_general(a, b, (((1,), (0,)), ((), ())), preferred_element_type=F32)


def spread(a, b):
    high, low = halves(a)
    b = b.astype(jnp.bfloat16)
    return product(high, b) + product(low, b)


def select_rows(a, b):
    high, low = halves(b)
    a = a.astype(jnp.bfloat16)
    return product(a, high) + product(a, low)


def rotate(a, shift, axis):
    shift = shift % a.shape[axis]
    return a if shift == 0 else pltpu.roll(a, shift, axis)


class Level:
    def __init__(self, s, no, fk, scale, closed, block, steps=None):
        self.f, self.k = fk.at[0], fk.at[1]
        self.xin, self.dr, self.db = s[f"xin{no}"], s[f"dr{no}"], s[f"db{no}"]
        self.v = {"r": s[f"vr{no}"], "b": s[f"vb{no}"]}
        self.xo, self.y, self.z, self.i, self.g = (
            {c: s[f"{n}{c}{no}"] for c in "rb"} for n in ("xo", "wy", "wz", "inv", "src")
        )
        self.pairs, self.rows, self.lanes = self.xin.shape
        self.scale, self.closed, self.block, self.steps = (scale, closed, block, steps)

    def even(self):
        shape = (self.rows, self.lanes)
        row = iota(shape, 0) if self.steps is None else iota(shape, 0) // 8
        return (row + iota(shape, 1)) & 1 == 0

    def read(self, ref, p):
        if self.steps is None:
            return ref[p]
        tiles = []
        for t in range(0, self.lanes, 128):
            rows = [ref[t // 128, p, pl.ds(r, 8, self.steps), :] for r in range(self.steps)]
            tiles.append(jnp.concatenate(rows, axis=0))
        return jnp.concatenate(tiles, axis=1)

    def shift(self, a, way):
        if self.steps is None:
            return rotate(a, way, 0)
        if way == 1:
            return jnp.concatenate([rotate(a[self.rows - 8 :], 1, 0), a[: self.rows - 8]], axis=0)
        return jnp.concatenate([a[8:], rotate(a[:8], -1, 0)], axis=0)

    def loop(self, lo, hi, body):
        block = min(self.block, hi - lo)
        if block == hi - lo:
            for j in range(lo, hi):
                body(j)
            return

        def step(i, carry):
            for t in range(block):
                body(lo + i * block + t)
            return carry

        lax.fori_loop(0, (hi - lo) // block, step, 0)
        for j in range(lo + (hi - lo) // block * block, hi):
            body(j)

    def prepare(self, lo, hi):
        shape = (self.rows, self.lanes)
        hs = 0.5 * self.scale

        def one(before, k, after):
            kyl, kyu = self.shift(k, 1), self.shift(k, -1)
            kzl, kzu = rotate(k, 1, 1), rotate(k, -1, 1)
            wy, wz = hs * (k + kyl), hs * (k + kzl)
            if self.closed:
                row, lane = iota(shape, 0), iota(shape, 1)
                kyl = jnp.where(row == 0, 0.0, kyl)
                kyu = jnp.where(row == self.rows - 1, 0.0, kyu)
                kzl = jnp.where(lane == 0, 0.0, kzl)
                kzu = jnp.where(lane == self.lanes - 1, 0.0, kzu)
                wy = jnp.where(row == 0, 0.0, wy)
                wz = jnp.where(lane == 0, 0.0, wz)
            diag = hs * (6.0 * k + before + after + kyl + kyu + kzl + kzu)
            inside = k > 0.0
            inv = jnp.where(inside, 1.0 / jnp.where(inside, diag, 1.0), 0.0)
            return wy, wz, inv, diag

        def body(j):
            even = self.even()
            k = [self.read(self.k, 2 * j - 2 + n) for n in range(4)]
            first, second = one(k[0], k[1], k[2]), one(k[1], k[2], k[3])
            below = hs * (k[0] + k[1])
            above = hs * (k[2] + k[3])
            self.xin[j] = hs * (k[1] + k[2])
            self.xo["r"][j] = jnp.where(even, below, above)
            self.xo["b"][j] = jnp.where(even, above, below)
            for ref, n in ((self.y, 0), (self.z, 1), (self.i, 2)):
                ref["r"][j] = jnp.where(even, first[n], second[n])
                ref["b"][j] = jnp.where(even, second[n], first[n])
            self.dr[j] = jnp.where(even, first[3], second[3])
            self.db[j] = jnp.where(even, second[3], first[3])

        self.loop(lo, hi, body)

    def sources(self, lo, hi):
        def body(j):
            even = self.even()
            a, b = self.read(self.f, 2 * j - 1), self.read(self.f, 2 * j)
            red = jnp.where(even, a, b)
            self.g["r"][j] = red
            self.g["b"][j] = jnp.where(even, b, a)
            self.v["r"][j] = self.i["r"][j] * red

        self.loop(lo, hi, body)

    def around(self, colour, other, j):
        far = "b" if colour == "r" else "r"
        u, before, after = other[j], other[j - 1], other[j + 1]
        if colour == "b":
            before, after = after, before
        total = self.xin[j] * u + self.xo[colour][j] * jnp.where(self.even(), before, after)
        total = total + (self.y[colour][j] * self.shift(u, 1) + self.shift(self.y[far][j] * u, -1))
        return total + (self.z[colour][j] * rotate(u, 1, 1) + rotate(self.z[far][j] * u, -1, 1))

    def updated(self, colour, other, j):
        return self.i[colour][j] * (self.g[colour][j] + self.around(colour, other, j))

    def half(self, colour, black, lo, hi):
        target, other = (self.v["r"], black) if colour == "r" else (black, self.v["r"])

        def body(j):
            target[j] = self.updated(colour, other, j)

        self.loop(lo, hi, body)

    def sweep(self, black, red_range, black_range):
        self.half("r", black, *red_range)
        self.half("b", black, *black_range)

    def residual(self, lo, hi, rows, out):
        def body(j):
            r, b = self.v["r"], self.v["b"]
            red = self.g["r"][j] - (self.dr[j] * r[j] - self.around("r", b, j))
            black = self.g["b"][j] - (self.db[j] * b[j] - self.around("b", r, j))
            both = (red + black)[:, 0:128]
            if self.steps is None:
                out[j - lo] = both[rows[0] : rows[1]]
                return
            for t in range(0, self.steps, 2):
                two = both[8 * t : 8 * t + 8] + both[8 * t + 8 : 8 * t + 16]
                out[j - lo, pl.ds(t // 2, 8, self.steps // 2), :] = two

        self.loop(lo, hi, body)

    def correct(self, black, j, value):
        black[j] = jnp.where(self.i["b"][j] > 0.0, black[j] + value, 0.0)

    def planes(self, black, j):
        r, b, even = self.v["r"][j], black[j], self.even()
        return jnp.where(even, r, b), jnp.where(even, b, r)


def row_pairs(ref, count):
    return ref[pl.ds(0, count, 2), :] + ref[pl.ds(1, count, 2), :]


def kernel(f_hbm, k_hbm, out_ref, *scratch):
    names = list(SCRATCH)
    s = dict(zip(names, scratch))
    ix, iy, iz = (lax.axis_index(a) for a in AXES)
    me = (ix, iy, iz)

    def device(off):
        return tuple(lax.rem(me[a] + (off[a] + N), N) for a in range(3))

    send, recv, dummy = s["send"], s["recv"], s["dummy"]
    sent = {}

    def push(src, dst, sem, off):
        pltpu.make_async_remote_copy(
            src_ref=src, dst_ref=dst, send_sem=send.at[sem], recv_sem=recv.at[sem],
            device_id=device(off), device_id_type=MESH,
        ).start()
        size = 1
        for d in src.shape:
            size *= d
        sent[sem] = sent.get(sem, 0) + size // 1024

    def wait(sems, sem):
        view = dummy.at[pl.ds(0, sent[sem])]
        pltpu.make_async_copy(view, view, sems.at[sem]).wait()

    fk0, fk1, fk2, fk3 = s["fk0"], s["fk1"], s["fk2"], s["fk3"]

    l0, l1 = Level(s, 0, fk0, 1.0, False, 2, 6), Level(s, 1, fk1, 0.25, False, 12)
    l2, l3 = Level(s, 2, fk2, 0.25**2, False, 12), Level(s, 3, fk3, 0.25**3, True, 12)

    own0 = [fk0.at[a, 0, pl.ds(5, 16), pl.ds(8, 32)] for a in range(2)]
    loads = [pltpu.make_async_copy(r, own0[a], s["load"].at[a]) for a, r in enumerate((f_hbm, k_hbm))]
    for c in loads:
        c.start()
    near = [(a, b, c) for a in (-1, 0, 1) for b in (-1, 0, 1) for c in (-1, 0, 1) if (a, b, c) != (0, 0, 0)]
    wide = [(a, b, c) for a in (-2, -1, 0, 1, 2) for b in (-1, 0, 1) for c in (-1, 0, 1) if (a, b, c) != (0, 0, 0)]
    lines = []
    for a in range(3):
        for d in range(1, N):
            lines.append(tuple((d if d <= 4 else d - N) if b == a else 0 for b in range(3)))
    partners = wide + [o for o in lines if o not in wide]
    barrier = pltpu.get_barrier_semaphore()
    for off in partners:
        pl.semaphore_signal(barrier, inc=1, device_id=device(off), device_id_type=MESH)
    for c in loads:
        c.wait()
    pl.semaphore_wait(barrier, len(partners))

    def pack(own, zp, planes, length):
        left = right = None
        for p in range(planes):
            v = rotate(own(p), 8 * p, 1)
            group = iota(v.shape, 1) // 8
            left = v if p == 0 else jnp.where(group == p, v, left)
            right = v if p == 0 else jnp.where(group == (p + length // 8 - 1) % 16, v, right)
        zp[0], zp[1] = left, rotate(right, 8 - length, 1)

    def slabs(src, dst, start, nx, w, ny, lead, sem, corners=None):
        for sx in (-1, 0, 1):
            for sy in (-1, 0, 1):
                if (sx, sy) == (0, 0):
                    continue
                xs = {1: (start + nx - w, w, start - w), -1: (start, w, start + nx), 0: (start, nx, start)}[sx]
                ys = {1: (8 + ny - 8, 8, 0), -1: (8, 8, 8 + ny), 0: (8, ny, 8)}[sy]
                a = lead + (pl.ds(xs[0], xs[1]), pl.ds(ys[0], ys[1]), pl.ds(0, 128))
                b = lead + (pl.ds(xs[2], xs[1]), pl.ds(ys[2], ys[1]), pl.ds(0, 128))
                push(src.at[a], dst.at[b], sem, (sx, sy, 0))

    def edges(zp, zr, ny, lead, sem, columns=(-1, 0, 1)):
        for sz in (-1, 1):
            side = 1 if sz == 1 else 0
            for sx in columns:
                for sy in (-1, 0, 1):
                    ys = {1: (ny - 8, 8, 0), -1: (0, 8, 8 + ny), 0: (0, ny, 8)}[sy]
                    a = (side,) + lead + (pl.ds(ys[0], ys[1]),)
                    b = (1 - side, 1 - sx) + lead + (pl.ds(ys[2], ys[1]),)
                    push(zp.at[a], zr.at[b], sem, (sx, sy, sz))

    def place(right, left, base):
        lane = iota(right.shape, 1)
        return jnp.where((lane >= base) & (lane < base + 8), right, jnp.where(lane >= 120, left, 0.0))

    def slot(p, start, nx):
        return (0, p - start + nx) if p < start else (1, p - start) if p < start + nx else (2, p - start - nx)

    def ghost(zr, lead, p, start, nx, base):
        b, q = slot(p, start, nx)
        right = rotate(zr[(1, b) + lead], base - 8 * q, 1)
        left = rotate(zr[(0, b) + lead], 120 - 8 * q, 1)
        return place(right, left, base)

    def flag(condition):
        return jnp.where(condition, 1.0, 0.0)

    def inside_yz(rows, ny, own_lanes, right_end, lanes):
        row, lane = iota((rows, lanes), 0), iota((rows, lanes), 1)
        in_y = ((row >= 8) | (iy > 0)) & ((row < 8 + ny) | (iy < N - 1))
        in_z = (lane < own_lanes) | ((lane < right_end) & (iz < N - 1)) | ((lane >= right_end) & (iz > 0))
        return jnp.where(in_y & in_z, 1.0, 0.0)

    def inside_x(p, h, nx):
        return flag(ix > 0) if p < h else flag(ix < N - 1) if p >= h + nx else 1.0

    zp0, ze0, zr0, zs0 = s["zp0"], s["ze0"], s["zr0"], s["zs0"]
    slabs(fk0, fk0, 5, 16, 4, 32, (slice(None), 0), 0)
    for sx, a, b in ((1, 16, 0), (-1, 9, 25)):
        push(fk0.at[1, 0, a, pl.ds(8, 32)], fk0.at[1, 0, b, pl.ds(8, 32)], 0, (sx, 0, 0))
    for a in range(2):
        pack(lambda p, a=a: fk0[a, 0, 5 + p, 8:40, :], zp0.at[:, a], 16, 128)
    edges(zp0, zr0, 32, (slice(None),), 1, (0,))
    lane32 = iota((32, 128), 1)
    for side in range(2):
        fs, ks = zp0[side, 0], zp0[side, 1]
        v = jnp.where(lane32 < 32, fs, rotate(fs, -64, 1))
        ze0[side] = jnp.where(lane32 < 64, v, jnp.where(lane32 < 96, rotate(ks, 64, 1), ks))
    edges(ze0, zs0, 32, (), 1, (-1, 1))

    def ghost0(a, p):
        b, q = slot(p, 5, 16)
        if b == 1:
            return ghost(zr0, (a,), p, 5, 16, 0)
        if not 0 < p < 25:
            return jnp.zeros((48, 128), F32)
        at = 64 * a + (8 * q if b == 2 else 32 + 8 * (q - 12))
        return place(rotate(zs0[1, b], -at, 1), rotate(zs0[0, b], 120 - at, 1), 0)

    lane_r, lane_c = iota((128, 128), 0), iota((128, 128), 1)
    halve1 = jnp.where((lane_r // 2 == lane_c), 0.125, 0.0)
    halve2 = jnp.where((lane_r // 2 == lane_c) & (lane_c < 32), 0.125, 0.0)

    pairk = s["pairk"]
    pair0, pair1, pair2, pair3 = s["pair0"], s["pair1"], s["pair2"], s["pair3"]

    def coarse1(rows):
        return spread(rows, halve1).reshape(8, 16, 128)

    def coarse2():
        flat = pair1.reshape(64, 128)
        return spread(row_pairs(flat, 32), halve2).reshape(4, 8, 128)

    def packed2(value):
        total = value[0]
        for q in range(1, 4):
            total = total + rotate(value[q], 32 * q, 1)
        return total

    row8, col8 = iota((8, 8), 0), iota((8, 8), 1)

    def coarse3():
        place_rows = jnp.where(row8 == 4 * lax.rem(iy, 2) + col8 // 2, 1.0, 0.0)
        total = None
        for dx in range(2):
            group = lax.rem(2 * ix + dx, 8)
            into = jnp.where((lane_r < 32) & (lane_c == 16 * group + lane_r // 2), 0.125, 0.0)
            part = spread(select_rows(place_rows, pair2[dx]), into)
            total = part if total is None else total + part
        return total

    def gather(tile, g1, g2, g3, sem):
        g1[ix] = tile
        for d in range(1, N):
            push(g1.at[ix], g1.at[ix], sem, (d, 0, 0))
        yield
        wait(recv, sem)
        g2[iy, 0] = g1[0] + g1[1] + g1[2] + g1[3]
        g2[iy, 1] = g1[4] + g1[5] + g1[6] + g1[7]
        for d in range(1, N):
            push(g2.at[iy], g2.at[iy], sem + 1, (0, d, 0))
        yield
        wait(recv, sem + 1)
        for o in range(4):
            for h in range(2):
                g3[iz, h, o] = g2[2 * o, h] + g2[2 * o + 1, h]
        for d in range(1, N):
            push(g3.at[iz], g3.at[iz], sem + 2, (0, 0, d))
        yield
        wait(recv, sem + 2)

    def unpack3(g3, out):
        group = iota((32, 128), 1) // 16
        for h in range(2):
            blocks = [g3[j, h].reshape(32, 128) for j in range(8)]
            for bit in (4, 2, 1):
                low = group & bit == 0
                for j in range(8):
                    if j & bit:
                        continue
                    a, c = blocks[j], blocks[j + bit]
                    blocks[j] = jnp.where(low, a, rotate(c, 16 * bit, 1))
                    blocks[j + bit] = jnp.where(low, rotate(a, -16 * bit, 1), c)
            for g in range(8):
                out[1 + 8 * h + g] = blocks[g]

    for i in range(8):
        pairk[i] = fk0[1, 0, 5 + 2 * i, 8:40, :] + fk0[1, 0, 6 + 2 * i, 8:40, :]
    k1_own = coarse1(row_pairs(pairk.reshape(256, 128), 128))
    fk1[1, 7:15, 8:24, :] = k1_own
    for i in range(4):
        pair1[i] = k1_own[2 * i] + k1_own[2 * i + 1]
    k2_own = coarse2()
    rk2 = s["rk2"]
    rk2[2, 1, 1] = packed2(k2_own)
    for i in range(2):
        pair2[i] = k2_own[2 * i] + k2_own[2 * i + 1]
    k_gather = gather(coarse3(), s["gk1"], s["gk2"], s["gk3"], 10)
    pack(lambda p: fk1[1, 7 + p, 8:24, :], s["zk1"], 8, 64)

    for lev, last in ((l0, 13), (l1, 11), (l2, 11), (l3, 9)):
        for colour in "rb":
            for j in (0, last):
                lev.v[colour][j] = jnp.zeros((lev.rows, lev.lanes), F32)
    for j in (0, 13):
        s["v0"][j] = jnp.zeros((48, 256), F32)
    for j in (0, 11):
        s["v1"][j] = jnp.zeros((32, 128), F32)
        s["v2"][j] = jnp.zeros((24, 128), F32)
    for p in (0, 21):
        fk1[1, p] = jnp.zeros((32, 128), F32)
        fk2[1, p] = jnp.zeros((24, 128), F32)
    for j in (1, 2, 9, 10):
        l2.v["r"][j] = jnp.zeros((24, 128), F32)
    for p in (1, 20):
        fk1[0, p] = jnp.zeros((32, 128), F32)
    for p in (0, 17):
        fk3[1, p] = jnp.zeros((32, 128), F32)
    u3 = s["u3"]
    for p in (0, 1, 2, 3, 20, 21, 22, 23):
        u3[p] = jnp.zeros((32, 128), F32)

    wait(recv, 0)
    wait(recv, 1)
    wait(send, 0)
    next(k_gather)
    slabs(fk1, fk1, 7, 8, 6, 16, (1,), 2)
    edges(s["zk1"], s["zrk1"], 16, (), 3)
    for off in wide:
        push(rk2.at[2, 1, 1], rk2.at[2 - off[0], 1 - off[1], 1 - off[2]], 16, off)
    myz0 = inside_yz(48, 32, 128, 192, 256)
    row48 = iota((48, 128), 0)
    for p in range(26):
        for a in range(2):
            g = ghost0(a, p)
            if a == 1:
                sx = inside_x(p, 5, 16)
                main = fk0[1, 0, p] * (myz0[:, 0:128] * sx)
                if not 0 < p < 25:
                    main = jnp.where((row48 >= 8) & (row48 < 40), main, 0.0)
                fk0[1, 0, p] = main
                g = g * (myz0[:, 128:256] * sx)
            fk0[a, 1, p] = g
    l0.prepare(1, 13)
    l0.sources(1, 13)
    l0.half("b", l0.v["b"], 1, 13)
    l0.sweep(l0.v["b"], (2, 12), (2, 12))
    l0.residual(3, 11, (8, 40), pair0)
    f1_own = coarse1(pair0[:, 4:20, :].reshape(128, 128))
    fk1[0, 7:15, 8:24, :] = f1_own

    slabs(fk1, fk1, 7, 8, 5, 16, (0,), 4)
    pack(lambda p: fk1[0, 7 + p, 8:24, :], s["zf1"], 8, 64)
    edges(s["zf1"], s["zrf1"], 16, (), 5)
    wait(recv, 2)
    wait(recv, 3)
    wait(send, 2)
    myz1 = inside_yz(32, 16, 64, 96, 128)
    for p in range(1, 21):
        v = jnp.where(lane32 < 64, fk1[1, p], ghost(s["zrk1"], (), p, 7, 8, 64))
        fk1[1, p] = v * (myz1 * inside_x(p, 7, 8))
    l1.prepare(1, 11)
    next(k_gather)

    lane8 = iota((8, 128), 1)

    def unpack2(block, b, q, by):
        own = rotate(block(b, by, 1), -32 * q, 1)
        right = rotate(block(b, by, 2), 32 * (1 - q), 1)
        left = rotate(block(b, by, 0), 32 * (3 - q), 1)
        return jnp.where(lane8 < 32, own, jnp.where(lane8 < 64, right, jnp.where(lane8 >= 96, left, 0.0)))

    row24, lane24 = iota((24, 128), 0), iota((24, 128), 1)
    in_y = ((row24 >= 8) | (iy > 0)) & ((row24 < 16) | (iy < N - 1))
    in_z = (lane24 < 32) | ((lane24 < 64) & (iz < N - 1)) | ((lane24 >= 96) & (iz > 0))
    myz2 = jnp.where(in_y & in_z, 1.0, 0.0)
    wait(recv, 16)
    for p in range(20):
        b, q = divmod(p, 4)
        sx = [flag(ix > 1), flag(ix > 0), 1.0, flag(ix < N - 1), flag(ix < N - 2)][b]
        for by in range(3):
            v = unpack2(lambda i, j, k: rk2[i, j, k], b, q, by)
            fk2[1, 1 + p, 8 * by : 8 * by + 8, :] = v * (myz2[8 * by : 8 * by + 8] * sx)
    l2.prepare(1, 11)

    wait(recv, 4)
    wait(recv, 5)
    wait(send, 4)
    for p in range(2, 20):
        fk1[0, p] = jnp.where(lane32 < 64, fk1[0, p], ghost(s["zrf1"], (), p, 7, 8, 64))
    l1.sources(1, 11)
    l1.half("b", l1.v["b"], 2, 10)
    l1.sweep(l1.v["b"], (3, 9), (3, 9))
    l1.residual(4, 8, (8, 24), pair1)
    rf2 = s["rf2"]
    rf2[2, 1, 1] = packed2(coarse2())

    far = [off for off in wide if off not in near]
    for sem, group in ((6, near), (19, far)):
        for off in group:
            push(rf2.at[2, 1, 1], rf2.at[2 - off[0], 1 - off[1], 1 - off[2]], sem, off)

    def source2(boxes):
        for b in boxes:
            for p in range(4 * b, 4 * b + 4):
                for by in range(3):
                    fk2[0, 1 + p, 8 * by : 8 * by + 8, :] = unpack2(lambda i, j, k: rf2[i, j, k], b, p % 4, by)
            l2.sources(1 + 2 * b, 3 + 2 * b)

    wait(recv, 6)
    next(k_gather)
    source2((1, 2, 3))
    l2.half("b", l2.v["b"], 3, 9)
    l2.sweep(l2.v["b"], (4, 8), (4, 8))
    l2.residual(5, 7, (8, 16), pair2)
    f_gather = gather(coarse3(), s["gf1"], s["gf2"], s["gf3"], 13)
    next(f_gather)
    slabs(l1.v["b"], s["v1"], 4, 4, 3, 16, (), 7)
    pack(lambda p: l1.v["b"][4 + p, 8:24, :], s["zpu1"], 4, 64)
    edges(s["zpu1"], s["zru1"], 16, (), 8)
    s["v1"][4:8, 8:24, :] = l1.v["b"][4:8, 8:24, :]
    vb0n, v0n = s["vb0n"], s["v0n"]
    for j in range(3, 11):
        for t in range(6):
            vb0n[j, pl.ds(t, 8, 6), :] = l0.v["b"][j, 8 * t : 8 * t + 8, 0:128]
    pack(lambda p: vb0n[3 + p, 8:40, :], s["zpu0"], 8, 128)
    v0n[0, 3:11, 8:40, :] = vb0n[3:11, 8:40, :]
    next(f_gather)
    slabs(vb0n, v0n.at[0], 3, 8, 2, 32, (), 17)
    edges(s["zpu0"], s["zru0"], 32, (), 18)
    wait(recv, 19)
    source2((0, 4))
    for _ in k_gather:
        pass
    unpack3(s["gk3"], fk3.at[1])
    l3.prepare(1, 9)
    next(f_gather)
    ru2 = s["ru2"]
    total = jnp.where(lane8 < 32, l2.v["b"][5, 8:16, :], 0.0)
    ru2[2, 1, 1] = total + rotate(jnp.where(lane8 < 32, l2.v["b"][6, 8:16, :], 0.0), 32, 1)
    for off in wide:
        push(ru2.at[2, 1, 1], ru2.at[2 - off[0], 1 - off[1], 1 - off[2]], 9, off)
    pair3_flat = pair3.reshape(8 * 32, 128)

    def coarse4():
        rows = row_pairs(pair3_flat, 128).reshape(8, 16, 128)
        out = None
        for h in range(2):
            into = jnp.where(lane_c == 64 * h + lane_r // 2, 0.125, 0.0)
            part = spread(rows[4 * h : 4 * h + 4].reshape(64, 128), into)
            out = part if out is None else out + part
        return out.reshape(4, 16, 128)

    for i in range(8):
        pair3[i] = fk3[1, 1 + 2 * i] + fk3[1, 2 + 2 * i]
    k4 = coarse4()
    shape4 = (4, 16, 128)
    row4, lane4 = iota(shape4, 1), iota(shape4, 2)
    z4 = lane4 & 63

    def cat(parts):
        return jnp.concatenate(parts, axis=0)

    def x_below(v):
        return cat([rotate(v[3], 64, 1)[None], v[0:3]])

    def x_above(v):
        return cat([v[1:4], rotate(v[0], 64, 1)[None]])

    def roll3(v, shift, axis):
        flat = [rotate(v[i], shift, axis)[None] for i in range(4)]
        return cat(flat)

    plane4 = iota(shape4, 0)
    first_x = (plane4 == 0) & (lane4 < 64)
    last_x = (plane4 == 3) & (lane4 >= 64)
    hs4 = 0.5 * 0.25**4
    kxl, kxu = jnp.where(first_x, 0.0, x_below(k4)), jnp.where(last_x, 0.0, x_above(k4))
    kyl = jnp.where(row4 == 0, 0.0, roll3(k4, 1, 0))
    kyu = jnp.where(row4 == 15, 0.0, roll3(k4, -1, 0))
    kzl = jnp.where(z4 == 0, 0.0, roll3(k4, 1, 1))
    kzu = jnp.where(z4 == 63, 0.0, roll3(k4, -1, 1))
    w4 = s["w4"]
    inv4 = 1.0 / (hs4 * (6.0 * k4 + kxl + kxu + kyl + kyu + kzl + kzu))
    odd4 = (plane4 + row4 + lane4) & 1
    w4[0] = jnp.where(first_x, 0.0, hs4 * (k4 + kxl))
    w4[1] = jnp.where(last_x, 0.0, hs4 * (k4 + kxu))
    w4[2] = jnp.where(row4 == 0, 0.0, hs4 * (k4 + kyl))
    w4[3] = jnp.where(row4 == 15, 0.0, hs4 * (k4 + kyu))
    w4[4] = jnp.where(z4 == 0, 0.0, hs4 * (k4 + kzl))
    w4[5] = jnp.where(z4 == 63, 0.0, hs4 * (k4 + kzu))
    w4[6] = jnp.where(odd4 == 0, inv4, 0.0)
    w4[7] = jnp.where(odd4 == 1, inv4, 0.0)

    for _ in f_gather:
        pass
    unpack3(s["gf3"], fk3.at[0])
    l3.sources(1, 9)
    l3.half("b", l3.v["b"], 1, 9)
    l3.sweep(l3.v["b"], (1, 9), (1, 9))
    l3.residual(1, 9, (0, 32), pair3)
    f4 = coarse4()
    w4[8] = f4

    def around4(v):
        total = w4[0] * x_below(v) + w4[1] * x_above(v)
        total = total + (w4[2] * roll3(v, 1, 0) + w4[3] * roll3(v, -1, 0))
        return total + (w4[4] * roll3(v, 1, 1) + w4[5] * roll3(v, -1, 1))

    def bottom(i, carry):
        black = carry[1]
        red = w4[6] * (w4[8] + around4(black))
        black = w4[7] * (w4[8] + around4(red))
        return (red, black)

    zero4 = jnp.zeros(shape4, F32)
    red4, black4 = lax.fori_loop(0, BOTTOM, bottom, (zero4, zero4))
    u4 = red4 + black4

    for h in range(2):
        into = jnp.where(lane_r == 64 * h + lane_c // 2, 1.0, 0.0)
        wide4 = spread(u4.reshape(64, 128), into)
        pair3_flat[pl.ds(128 * h, 64, 2), :] = wide4
        pair3_flat[pl.ds(128 * h + 1, 64, 2), :] = wide4
    v3 = l3.v["b"]
    for j in range(1, 9):
        l3.correct(v3, j, pair3[j - 1])
    for _ in range(2):
        l3.sweep(v3, (1, 9), (1, 9))
    for j in range(1, 9):
        u3[2 + 2 * j], u3[3 + 2 * j] = l3.planes(v3, j)

    v2 = s["v2"]
    zoff = jnp.where(lane_c < 64, lane_c, lane_c - 128)
    source_lane = 16 * iz + ((zoff + 128) // 2 - 64)
    spread_z = jnp.where((lane_r == source_lane) & ((lane_c < 64) | (lane_c >= 96)), 1.0, 0.0)
    spread_y = jnp.where(iota((24, 32), 1) == 4 * iy - 4 + iota((24, 32), 0) // 2, 1.0, 0.0)
    stretched = spread(u3[pl.ds(2 * ix, 10)].reshape(320, 128), spread_z)
    side_by_side = jnp.concatenate([stretched[32 * j : 32 * j + 32] for j in range(10)], axis=1)
    corr2 = select_rows(spread_y, side_by_side)
    wait(recv, 9)
    for j in range(1, 11):
        b, q = divmod(j - 1, 2)
        for by in range(3):
            v2[j, 8 * by : 8 * by + 8, :] = unpack2(lambda i, j, k: ru2[i, j, k], b, q, by)
        l2.correct(v2, j, corr2[:, 128 * (j - 1) : 128 * j])
    l2.sweep(v2, (2, 10), (2, 10))
    l2.sweep(v2, (3, 9), (3, 9))

    spread1 = jnp.where(lane_r == jnp.where(lane_c >= 96, 64 + lane_c // 2, lane_c // 2), 1.0, 0.0)
    up1 = s["up1"]
    coarse = []
    for j in range(3, 9):
        coarse += list(l2.planes(v2, j))
    up1[...] = spread(jnp.concatenate(coarse[1:11], axis=0), spread1).reshape(10, 24, 128)
    tall1 = s["tall1"]
    wait(recv, 7)
    wait(recv, 8)
    v1 = s["v1"]
    for j in range(1, 11):
        v1[j] = jnp.where(lane32 < 64, v1[j], ghost(s["zru1"], (), j, 4, 4, 64))
        part = up1[j - 1, 4:20, :]
        tall1[j - 1, pl.ds(0, 16, 2), :] = part
        tall1[j - 1, pl.ds(1, 16, 2), :] = part
        l1.correct(v1, j, tall1[j - 1])
    l1.sweep(v1, (1, 11), (2, 10))
    l1.sweep(v1, (2, 10), (3, 9))

    spread0 = jnp.where(iota((128, 256), 0) == iota((128, 256), 1) // 2, 1.0, 0.0)
    up0 = s["up0"]
    coarse = []
    for j in range(3, 9):
        coarse += list(l1.planes(v1, j))
    wide0 = spread(jnp.concatenate(coarse, axis=0), spread0).reshape(12, 32, 256)
    up0[0], up0[1] = wide0[:, :, 0:128], wide0[:, :, 128:256]
    wait(recv, 17)
    wait(recv, 18)
    v0 = s["v0"]
    for j in range(1, 13):
        v0n[1, j] = ghost(s["zru0"], (), j, 3, 8, 0)
    for j in range(1, 13):
        tiles = []
        for t in range(2):
            rows = [up0[t, j - 1, pl.ds(4 + c, 8, 3), :] for c in range(3)]
            tiles.append(jnp.concatenate([rows[c // 2] for c in range(6)], axis=0))
        corr = jnp.concatenate(tiles, axis=1)
        v0[j] = jnp.where(l0.i["b"][j] > 0.0, l0.read(v0n, j) + corr, 0.0)
    l0.sweep(v0, (1, 13), (2, 12))
    l0.half("r", v0, 2, 12)
    outn = s["outn"]

    def last(j):
        black = l0.updated("b", l0.v["r"], j)
        red, even = l0.v["r"][j], l0.even()
        for n, plane in enumerate((jnp.where(even, red, black), jnp.where(even, black, red))):
            for t in range(6):
                outn[2 * j - 6 + n, pl.ds(t, 8, 6), :] = plane[8 * t : 8 * t + 8, 0:128]

    l0.loop(3, 11, last)
    out_ref[...] = outn[:, 8:40, :]
    for sem in sorted(sent):
        if sem not in (0, 2, 4):
            wait(send, sem)


def vmem(*shape):
    return pltpu.VMEM(shape, F32)


def scratch_shapes():
    shapes = {}
    sizes = [(26, 12, 48, 256), (22, 10, 32, 128), (22, 10, 24, 128), (18, 8, 32, 128)]
    for no, (planes, pairs, rows, lanes) in enumerate(sizes):
        shapes[f"fk{no}"] = vmem(2, 2, planes, rows, 128) if no == 0 else vmem(2, planes, rows, lanes)
        names = ["xin", "dr", "db"] + [n + c for n in ("v", "xo", "wy", "wz", "inv", "src") for c in "rb"]
        for name in names + (["v"] if no < 3 else []):
            shapes[f"{name}{no}"] = vmem(pairs + 2, rows, lanes)
    shapes["zp0"], shapes["zr0"] = vmem(2, 2, 32, 128), vmem(2, 3, 2, 48, 128)
    shapes["ze0"], shapes["zs0"] = vmem(2, 32, 128), vmem(2, 3, 48, 128)
    shapes["zpu0"], shapes["zru0"] = vmem(2, 32, 128), vmem(2, 3, 48, 128)
    for name in ("k1", "f1", "pu1"):
        shapes["z" + name] = vmem(2, 16, 128)
    for name in ("zrk1", "zrf1", "zru1"):
        shapes[name] = vmem(2, 3, 32, 128)
    for name in ("rk2", "rf2", "ru2"):
        shapes[name] = vmem(5, 3, 3, 8, 128)
    for name in "kf":
        shapes[f"g{name}1"] = vmem(8, 8, 128)
        shapes[f"g{name}2"] = vmem(8, 2, 8, 128)
        shapes[f"g{name}3"] = vmem(8, 2, 4, 8, 128)
    shapes["pair0"], shapes["pair1"] = vmem(8, 24, 128), vmem(4, 16, 128)
    shapes["pairk"], shapes["outn"] = vmem(8, 32, 128), vmem(16, 48, 128)
    shapes["vb0n"], shapes["v0n"] = vmem(14, 48, 128), vmem(2, 14, 48, 128)
    shapes["pair2"], shapes["pair3"] = vmem(2, 8, 128), vmem(8, 32, 128)
    shapes["w4"], shapes["u3"] = vmem(9, 4, 16, 128), vmem(24, 32, 128)
    shapes["up0"] = vmem(2, 12, 32, 128)
    shapes["up1"], shapes["tall1"] = vmem(10, 24, 128), vmem(10, 32, 128)
    shapes["dummy"] = vmem(256, 8, 128)
    shapes["send"] = pltpu.SemaphoreType.DMA((20,))
    shapes["recv"] = pltpu.SemaphoreType.DMA((20,))
    shapes["load"] = pltpu.SemaphoreType.DMA((2,))
    return shapes


SCRATCH = scratch_shapes()


def on_device(source_term, conductivity):
    return pl.pallas_call(
        kernel,
        out_shape=jax.ShapeDtypeStruct((16, 32, 128), F32),
        in_specs=[pl.BlockSpec(memory_space=pl.ANY)] * 2,
        out_specs=pl.BlockSpec(memory_space=pltpu.VMEM),
        scratch_shapes=list(SCRATCH.values()),
        compiler_params=pltpu.CompilerParams(
            collective_id=0, has_side_effects=True, vmem_limit_bytes=107 * 2**19
        ),
        name="vcycle",
    )(source_term, conductivity)


def solution(mesh):
    spec = P("gx", "gy", "gz")
    return jax.shard_map(
        on_device, mesh=mesh, in_specs=(spec, spec), out_specs=spec, check_vma=False
    )
```

```python
import functools

import jax
import jax.numpy as jnp
from jax import lax
from jax.experimental import pallas as pl
from jax.experimental.pallas import tpu as pltpu
from jax.sharding import PartitionSpec as P

MESH = pl.DeviceIdType.MESH
AXES = ("gx", "gy", "gz")
N = 8
BOTTOM = 16
F32 = jnp.float32


def iota(shape, axis):
    return lax.broadcasted_iota(jnp.int32, shape, axis)


def halves(a):
    high = a.astype(jnp.bfloat16)
    return high, (a - high.astype(F32)).astype(jnp.bfloat16)


def product(a, b):
    return lax.dot_general(a, b, (((1,), (0,)), ((), ())), preferred_element_type=F32)


def spread(a, b):
    high, low = halves(a)
    b = b.astype(jnp.bfloat16)
    return product(high, b) + product(low, b)


def select_rows(a, b):
    high, low = halves(b)
    a = a.astype(jnp.bfloat16)
    return product(a, high) + product(a, low)


def rotate(a, shift, axis):
    shift = shift % a.shape[axis]
    return a if shift == 0 else pltpu.roll(a, shift, axis)


class Level:
    def __init__(self, s, no, fk, scale, closed, block, steps=None):
        self.f, self.k = fk.at[0], fk.at[1]
        self.xin, self.dr, self.db = s[f"xin{no}"], s[f"dr{no}"], s[f"db{no}"]
        self.v = {"r": s[f"vr{no}"], "b": s[f"vb{no}"]}
        self.xo, self.y, self.z, self.i, self.g = (
            {c: s[f"{n}{c}{no}"] for c in "rb"} for n in ("xo", "wy", "wz", "inv", "src")
        )
        self.pairs, self.rows, self.lanes = self.xin.shape
        self.scale, self.closed, self.block, self.steps = (scale, closed, block, steps)

    def even(self):
        shape = (self.rows, self.lanes)
        row = iota(shape, 0) if self.steps is None else iota(shape, 0) // 8
        return (row + iota(shape, 1)) & 1 == 0

    def read(self, ref, p):
        if self.steps is None:
            return ref[p]
        tiles = []
        for t in range(0, self.lanes, 128):
            rows = [ref[t // 128, p, pl.ds(r, 8, self.steps), :] for r in range(self.steps)]
            tiles.append(jnp.concatenate(rows, axis=0))
        return jnp.concatenate(tiles, axis=1)

    def shift(self, a, way):
        if self.steps is None:
            return rotate(a, way, 0)
        if way == 1:
            return jnp.concatenate([rotate(a[self.rows - 8 :], 1, 0), a[: self.rows - 8]], axis=0)
        return jnp.concatenate([a[8:], rotate(a[:8], -1, 0)], axis=0)

    def loop(self, lo, hi, body):
        block = min(self.block, hi - lo)
        if block == hi - lo:
            for j in range(lo, hi):
                body(j)
            return

        def step(i, carry):
            for t in range(block):
                body(lo + i * block + t)
            return carry

        lax.fori_loop(0, (hi - lo) // block, step, 0)
        for j in range(lo + (hi - lo) // block * block, hi):
            body(j)

    def prepare(self, lo, hi):
        shape = (self.rows, self.lanes)
        hs = 0.5 * self.scale

        def one(before, k, after):
            kyl, kyu = self.shift(k, 1), self.shift(k, -1)
            kzl, kzu = rotate(k, 1, 1), rotate(k, -1, 1)
            wy, wz = hs * (k + kyl), hs * (k + kzl)
            if self.closed:
                row, lane = iota(shape, 0), iota(shape, 1)
                kyl = jnp.where(row == 0, 0.0, kyl)
                kyu = jnp.where(row == self.rows - 1, 0.0, kyu)
                kzl = jnp.where(lane == 0, 0.0, kzl)
                kzu = jnp.where(lane == self.lanes - 1, 0.0, kzu)
                wy = jnp.where(row == 0, 0.0, wy)
                wz = jnp.where(lane == 0, 0.0, wz)
            diag = hs * (6.0 * k + before + after + kyl + kyu + kzl + kzu)
            inside = k > 0.0
            inv = jnp.where(inside, 1.0 / jnp.where(inside, diag, 1.0), 0.0)
            return wy, wz, inv, diag

        def body(j):
            even = self.even()
            k = [self.read(self.k, 2 * j - 2 + n) for n in range(4)]
            first, second = one(k[0], k[1], k[2]), one(k[1], k[2], k[3])
            below = hs * (k[0] + k[1])
            above = hs * (k[2] + k[3])
            self.xin[j] = hs * (k[1] + k[2])
            self.xo["r"][j] = jnp.where(even, below, above)
            self.xo["b"][j] = jnp.where(even, above, below)
            for ref, n in ((self.y, 0), (self.z, 1), (self.i, 2)):
                ref["r"][j] = jnp.where(even, first[n], second[n])
                ref["b"][j] = jnp.where(even, second[n], first[n])
            self.dr[j] = jnp.where(even, first[3], second[3])
            self.db[j] = jnp.where(even, second[3], first[3])

        self.loop(lo, hi, body)

    def sources(self, lo, hi):
        def body(j):
            even = self.even()
            a, b = self.read(self.f, 2 * j - 1), self.read(self.f, 2 * j)
            red = jnp.where(even, a, b)
            self.g["r"][j] = red
            self.g["b"][j] = jnp.where(even, b, a)
            self.v["r"][j] = self.i["r"][j] * red

        self.loop(lo, hi, body)

    def around(self, colour, other, j):
        far = "b" if colour == "r" else "r"
        u, before, after = other[j], other[j - 1], other[j + 1]
        if colour == "b":
            before, after = after, before
        total = self.xin[j] * u + self.xo[colour][j] * jnp.where(self.even(), before, after)
        total = total + (self.y[colour][j] * self.shift(u, 1) + self.shift(self.y[far][j] * u, -1))
        return total + (self.z[colour][j] * rotate(u, 1, 1) + rotate(self.z[far][j] * u, -1, 1))

    def updated(self, colour, other, j):
        return self.i[colour][j] * (self.g[colour][j] + self.around(colour, other, j))

    def half(self, colour, black, lo, hi):
        target, other = (self.v["r"], black) if colour == "r" else (black, self.v["r"])

        def body(j):
            target[j] = self.updated(colour, other, j)

        self.loop(lo, hi, body)

    def sweep(self, black, red_range, black_range):
        self.half("r", black, *red_range)
        self.half("b", black, *black_range)

    def residual(self, lo, hi, rows, out):
        def body(j):
            r, b = self.v["r"], self.v["b"]
            red = self.g["r"][j] - (self.dr[j] * r[j] - self.around("r", b, j))
            black = self.g["b"][j] - (self.db[j] * b[j] - self.around("b", r, j))
            both = (red + black)[:, 0:128]
            if self.steps is None:
                out[j - lo] = both[rows[0] : rows[1]]
                return
            for t in range(0, self.steps, 2):
                two = both[8 * t : 8 * t + 8] + both[8 * t + 8 : 8 * t + 16]
                out[j - lo, pl.ds(t // 2, 8, self.steps // 2), :] = two

        self.loop(lo, hi, body)

    def correct(self, black, j, value):
        black[j] = jnp.where(self.i["b"][j] > 0.0, black[j] + value, 0.0)

    def planes(self, black, j):
        r, b, even = self.v["r"][j], black[j], self.even()
        return jnp.where(even, r, b), jnp.where(even, b, r)


def row_pairs(ref, count):
    return ref[pl.ds(0, count, 2), :] + ref[pl.ds(1, count, 2), :]


def kernel(f_hbm, k_hbm, out_ref, *scratch):
    names = list(SCRATCH)
    s = dict(zip(names, scratch))
    ix, iy, iz = (lax.axis_index(a) for a in AXES)
    me = (ix, iy, iz)

    def device(off):
        return tuple(lax.rem(me[a] + (off[a] + N), N) for a in range(3))

    send, recv, dummy = s["send"], s["recv"], s["dummy"]
    sent = {}

    def push(src, dst, sem, off):
        pltpu.make_async_remote_copy(
            src_ref=src, dst_ref=dst, send_sem=send.at[sem], recv_sem=recv.at[sem],
            device_id=device(off), device_id_type=MESH,
        ).start()
        size = 1
        for d in src.shape:
            size *= d
        sent[sem] = sent.get(sem, 0) + size // 1024

    def wait(sems, sem):
        view = dummy.at[pl.ds(0, sent[sem])]
        pltpu.make_async_copy(view, view, sems.at[sem]).wait()

    fk0, fk1, fk2, fk3 = s["fk0"], s["fk1"], s["fk2"], s["fk3"]

    l0, l1 = Level(s, 0, fk0, 1.0, False, 12, 6), Level(s, 1, fk1, 0.25, False, 12)
    l2, l3 = Level(s, 2, fk2, 0.25**2, False, 12), Level(s, 3, fk3, 0.25**3, True, 12)

    own0 = [fk0.at[a, 0, pl.ds(5, 16), pl.ds(8, 32)] for a in range(2)]
    loads = [pltpu.make_async_copy(r, own0[a], s["load"].at[a]) for a, r in enumerate((f_hbm, k_hbm))]
    for c in loads:
        c.start()
    near = [(a, b, c) for a in (-1, 0, 1) for b in (-1, 0, 1) for c in (-1, 0, 1) if (a, b, c) != (0, 0, 0)]
    wide = [(a, b, c) for a in (-2, -1, 0, 1, 2) for b in (-1, 0, 1) for c in (-1, 0, 1) if (a, b, c) != (0, 0, 0)]
    lines = []
    for a in range(3):
        for d in range(1, N):
            lines.append(tuple((d if d <= 4 else d - N) if b == a else 0 for b in range(3)))
    partners = wide + [o for o in lines if o not in wide]
    barrier = pltpu.get_barrier_semaphore()
    for off in partners:
        pl.semaphore_signal(barrier, inc=1, device_id=device(off), device_id_type=MESH)
    for c in loads:
        c.wait()
    pl.semaphore_wait(barrier, len(partners))

    def pack(own, zp, planes, length):
        left = right = None
        for p in range(planes):
            v = rotate(own(p), 8 * p, 1)
            group = iota(v.shape, 1) // 8
            left = v if p == 0 else jnp.where(group == p, v, left)
            right = v if p == 0 else jnp.where(group == (p + length // 8 - 1) % 16, v, right)
        zp[0], zp[1] = left, right

    def slabs(src, dst, start, nx, w, ny, lead, sem, corners=None):
        for sx in (-1, 0, 1):
            for sy in (-1, 0, 1):
                if (sx, sy) == (0, 0):
                    continue
                xs = {1: (start + nx - w, w, start - w), -1: (start, w, start + nx), 0: (start, nx, start)}[sx]
                ys = {1: (8 + ny - 8, 8, 0), -1: (8, 8, 8 + ny), 0: (8, ny, 8)}[sy]
                a = lead + (pl.ds(xs[0], xs[1]), pl.ds(ys[0], ys[1]), pl.ds(0, 128))
                b = lead + (pl.ds(xs[2], xs[1]), pl.ds(ys[2], ys[1]), pl.ds(0, 128))
                push(src.at[a], dst.at[b], sem, (sx, sy, 0))

    def edges(zp, zr, ny, lead, sem, columns=(-1, 0, 1)):
        for sz in (-1, 1):
            side = 1 if sz == 1 else 0
            for sx in columns:
                for sy in (-1, 0, 1):
                    ys = {1: (ny - 8, 8, 0), -1: (0, 8, 8 + ny), 0: (0, ny, 8)}[sy]
                    a = (side,) + lead + (pl.ds(ys[0], ys[1]),)
                    b = (1 - side, 1 - sx) + lead + (pl.ds(ys[2], ys[1]),)
                    push(zp.at[a], zr.at[b], sem, (sx, sy, sz))

    def place(right, left, at, base):
        lane = iota(right.shape, 1)
        both = rotate(jnp.where(lane // 8 == at, right, left), base - 8 * at, 1)
        return jnp.where((lane >= base) & (lane < base + 8) | (lane >= 120), both, 0.0)

    def slot(p, start, nx):
        return (0, p - start + nx) if p < start else (1, p - start) if p < start + nx else (2, p - start - nx)

    def ghost(zr, lead, p, start, nx, base):
        b, q = slot(p, start, nx)
        return place(zr[(1, b) + lead], zr[(0, b) + lead], q, base)

    def flag(condition):
        return jnp.where(condition, 1.0, 0.0)

    def inside_yz(rows, ny, own_lanes, right_end, lanes):
        row, lane = iota((rows, lanes), 0), iota((rows, lanes), 1)
        in_y = ((row >= 8) | (iy > 0)) & ((row < 8 + ny) | (iy < N - 1))
        in_z = (lane < own_lanes) | ((lane < right_end) & (iz < N - 1)) | ((lane >= right_end) & (iz > 0))
        return jnp.where(in_y & in_z, 1.0, 0.0)

    def inside_x(p, h, nx):
        return flag(ix > 0) if p < h else flag(ix < N - 1) if p >= h + nx else 1.0

    zp0, ze0, zr0, zs0 = s["zp0"], s["ze0"], s["zr0"], s["zs0"]
    slabs(fk0, fk0, 5, 16, 4, 32, (1, 0), 0)
    for sx, a, b in ((1, 16, 0), (-1, 9, 25)):
        push(fk0.at[1, 0, a, pl.ds(8, 32)], fk0.at[1, 0, b, pl.ds(8, 32)], 0, (sx, 0, 0))
    for a in (1, 0):
        pack(lambda p, a=a: fk0[a, 0, 5 + p, 8:40, :], zp0.at[:, a], 16, 128)
    lane32 = iota((32, 128), 1)
    for side in range(2):
        fs, ks = [rotate(zp0[side, a], 8 * side, 1) for a in range(2)]
        v = jnp.where(lane32 < 32, fs, rotate(fs, -64, 1))
        v = jnp.where(lane32 < 64, v, jnp.where(lane32 < 96, rotate(ks, 64, 1), ks))
        ze0[side] = rotate(v, -8 * side, 1)
    edges(zp0, zr0, 32, (1,), 1, (0,))
    edges(ze0, zs0, 32, (), 1, (-1, 1))
    slabs(fk0, fk0, 5, 16, 4, 32, (0, 0), 20)
    edges(zp0, zr0, 32, (0,), 21, (0,))

    def ghost0(a, p):
        b, q = slot(p, 5, 16)
        if b == 1:
            return ghost(zr0, (a,), p, 5, 16, 0)
        if not 0 < p < 25:
            return jnp.zeros((48, 128), F32)
        return place(zs0[1, b], zs0[0, b], 8 * a + (q if b == 2 else 4 + q - 12), 0)

    lane_r, lane_c = iota((128, 128), 0), iota((128, 128), 1)
    halve1 = jnp.where((lane_r // 2 == lane_c), 0.125, 0.0)
    halve2 = jnp.where((lane_r // 2 == lane_c) & (lane_c < 32), 0.125, 0.0)

    pairk = s["pairk"]
    pair0, pair1, pair2, pair3 = s["pair0"], s["pair1"], s["pair2"], s["pair3"]

    def coarse1(rows):
        return spread(rows, halve1).reshape(8, 16, 128)

    def coarse2():
        flat = pair1.reshape(64, 128)
        return spread(row_pairs(flat, 32), halve2).reshape(4, 8, 128)

    def packed2(value):
        total = value[0]
        for q in range(1, 4):
            total = total + rotate(value[q], 32 * q, 1)
        return total

    row8, col8 = iota((8, 8), 0), iota((8, 8), 1)

    def coarse3():
        place_rows = jnp.where(row8 == 4 * lax.rem(iy, 2) + col8 // 2, 1.0, 0.0)
        total = None
        for dx in range(2):
            group = lax.rem(2 * ix + dx, 8)
            into = jnp.where((lane_r < 32) & (lane_c == 16 * group + lane_r // 2), 0.125, 0.0)
            part = spread(select_rows(place_rows, pair2[dx]), into)
            total = part if total is None else total + part
        return total

    def gather(tile, g1, g2, g3, sem):
        g1[ix] = tile
        for d in range(1, N):
            push(g1.at[ix], g1.at[ix], sem, (d, 0, 0))
        yield
        wait(recv, sem)
        g2[iy, 0] = g1[0] + g1[1] + g1[2] + g1[3]
        g2[iy, 1] = g1[4] + g1[5] + g1[6] + g1[7]
        for d in range(1, N):
            push(g2.at[iy], g2.at[iy], sem + 1, (0, d, 0))
        yield
        wait(recv, sem + 1)
        for o in range(4):
            for h in range(2):
                g3[iz, h, o] = g2[2 * o, h] + g2[2 * o + 1, h]
        for d in range(1, N):
            push(g3.at[iz], g3.at[iz], sem + 2, (0, 0, d))
        yield
        wait(recv, sem + 2)

    def unpack3(g3, out):
        group = iota((32, 128), 1) // 16
        for h in range(2):
            blocks = [g3[j, h].reshape(32, 128) for j in range(8)]
            for bit in (4, 2, 1):
                low = group & bit == 0
                for j in range(8):
                    if j & bit:
                        continue
                    a, c = blocks[j], blocks[j + bit]
                    blocks[j] = jnp.where(low, a, rotate(c, 16 * bit, 1))
                    blocks[j + bit] = jnp.where(low, rotate(a, -16 * bit, 1), c)
            for g in range(8):
                out[1 + 8 * h + g] = blocks[g]

    for i in range(8):
        pairk[i] = fk0[1, 0, 5 + 2 * i, 8:40, :] + fk0[1, 0, 6 + 2 * i, 8:40, :]
    k1_own = coarse1(row_pairs(pairk.reshape(256, 128), 128))
    fk1[1, 7:15, 8:24, :] = k1_own
    for i in range(4):
        pair1[i] = k1_own[2 * i] + k1_own[2 * i + 1]
    k2_own = coarse2()
    rk2 = s["rk2"]
    rk2[2, 1, 1] = packed2(k2_own)
    for i in range(2):
        pair2[i] = k2_own[2 * i] + k2_own[2 * i + 1]
    k_gather = gather(coarse3(), s["gk1"], s["gk2"], s["gk3"], 10)
    pack(lambda p: fk1[1, 7 + p, 8:24, :], s["zk1"], 8, 64)

    for lev, last in ((l0, 13), (l1, 11), (l2, 11), (l3, 9)):
        for colour in "rb":
            for j in (0, last):
                lev.v[colour][j] = jnp.zeros((lev.rows, lev.lanes), F32)
    for j in (0, 13):
        s["v0"][j] = jnp.zeros((48, 256), F32)
    for j in (0, 11):
        s["v1"][j] = jnp.zeros((32, 128), F32)
        s["v2"][j] = jnp.zeros((24, 128), F32)
    for p in (0, 21):
        fk1[1, p] = jnp.zeros((32, 128), F32)
        fk2[1, p] = jnp.zeros((24, 128), F32)
    for j in (1, 2, 9, 10):
        l2.v["r"][j] = jnp.zeros((24, 128), F32)
    for p in (1, 20):
        fk1[0, p] = jnp.zeros((32, 128), F32)
    for p in (0, 17):
        fk3[1, p] = jnp.zeros((32, 128), F32)
    u3 = s["u3"]
    for p in (0, 1, 2, 3, 20, 21, 22, 23):
        u3[p] = jnp.zeros((32, 128), F32)

    wait(recv, 0)
    wait(recv, 1)
    wait(send, 0)
    next(k_gather)
    slabs(fk1, fk1, 7, 8, 6, 16, (1,), 2)
    edges(s["zk1"], s["zrk1"], 16, (), 3)
    myz0 = inside_yz(48, 32, 128, 192, 256)
    row48 = iota((48, 128), 0)
    for p in range(26):
        sx = inside_x(p, 5, 16)
        main = fk0[1, 0, p] * (myz0[:, 0:128] * sx)
        if not 0 < p < 25:
            main = jnp.where((row48 >= 8) & (row48 < 40), main, 0.0)
        fk0[1, 0, p] = main
        fk0[1, 1, p] = ghost0(1, p) * (myz0[:, 128:256] * sx)
    l0.prepare(1, 13)
    wait(recv, 20)
    wait(recv, 21)
    for p in range(1, 25):
        fk0[0, 1, p] = ghost0(0, p)
    l0.sources(1, 13)
    l0.half("b", l0.v["b"], 1, 13)
    l0.sweep(l0.v["b"], (2, 12), (2, 12))
    l0.residual(3, 11, (8, 40), pair0)
    f1_own = coarse1(pair0[:, 4:20, :].reshape(128, 128))
    fk1[0, 7:15, 8:24, :] = f1_own

    slabs(fk1, fk1, 7, 8, 5, 16, (0,), 4)
    pack(lambda p: fk1[0, 7 + p, 8:24, :], s["zf1"], 8, 64)
    edges(s["zf1"], s["zrf1"], 16, (), 5)
    for off in wide:
        push(rk2.at[2, 1, 1], rk2.at[2 - off[0], 1 - off[1], 1 - off[2]], 16, off)
    wait(recv, 2)
    wait(recv, 3)
    wait(send, 2)
    myz1 = inside_yz(32, 16, 64, 96, 128)
    for p in range(1, 21):
        v = jnp.where(lane32 < 64, fk1[1, p], ghost(s["zrk1"], (), p, 7, 8, 64))
        fk1[1, p] = v * (myz1 * inside_x(p, 7, 8))
    l1.prepare(1, 11)
    next(k_gather)

    lane8 = iota((8, 128), 1)

    def unpack2(block, b, q, by):
        own = rotate(block(b, by, 1), -32 * q, 1)
        right = rotate(block(b, by, 2), 32 * (1 - q), 1)
        left = rotate(block(b, by, 0), 32 * (3 - q), 1)
        return jnp.where(lane8 < 32, own, jnp.where(lane8 < 64, right, jnp.where(lane8 >= 96, left, 0.0)))

    row24, lane24 = iota((24, 128), 0), iota((24, 128), 1)
    in_y = ((row24 >= 8) | (iy > 0)) & ((row24 < 16) | (iy < N - 1))
    in_z = (lane24 < 32) | ((lane24 < 64) & (iz < N - 1)) | ((lane24 >= 96) & (iz > 0))
    myz2 = jnp.where(in_y & in_z, 1.0, 0.0)
    wait(recv, 4)
    wait(recv, 5)
    wait(send, 4)
    for p in range(2, 20):
        fk1[0, p] = jnp.where(lane32 < 64, fk1[0, p], ghost(s["zrf1"], (), p, 7, 8, 64))
    l1.sources(1, 11)
    l1.half("b", l1.v["b"], 2, 10)
    l1.sweep(l1.v["b"], (3, 9), (3, 9))
    l1.residual(4, 8, (8, 24), pair1)
    rf2 = s["rf2"]
    rf2[2, 1, 1] = packed2(coarse2())

    far = [off for off in wide if off not in near]
    for sem, group in ((6, near), (19, far)):
        for off in group:
            push(rf2.at[2, 1, 1], rf2.at[2 - off[0], 1 - off[1], 1 - off[2]], sem, off)

    def source2(boxes):
        for b in boxes:
            for p in range(4 * b, 4 * b + 4):
                for by in range(3):
                    fk2[0, 1 + p, 8 * by : 8 * by + 8, :] = unpack2(lambda i, j, k: rf2[i, j, k], b, p % 4, by)
            l2.sources(1 + 2 * b, 3 + 2 * b)

    wait(recv, 16)
    for p in range(20):
        b, q = divmod(p, 4)
        sx = [flag(ix > 1), flag(ix > 0), 1.0, flag(ix < N - 1), flag(ix < N - 2)][b]
        for by in range(3):
            v = unpack2(lambda i, j, k: rk2[i, j, k], b, q, by)
            fk2[1, 1 + p, 8 * by : 8 * by + 8, :] = v * (myz2[8 * by : 8 * by + 8] * sx)
    l2.prepare(1, 11)

    wait(recv, 6)
    next(k_gather)
    source2((1, 2, 3))
    l2.half("b", l2.v["b"], 3, 9)
    l2.sweep(l2.v["b"], (4, 8), (4, 8))
    l2.residual(5, 7, (8, 16), pair2)
    f_gather = gather(coarse3(), s["gf1"], s["gf2"], s["gf3"], 13)
    next(f_gather)
    slabs(l1.v["b"], s["v1"], 4, 4, 3, 16, (), 7)
    pack(lambda p: l1.v["b"][4 + p, 8:24, :], s["zpu1"], 4, 64)
    edges(s["zpu1"], s["zru1"], 16, (), 8)
    s["v1"][4:8, 8:24, :] = l1.v["b"][4:8, 8:24, :]
    vb0n, v0n = s["vb0n"], s["v0n"]
    for j in range(3, 11):
        for t in range(6):
            vb0n[j, pl.ds(t, 8, 6), :] = l0.v["b"][j, 8 * t : 8 * t + 8, 0:128]
    pack(lambda p: vb0n[3 + p, 8:40, :], s["zpu0"], 8, 128)
    v0n[0, 3:11, 8:40, :] = vb0n[3:11, 8:40, :]
    next(f_gather)
    slabs(vb0n, v0n.at[0], 3, 8, 2, 32, (), 17)
    edges(s["zpu0"], s["zru0"], 32, (), 18)
    wait(recv, 19)
    source2((0, 4))
    for _ in k_gather:
        pass
    unpack3(s["gk3"], fk3.at[1])
    l3.prepare(1, 9)
    next(f_gather)
    ru2 = s["ru2"]
    total = jnp.where(lane8 < 32, l2.v["b"][5, 8:16, :], 0.0)
    ru2[2, 1, 1] = total + rotate(jnp.where(lane8 < 32, l2.v["b"][6, 8:16, :], 0.0), 32, 1)
    for off in wide:
        push(ru2.at[2, 1, 1], ru2.at[2 - off[0], 1 - off[1], 1 - off[2]], 9, off)
    pair3_flat = pair3.reshape(8 * 32, 128)

    def coarse4():
        rows = row_pairs(pair3_flat, 128).reshape(8, 16, 128)
        out = None
        for h in range(2):
            into = jnp.where(lane_c == 64 * h + lane_r // 2, 0.125, 0.0)
            part = spread(rows[4 * h : 4 * h + 4].reshape(64, 128), into)
            out = part if out is None else out + part
        return out.reshape(4, 16, 128)

    for i in range(8):
        pair3[i] = fk3[1, 1 + 2 * i] + fk3[1, 2 + 2 * i]
    k4 = coarse4()
    shape4 = (4, 16, 128)
    row4, lane4 = iota(shape4, 1), iota(shape4, 2)
    z4 = lane4 & 63

    def cat(parts):
        return jnp.concatenate(parts, axis=0)

    def x_below(v):
        return cat([rotate(v[3], 64, 1)[None], v[0:3]])

    def x_above(v):
        return cat([v[1:4], rotate(v[0], 64, 1)[None]])

    def roll3(v, shift, axis):
        flat = [rotate(v[i], shift, axis)[None] for i in range(4)]
        return cat(flat)

    plane4 = iota(shape4, 0)
    first_x = (plane4 == 0) & (lane4 < 64)
    last_x = (plane4 == 3) & (lane4 >= 64)
    hs4 = 0.5 * 0.25**4
    kxl, kxu = jnp.where(first_x, 0.0, x_below(k4)), jnp.where(last_x, 0.0, x_above(k4))
    kyl = jnp.where(row4 == 0, 0.0, roll3(k4, 1, 0))
    kyu = jnp.where(row4 == 15, 0.0, roll3(k4, -1, 0))
    kzl = jnp.where(z4 == 0, 0.0, roll3(k4, 1, 1))
    kzu = jnp.where(z4 == 63, 0.0, roll3(k4, -1, 1))
    w4 = s["w4"]
    inv4 = 1.0 / (hs4 * (6.0 * k4 + kxl + kxu + kyl + kyu + kzl + kzu))
    odd4 = (plane4 + row4 + lane4) & 1
    w4[0] = jnp.where(first_x, 0.0, hs4 * (k4 + kxl))
    w4[1] = jnp.where(last_x, 0.0, hs4 * (k4 + kxu))
    w4[2] = jnp.where(row4 == 0, 0.0, hs4 * (k4 + kyl))
    w4[3] = jnp.where(row4 == 15, 0.0, hs4 * (k4 + kyu))
    w4[4] = jnp.where(z4 == 0, 0.0, hs4 * (k4 + kzl))
    w4[5] = jnp.where(z4 == 63, 0.0, hs4 * (k4 + kzu))
    w4[6] = jnp.where(odd4 == 0, inv4, 0.0)
    w4[7] = jnp.where(odd4 == 1, inv4, 0.0)

    for _ in f_gather:
        pass
    unpack3(s["gf3"], fk3.at[0])
    l3.sources(1, 9)
    l3.half("b", l3.v["b"], 1, 9)
    l3.sweep(l3.v["b"], (1, 9), (1, 9))
    l3.residual(1, 9, (0, 32), pair3)
    f4 = coarse4()
    w4[8] = f4

    def around4(v):
        total = w4[0] * x_below(v) + w4[1] * x_above(v)
        total = total + (w4[2] * roll3(v, 1, 0) + w4[3] * roll3(v, -1, 0))
        return total + (w4[4] * roll3(v, 1, 1) + w4[5] * roll3(v, -1, 1))

    def bottom(i, carry):
        black = carry[1]
        red = w4[6] * (w4[8] + around4(black))
        black = w4[7] * (w4[8] + around4(red))
        return (red, black)

    zero4 = jnp.zeros(shape4, F32)
    red4, black4 = lax.fori_loop(0, BOTTOM, bottom, (zero4, zero4))
    u4 = red4 + black4

    for h in range(2):
        into = jnp.where(lane_r == 64 * h + lane_c // 2, 1.0, 0.0)
        wide4 = spread(u4.reshape(64, 128), into)
        pair3_flat[pl.ds(128 * h, 64, 2), :] = wide4
        pair3_flat[pl.ds(128 * h + 1, 64, 2), :] = wide4
    v3 = l3.v["b"]
    for j in range(1, 9):
        l3.correct(v3, j, pair3[j - 1])
    for _ in range(2):
        l3.sweep(v3, (1, 9), (1, 9))
    for j in range(1, 9):
        u3[2 + 2 * j], u3[3 + 2 * j] = l3.planes(v3, j)

    v2 = s["v2"]
    zoff = jnp.where(lane_c < 64, lane_c, lane_c - 128)
    source_lane = 16 * iz + ((zoff + 128) // 2 - 64)
    spread_z = jnp.where((lane_r == source_lane) & ((lane_c < 64) | (lane_c >= 96)), 1.0, 0.0)
    spread_y = jnp.where(iota((24, 32), 1) == 4 * iy - 4 + iota((24, 32), 0) // 2, 1.0, 0.0)
    stretched = spread(u3[pl.ds(2 * ix, 10)].reshape(320, 128), spread_z)
    side_by_side = jnp.concatenate([stretched[32 * j : 32 * j + 32] for j in range(10)], axis=1)
    corr2 = select_rows(spread_y, side_by_side)
    wait(recv, 9)
    for j in range(1, 11):
        b, q = divmod(j - 1, 2)
        for by in range(3):
            v2[j, 8 * by : 8 * by + 8, :] = unpack2(lambda i, j, k: ru2[i, j, k], b, q, by)
        l2.correct(v2, j, corr2[:, 128 * (j - 1) : 128 * j])
    l2.sweep(v2, (2, 10), (2, 10))
    l2.sweep(v2, (3, 9), (3, 9))

    spread1 = jnp.where(lane_r == jnp.where(lane_c >= 96, 64 + lane_c // 2, lane_c // 2), 1.0, 0.0)
    up1 = s["up1"]
    coarse = []
    for j in range(3, 9):
        coarse += list(l2.planes(v2, j))
    up1[...] = spread(jnp.concatenate(coarse[1:11], axis=0), spread1).reshape(10, 24, 128)
    tall1 = s["tall1"]
    wait(recv, 7)
    wait(recv, 8)
    v1 = s["v1"]
    for j in range(1, 11):
        v1[j] = jnp.where(lane32 < 64, v1[j], ghost(s["zru1"], (), j, 4, 4, 64))
        part = up1[j - 1, 4:20, :]
        tall1[j - 1, pl.ds(0, 16, 2), :] = part
        tall1[j - 1, pl.ds(1, 16, 2), :] = part
        l1.correct(v1, j, tall1[j - 1])
    l1.sweep(v1, (1, 11), (2, 10))
    l1.sweep(v1, (2, 10), (3, 9))

    spread0 = jnp.where(iota((128, 256), 0) == iota((128, 256), 1) // 2, 1.0, 0.0)
    up0 = s["up0"]
    coarse = []
    for j in range(3, 9):
        coarse += list(l1.planes(v1, j))
    wide0 = spread(jnp.concatenate(coarse, axis=0), spread0).reshape(12, 32, 256)
    up0[0], up0[1] = wide0[:, :, 0:128], wide0[:, :, 128:256]
    wait(recv, 17)
    wait(recv, 18)
    v0 = s["v0"]
    for j in range(1, 13):
        v0n[1, j] = ghost(s["zru0"], (), j, 3, 8, 0)
    for j in range(1, 13):
        tiles = []
        for t in range(2):
            rows = [up0[t, j - 1, pl.ds(4 + c, 8, 3), :] for c in range(3)]
            tiles.append(jnp.concatenate([rows[c // 2] for c in range(6)], axis=0))
        corr = jnp.concatenate(tiles, axis=1)
        v0[j] = jnp.where(l0.i["b"][j] > 0.0, l0.read(v0n, j) + corr, 0.0)
    l0.sweep(v0, (1, 13), (2, 12))
    l0.half("r", v0, 2, 12)
    outn = s["outn"]

    def last(j):
        black = l0.updated("b", l0.v["r"], j)
        red, even = l0.v["r"][j], l0.even()
        for n, plane in enumerate((jnp.where(even, red, black), jnp.where(even, black, red))):
            for t in range(6):
                outn[2 * j - 6 + n, pl.ds(t, 8, 6), :] = plane[8 * t : 8 * t + 8, 0:128]

    l0.loop(3, 11, last)
    out_ref[...] = outn[:, 8:40, :]
    for sem in sorted(sent):
        if sem not in (0, 2, 4):
            wait(send, sem)


def vmem(*shape):
    return pltpu.VMEM(shape, F32)


def scratch_shapes():
    shapes = {}
    sizes = [(26, 12, 48, 256), (22, 10, 32, 128), (22, 10, 24, 128), (18, 8, 32, 128)]
    for no, (planes, pairs, rows, lanes) in enumerate(sizes):
        shapes[f"fk{no}"] = vmem(2, 2, planes, rows, 128) if no == 0 else vmem(2, planes, rows, lanes)
        names = ["xin", "dr", "db"] + [n + c for n in ("v", "xo", "wy", "wz", "inv", "src") for c in "rb"]
        for name in names + (["v"] if no < 3 else []):
            shapes[f"{name}{no}"] = vmem(pairs + 2, rows, lanes)
    shapes["zp0"], shapes["zr0"] = vmem(2, 2, 32, 128), vmem(2, 3, 2, 48, 128)
    shapes["ze0"], shapes["zs0"] = vmem(2, 32, 128), vmem(2, 3, 48, 128)
    shapes["zpu0"], shapes["zru0"] = vmem(2, 32, 128), vmem(2, 3, 48, 128)
    for name in ("k1", "f1", "pu1"):
        shapes["z" + name] = vmem(2, 16, 128)
    for name in ("zrk1", "zrf1", "zru1"):
        shapes[name] = vmem(2, 3, 32, 128)
    for name in ("rk2", "rf2", "ru2"):
        shapes[name] = vmem(5, 3, 3, 8, 128)
    for name in "kf":
        shapes[f"g{name}1"] = vmem(8, 8, 128)
        shapes[f"g{name}2"] = vmem(8, 2, 8, 128)
        shapes[f"g{name}3"] = vmem(8, 2, 4, 8, 128)
    shapes["pair0"], shapes["pair1"] = vmem(8, 24, 128), vmem(4, 16, 128)
    shapes["pairk"], shapes["outn"] = vmem(8, 32, 128), vmem(16, 48, 128)
    shapes["vb0n"], shapes["v0n"] = vmem(14, 48, 128), vmem(2, 14, 48, 128)
    shapes["pair2"], shapes["pair3"] = vmem(2, 8, 128), vmem(8, 32, 128)
    shapes["w4"], shapes["u3"] = vmem(9, 4, 16, 128), vmem(24, 32, 128)
    shapes["up0"] = vmem(2, 12, 32, 128)
    shapes["up1"], shapes["tall1"] = vmem(10, 24, 128), vmem(10, 32, 128)
    shapes["dummy"] = vmem(256, 8, 128)
    shapes["send"] = pltpu.SemaphoreType.DMA((22,))
    shapes["recv"] = pltpu.SemaphoreType.DMA((22,))
    shapes["load"] = pltpu.SemaphoreType.DMA((2,))
    return shapes


SCRATCH = scratch_shapes()


def on_device(source_term, conductivity):
    return pl.pallas_call(
        kernel,
        out_shape=jax.ShapeDtypeStruct((16, 32, 128), F32),
        in_specs=[pl.BlockSpec(memory_space=pl.ANY)] * 2,
        out_specs=pl.BlockSpec(memory_space=pltpu.VMEM),
        scratch_shapes=list(SCRATCH.values()),
        compiler_params=pltpu.CompilerParams(
            collective_id=0, has_side_effects=True, vmem_limit_bytes=107 * 2**19
        ),
        name="vcycle",
    )(source_term, conductivity)


def solution(mesh):
    spec = P("gx", "gy", "gz")
    return jax.shard_map(
        on_device, mesh=mesh, in_specs=(spec, spec), out_specs=spec, check_vma=False
    )
```

```python
import functools

import jax
import jax.numpy as jnp
from jax import lax
from jax.experimental import pallas as pl
from jax.experimental.pallas import tpu as pltpu
from jax.sharding import PartitionSpec as P

MESH = pl.DeviceIdType.MESH
AXES = ("gx", "gy", "gz")
N = 8
BOTTOM = 16
F32 = jnp.float32


def iota(shape, axis):
    return lax.broadcasted_iota(jnp.int32, shape, axis)


def halves(a):
    high = a.astype(jnp.bfloat16)
    return high, (a - high.astype(F32)).astype(jnp.bfloat16)


def product(a, b):
    return lax.dot_general(a, b, (((1,), (0,)), ((), ())), preferred_element_type=F32)


def spread(a, b):
    high, low = halves(a)
    b = b.astype(jnp.bfloat16)
    return product(high, b) + product(low, b)


def select_rows(a, b):
    high, low = halves(b)
    a = a.astype(jnp.bfloat16)
    return product(a, high) + product(a, low)


def rotate(a, shift, axis):
    shift = shift % a.shape[axis]
    return a if shift == 0 else pltpu.roll(a, shift, axis)


class Level:
    def __init__(self, s, no, fk, scale, closed, block, steps=None):
        self.f, self.k = fk.at[0], fk.at[1]
        self.xin, self.dr, self.db = s[f"xin{no}"], s[f"dr{no}"], s[f"db{no}"]
        self.v = {"r": s[f"vr{no}"], "b": s[f"vb{no}"]}
        self.xo, self.y, self.z, self.i, self.g = (
            {c: s[f"{n}{c}{no}"] for c in "rb"} for n in ("xo", "wy", "wz", "inv", "src")
        )
        self.pairs, self.rows, self.lanes = self.xin.shape
        self.scale, self.closed, self.block, self.steps = (scale, closed, block, steps)

    def even(self):
        shape = (self.rows, self.lanes)
        row = iota(shape, 0) if self.steps is None else iota(shape, 0) // 8
        return (row + iota(shape, 1)) & 1 == 0

    def read(self, ref, p):
        if self.steps is None:
            return ref[p]
        tiles = []
        for t in range(0, self.lanes, 128):
            rows = [ref[t // 128, p, pl.ds(r, 8, self.steps), :] for r in range(self.steps)]
            tiles.append(jnp.concatenate(rows, axis=0))
        return jnp.concatenate(tiles, axis=1)

    def shift(self, a, way):
        if self.steps is None:
            return rotate(a, way, 0)
        if way == 1:
            return jnp.concatenate([rotate(a[self.rows - 8 :], 1, 0), a[: self.rows - 8]], axis=0)
        return jnp.concatenate([a[8:], rotate(a[:8], -1, 0)], axis=0)

    def loop(self, lo, hi, body):
        block = min(self.block, hi - lo)
        if block == hi - lo:
            for j in range(lo, hi):
                body(j)
            return

        def step(i, carry):
            for t in range(block):
                body(lo + i * block + t)
            return carry

        lax.fori_loop(0, (hi - lo) // block, step, 0)
        for j in range(lo + (hi - lo) // block * block, hi):
            body(j)

    def prepare(self, lo, hi):
        shape = (self.rows, self.lanes)
        hs = self.scale

        def times(a):
            return a if hs == 1.0 else hs * a

        def one(before, k, after):
            kyl, kyu = self.shift(k, 1), self.shift(k, -1)
            kzl, kzu = rotate(k, 1, 1), rotate(k, -1, 1)
            wy, wz = times(k + kyl), times(k + kzl)
            if self.closed:
                row, lane = iota(shape, 0), iota(shape, 1)
                kyl = jnp.where(row == 0, 0.0, kyl)
                kyu = jnp.where(row == self.rows - 1, 0.0, kyu)
                kzl = jnp.where(lane == 0, 0.0, kzl)
                kzu = jnp.where(lane == self.lanes - 1, 0.0, kzu)
                wy = jnp.where(row == 0, 0.0, wy)
                wz = jnp.where(lane == 0, 0.0, wz)
            diag = times(6.0 * k + before + after + kyl + kyu + kzl + kzu)
            inside = k > 0.0
            inv = jnp.where(inside, 1.0 / jnp.where(inside, diag, 1.0), 0.0)
            return wy, wz, inv, diag

        def body(j):
            even = self.even()
            k = [self.read(self.k, 2 * j - 2 + n) for n in range(4)]
            first, second = one(k[0], k[1], k[2]), one(k[1], k[2], k[3])
            below = times(k[0] + k[1])
            above = times(k[2] + k[3])
            self.xin[j] = times(k[1] + k[2])
            self.xo["r"][j] = jnp.where(even, below, above)
            self.xo["b"][j] = jnp.where(even, above, below)
            for ref, n in ((self.y, 0), (self.z, 1), (self.i, 2)):
                ref["r"][j] = jnp.where(even, first[n], second[n])
                ref["b"][j] = jnp.where(even, second[n], first[n])
            self.dr[j] = jnp.where(even, first[3], second[3])
            self.db[j] = jnp.where(even, second[3], first[3])

        self.loop(lo, hi, body)

    def sources(self, lo, hi):
        def body(j):
            even = self.even()
            a, b = self.read(self.f, 2 * j - 1), self.read(self.f, 2 * j)
            a, b = a + a, b + b
            red = jnp.where(even, a, b)
            self.g["r"][j] = red
            self.g["b"][j] = jnp.where(even, b, a)
            self.v["r"][j] = self.i["r"][j] * red

        self.loop(lo, hi, body)

    def around(self, colour, other, j):
        far = "b" if colour == "r" else "r"
        u, before, after = other[j], other[j - 1], other[j + 1]
        if colour == "b":
            before, after = after, before
        total = self.xin[j] * u + self.xo[colour][j] * jnp.where(self.even(), before, after)
        total = total + (self.y[colour][j] * self.shift(u, 1) + self.shift(self.y[far][j] * u, -1))
        return total + (self.z[colour][j] * rotate(u, 1, 1) + rotate(self.z[far][j] * u, -1, 1))

    def updated(self, colour, other, j):
        return self.i[colour][j] * (self.g[colour][j] + self.around(colour, other, j))

    def half(self, colour, black, lo, hi):
        target, other = (self.v["r"], black) if colour == "r" else (black, self.v["r"])

        def body(j):
            target[j] = self.updated(colour, other, j)

        self.loop(lo, hi, body)

    def sweep(self, black, red_range, black_range):
        self.half("r", black, *red_range)
        self.half("b", black, *black_range)

    def residual(self, lo, hi, rows, out):
        def body(j):
            r, b = self.v["r"], self.v["b"]
            red = self.g["r"][j] - (self.dr[j] * r[j] - self.around("r", b, j))
            black = self.g["b"][j] - (self.db[j] * b[j] - self.around("b", r, j))
            both = (red + black)[:, 0:128]
            if self.steps is None:
                out[j - lo] = both[rows[0] : rows[1]]
                return
            for t in range(0, self.steps, 2):
                two = both[8 * t : 8 * t + 8] + both[8 * t + 8 : 8 * t + 16]
                out[j - lo, pl.ds(t // 2, 8, self.steps // 2), :] = two

        self.loop(lo, hi, body)

    def correct(self, black, j, value):
        black[j] = jnp.where(self.i["b"][j] > 0.0, black[j] + value, 0.0)

    def planes(self, black, j):
        r, b, even = self.v["r"][j], black[j], self.even()
        return jnp.where(even, r, b), jnp.where(even, b, r)


def row_pairs(ref, count):
    return ref[pl.ds(0, count, 2), :] + ref[pl.ds(1, count, 2), :]


def kernel(f_hbm, k_hbm, out_ref, *scratch):
    names = list(SCRATCH)
    s = dict(zip(names, scratch))
    ix, iy, iz = (lax.axis_index(a) for a in AXES)
    me = (ix, iy, iz)

    def device(off):
        return tuple(lax.rem(me[a] + (off[a] + N), N) for a in range(3))

    send, recv, dummy = s["send"], s["recv"], s["dummy"]
    sent = {}

    def push(src, dst, sem, off):
        pltpu.make_async_remote_copy(
            src_ref=src, dst_ref=dst, send_sem=send.at[sem], recv_sem=recv.at[sem],
            device_id=device(off), device_id_type=MESH,
        ).start()
        size = 1
        for d in src.shape:
            size *= d
        sent[sem] = sent.get(sem, 0) + size // 1024

    def wait(sems, sem):
        view = dummy.at[pl.ds(0, sent[sem])]
        pltpu.make_async_copy(view, view, sems.at[sem]).wait()

    fk0, fk1, fk2, fk3 = s["fk0"], s["fk1"], s["fk2"], s["fk3"]

    l0, l1 = Level(s, 0, fk0, 1.0, False, 12, 6), Level(s, 1, fk1, 0.25, False, 12)
    l2, l3 = Level(s, 2, fk2, 0.25**2, False, 12), Level(s, 3, fk3, 0.25**3, True, 12)

    own0 = [fk0.at[a, 0, pl.ds(5, 16), pl.ds(8, 32)] for a in range(2)]
    loads = [pltpu.make_async_copy(r, own0[a], s["load"].at[a]) for a, r in enumerate((f_hbm, k_hbm))]
    loads[1].start()
    loads[0].start()
    near = [(a, b, c) for a in (-1, 0, 1) for b in (-1, 0, 1) for c in (-1, 0, 1) if (a, b, c) != (0, 0, 0)]
    wide = [(a, b, c) for a in (-2, -1, 0, 1, 2) for b in (-1, 0, 1) for c in (-1, 0, 1) if (a, b, c) != (0, 0, 0)]
    lines = []
    for a in range(3):
        for d in range(1, N):
            lines.append(tuple((d if d <= 4 else d - N) if b == a else 0 for b in range(3)))
    partners = wide + [o for o in lines if o not in wide]
    barrier = pltpu.get_barrier_semaphore()
    for off in partners:
        pl.semaphore_signal(barrier, inc=1, device_id=device(off), device_id_type=MESH)
    loads[1].wait()
    pl.semaphore_wait(barrier, len(partners))

    def pack(own, zp, planes, length):
        left = right = None
        for p in range(planes):
            v = rotate(own(p), 8 * p, 1)
            group = iota(v.shape, 1) // 8
            left = v if p == 0 else jnp.where(group == p, v, left)
            right = v if p == 0 else jnp.where(group == (p + length // 8 - 1) % 16, v, right)
        zp[0], zp[1] = left, right

    def slabs(src, dst, start, nx, w, ny, lead, sem, corners=None):
        for sx in (-1, 0, 1):
            for sy in (-1, 0, 1):
                if (sx, sy) == (0, 0):
                    continue
                xs = {1: (start + nx - w, w, start - w), -1: (start, w, start + nx), 0: (start, nx, start)}[sx]
                ys = {1: (8 + ny - 8, 8, 0), -1: (8, 8, 8 + ny), 0: (8, ny, 8)}[sy]
                a = lead + (pl.ds(xs[0], xs[1]), pl.ds(ys[0], ys[1]), pl.ds(0, 128))
                b = lead + (pl.ds(xs[2], xs[1]), pl.ds(ys[2], ys[1]), pl.ds(0, 128))
                push(src.at[a], dst.at[b], sem, (sx, sy, 0))

    def edges(zp, zr, ny, lead, sem, columns=(-1, 0, 1)):
        for sz in (-1, 1):
            side = 1 if sz == 1 else 0
            for sx in columns:
                for sy in (-1, 0, 1):
                    ys = {1: (ny - 8, 8, 0), -1: (0, 8, 8 + ny), 0: (0, ny, 8)}[sy]
                    a = (side,) + lead + (pl.ds(ys[0], ys[1]),)
                    b = (1 - side, 1 - sx) + lead + (pl.ds(ys[2], ys[1]),)
                    push(zp.at[a], zr.at[b], sem, (sx, sy, sz))

    def place(right, left, at, base):
        lane = iota(right.shape, 1)
        both = rotate(jnp.where(lane // 8 == at, right, left), base - 8 * at, 1)
        return jnp.where((lane >= base) & (lane < base + 8) | (lane >= 120), both, 0.0)

    def slot(p, start, nx):
        return (0, p - start + nx) if p < start else (1, p - start) if p < start + nx else (2, p - start - nx)

    def ghost(zr, lead, p, start, nx, base):
        b, q = slot(p, start, nx)
        return place(zr[(1, b) + lead], zr[(0, b) + lead], q, base)

    def flag(condition):
        return jnp.where(condition, 1.0, 0.0)

    def inside_yz(rows, ny, own_lanes, right_end, lanes):
        row, lane = iota((rows, lanes), 0), iota((rows, lanes), 1)
        in_y = ((row >= 8) | (iy > 0)) & ((row < 8 + ny) | (iy < N - 1))
        in_z = (lane < own_lanes) | ((lane < right_end) & (iz < N - 1)) | ((lane >= right_end) & (iz > 0))
        return jnp.where(in_y & in_z, 1.0, 0.0)

    def inside_x(p, h, nx):
        return flag(ix > 0) if p < h else flag(ix < N - 1) if p >= h + nx else 1.0

    zp0, ze0, zr0, zs0 = s["zp0"], s["ze0"], s["zr0"], s["zs0"]
    slabs(fk0, fk0, 5, 16, 4, 32, (1, 0), 0)
    for sx, a, b in ((1, 16, 0), (-1, 9, 25)):
        push(fk0.at[1, 0, a, pl.ds(8, 32)], fk0.at[1, 0, b, pl.ds(8, 32)], 0, (sx, 0, 0))
    loads[0].wait()
    for a in (1, 0):
        pack(lambda p, a=a: fk0[a, 0, 5 + p, 8:40, :], zp0.at[:, a], 16, 128)
    lane32 = iota((32, 128), 1)
    for side in range(2):
        fs, ks = [rotate(zp0[side, a], 8 * side, 1) for a in range(2)]
        v = jnp.where(lane32 < 32, fs, rotate(fs, -64, 1))
        v = jnp.where(lane32 < 64, v, jnp.where(lane32 < 96, rotate(ks, 64, 1), ks))
        ze0[side] = rotate(v, -8 * side, 1)
    edges(zp0, zr0, 32, (1,), 1, (0,))
    edges(ze0, zs0, 32, (), 1, (-1, 1))
    slabs(fk0, fk0, 5, 16, 4, 32, (0, 0), 20)
    edges(zp0, zr0, 32, (0,), 21, (0,))

    def ghost0(a, p):
        b, q = slot(p, 5, 16)
        if b == 1:
            return ghost(zr0, (a,), p, 5, 16, 0)
        if not 0 < p < 25:
            return jnp.zeros((48, 128), F32)
        return place(zs0[1, b], zs0[0, b], 8 * a + (q if b == 2 else 4 + q - 12), 0)

    lane_r, lane_c = iota((128, 128), 0), iota((128, 128), 1)
    halve1 = jnp.where((lane_r // 2 == lane_c), 0.125, 0.0)
    halve2 = jnp.where((lane_r // 2 == lane_c) & (lane_c < 32), 0.125, 0.0)

    pairk = s["pairk"]
    pair0, pair1, pair2, pair3 = s["pair0"], s["pair1"], s["pair2"], s["pair3"]

    def coarse1(rows, part):
        return spread(rows, part * halve1).reshape(8, 16, 128)

    def coarse2(part):
        flat = pair1.reshape(64, 128)
        return spread(row_pairs(flat, 32), part * halve2).reshape(4, 8, 128)

    def packed2(value):
        total = value[0]
        for q in range(1, 4):
            total = total + rotate(value[q], 32 * q, 1)
        return total

    row8, col8 = iota((8, 8), 0), iota((8, 8), 1)

    def coarse3(part):
        place_rows = jnp.where(row8 == 4 * (ix // 4) + col8 // 2, 1.0, 0.0)
        total = None
        for dx in range(2):
            group = lax.rem(2 * ix + dx, 8)
            into = jnp.where((lane_r < 32) & (lane_c == 16 * group + lane_r // 2), 0.125 * part, 0.0)
            piece = spread(select_rows(place_rows, pair2[dx]), into)
            total = piece if total is None else total + piece
        return total

    def gather(tile, g1, g2, g3, sem):
        g1[ix] = tile
        for d in range(1, N):
            push(g1.at[ix], g1.at[ix], sem, (d, 0, 0))
        yield
        wait(recv, sem)
        g2[iy] = (g1[0] + g1[1]) + (g1[2] + g1[3]) + ((g1[4] + g1[5]) + (g1[6] + g1[7]))
        for d in range(1, N):
            push(g2.at[iy], g2.at[iy], sem + 1, (0, d, 0))
        yield
        wait(recv, sem + 1)
        for o in range(4):
            a, b = g2[2 * o], g2[2 * o + 1]
            g3[iz, 0, o] = jnp.where(iota((8, 128), 0) < 4, a, rotate(b, 4, 0))
            g3[iz, 1, o] = jnp.where(iota((8, 128), 0) < 4, rotate(a, 4, 0), b)
        for d in range(1, N):
            push(g3.at[iz], g3.at[iz], sem + 2, (0, 0, d))
        yield
        wait(recv, sem + 2)

    def unpack3(g3, out):
        group = iota((32, 128), 1) // 16
        for h in range(2):
            blocks = [g3[j, h].reshape(32, 128) for j in range(8)]
            for bit in (4, 2, 1):
                low = group & bit == 0
                for j in range(8):
                    if j & bit:
                        continue
                    a, c = blocks[j], blocks[j + bit]
                    blocks[j] = jnp.where(low, a, rotate(c, 16 * bit, 1))
                    blocks[j + bit] = jnp.where(low, rotate(a, -16 * bit, 1), c)
            for g in range(8):
                out[1 + 8 * h + g] = blocks[g]

    for i in range(8):
        pairk[i] = fk0[1, 0, 5 + 2 * i, 8:40, :] + fk0[1, 0, 6 + 2 * i, 8:40, :]
    k1_own = coarse1(row_pairs(pairk.reshape(256, 128), 128), 1.0)
    fk1[1, 7:15, 8:24, :] = k1_own
    for i in range(4):
        pair1[i] = k1_own[2 * i] + k1_own[2 * i + 1]
    k2_own = coarse2(1.0)
    rk2 = s["rk2"]
    rk2[1, 1, 2] = packed2(k2_own)
    for i in range(2):
        pair2[i] = k2_own[2 * i] + k2_own[2 * i + 1]
    k_gather = gather(coarse3(1.0), s["gk1"], s["gk2"], s["gk3"], 10)
    pack(lambda p: fk1[1, 7 + p, 8:24, :], s["zk1"], 8, 64)

    for lev, last in ((l0, 13), (l1, 11), (l2, 11), (l3, 9)):
        for colour in "rb":
            for j in (0, last):
                lev.v[colour][j] = jnp.zeros((lev.rows, lev.lanes), F32)
    for j in (0, 13):
        s["v0"][j] = jnp.zeros((48, 256), F32)
    for j in (0, 11):
        s["v1"][j] = jnp.zeros((32, 128), F32)
        s["v2"][j] = jnp.zeros((24, 128), F32)
    for p in (0, 21):
        fk1[1, p] = jnp.zeros((32, 128), F32)
        fk2[1, p] = jnp.zeros((24, 128), F32)
    for j in (1, 2, 9, 10):
        l2.v["r"][j] = jnp.zeros((24, 128), F32)
    for p in (1, 20):
        fk1[0, p] = jnp.zeros((32, 128), F32)
    for p in (0, 17):
        fk3[1, p] = jnp.zeros((32, 128), F32)
    u3 = s["u3"]
    for p in (0, 1, 2, 3, 20, 21, 22, 23):
        u3[p] = jnp.zeros((32, 128), F32)

    wait(recv, 0)
    wait(recv, 1)
    wait(send, 0)
    next(k_gather)
    for sx in (-2, -1, 1, 2):
        push(rk2.at[1, 1, 2], rk2.at[1, 1, 2 - sx], 16, (sx, 0, 0))
    slabs(fk1, fk1, 7, 8, 6, 16, (1,), 2)
    edges(s["zk1"], s["zrk1"], 16, (), 3)
    myz0 = inside_yz(48, 32, 128, 192, 256)
    row48 = iota((48, 128), 0)
    for p in range(26):
        sx = inside_x(p, 5, 16)
        main = fk0[1, 0, p] * (myz0[:, 0:128] * sx)
        if not 0 < p < 25:
            main = jnp.where((row48 >= 8) & (row48 < 40), main, 0.0)
        fk0[1, 0, p] = main
        fk0[1, 1, p] = ghost0(1, p) * (myz0[:, 128:256] * sx)
    l0.prepare(1, 13)
    wait(recv, 20)
    wait(recv, 21)
    for p in range(1, 25):
        fk0[0, 1, p] = ghost0(0, p)
    l0.sources(1, 13)
    l0.half("b", l0.v["b"], 1, 13)
    l0.sweep(l0.v["b"], (2, 12), (2, 12))
    l0.residual(3, 11, (8, 40), pair0)
    f1_own = coarse1(pair0[:, 4:20, :].reshape(128, 128), 0.5)
    fk1[0, 7:15, 8:24, :] = f1_own

    slabs(fk1, fk1, 7, 8, 5, 16, (0,), 4)
    pack(lambda p: fk1[0, 7 + p, 8:24, :], s["zf1"], 8, 64)
    edges(s["zf1"], s["zrf1"], 16, (), 5)
    wait(recv, 16)
    for sy in (-1, 1):
        push(rk2.at[1, 1], rk2.at[1, 1 - sy], 22, (0, sy, 0))
    wait(recv, 2)
    wait(recv, 3)
    wait(send, 2)
    myz1 = inside_yz(32, 16, 64, 96, 128)
    for p in range(1, 21):
        v = jnp.where(lane32 < 64, fk1[1, p], ghost(s["zrk1"], (), p, 7, 8, 64))
        fk1[1, p] = v * (myz1 * inside_x(p, 7, 8))
    l1.prepare(1, 11)
    wait(recv, 22)
    for sz in (-1, 1):
        push(rk2.at[1], rk2.at[1 - sz], 23, (0, 0, sz))
    next(k_gather)

    lane8 = iota((8, 128), 1)

    def unpack2(block, b, q, by):
        own = rotate(block(b, by, 1), -32 * q, 1)
        right = rotate(block(b, by, 2), 32 * (1 - q), 1)
        left = rotate(block(b, by, 0), 32 * (3 - q), 1)
        return jnp.where(lane8 < 32, own, jnp.where(lane8 < 64, right, jnp.where(lane8 >= 96, left, 0.0)))

    row24, lane24 = iota((24, 128), 0), iota((24, 128), 1)
    in_y = ((row24 >= 8) | (iy > 0)) & ((row24 < 16) | (iy < N - 1))
    in_z = (lane24 < 32) | ((lane24 < 64) & (iz < N - 1)) | ((lane24 >= 96) & (iz > 0))
    myz2 = jnp.where(in_y & in_z, 1.0, 0.0)
    wait(recv, 4)
    wait(recv, 5)
    wait(send, 4)
    for p in range(2, 20):
        fk1[0, p] = jnp.where(lane32 < 64, fk1[0, p], ghost(s["zrf1"], (), p, 7, 8, 64))
    l1.sources(1, 11)
    l1.half("b", l1.v["b"], 2, 10)
    l1.sweep(l1.v["b"], (3, 9), (3, 9))
    l1.residual(4, 8, (8, 24), pair1)
    rf2 = s["rf2"]
    rf2[2, 1, 1] = packed2(coarse2(0.5))

    far = [off for off in wide if off not in near]
    for sem, group in ((6, near), (19, far)):
        for off in group:
            push(rf2.at[2, 1, 1], rf2.at[2 - off[0], 1 - off[1], 1 - off[2]], sem, off)

    def source2(boxes):
        for b in boxes:
            for p in range(4 * b, 4 * b + 4):
                for by in range(3):
                    fk2[0, 1 + p, 8 * by : 8 * by + 8, :] = unpack2(lambda i, j, k: rf2[i, j, k], b, p % 4, by)
            l2.sources(1 + 2 * b, 3 + 2 * b)

    wait(recv, 23)
    for p in range(20):
        b, q = divmod(p, 4)
        sx = [flag(ix > 1), flag(ix > 0), 1.0, flag(ix < N - 1), flag(ix < N - 2)][b]
        for by in range(3):
            v = unpack2(lambda i, j, k: rk2[k, j, i], b, q, by)
            fk2[1, 1 + p, 8 * by : 8 * by + 8, :] = v * (myz2[8 * by : 8 * by + 8] * sx)
    l2.prepare(1, 11)

    wait(recv, 6)
    next(k_gather)
    source2((1, 2, 3))
    l2.half("b", l2.v["b"], 3, 9)
    l2.sweep(l2.v["b"], (4, 8), (4, 8))
    l2.residual(5, 7, (8, 16), pair2)
    f_gather = gather(coarse3(0.5), s["gf1"], s["gf2"], s["gf3"], 13)
    next(f_gather)
    slabs(l1.v["b"], s["v1"], 4, 4, 3, 16, (), 7)
    pack(lambda p: l1.v["b"][4 + p, 8:24, :], s["zpu1"], 4, 64)
    edges(s["zpu1"], s["zru1"], 16, (), 8)
    s["v1"][4:8, 8:24, :] = l1.v["b"][4:8, 8:24, :]
    vb0n, v0n = s["vb0n"], s["v0n"]
    for j in range(3, 11):
        for t in range(6):
            vb0n[j, pl.ds(t, 8, 6), :] = l0.v["b"][j, 8 * t : 8 * t + 8, 0:128]
    pack(lambda p: vb0n[3 + p, 8:40, :], s["zpu0"], 8, 128)
    v0n[0, 3:11, 8:40, :] = vb0n[3:11, 8:40, :]
    next(f_gather)
    slabs(vb0n, v0n.at[0], 3, 8, 2, 32, (), 17)
    edges(s["zpu0"], s["zru0"], 32, (), 18)
    wait(recv, 19)
    source2((0, 4))
    for _ in k_gather:
        pass
    unpack3(s["gk3"], fk3.at[1])
    l3.prepare(1, 9)
    next(f_gather)
    ru2 = s["ru2"]
    total = jnp.where(lane8 < 32, l2.v["b"][5, 8:16, :], 0.0)
    ru2[2, 1, 1] = total + rotate(jnp.where(lane8 < 32, l2.v["b"][6, 8:16, :], 0.0), 32, 1)
    for off in wide:
        push(ru2.at[2, 1, 1], ru2.at[2 - off[0], 1 - off[1], 1 - off[2]], 9, off)
    pair3_flat = pair3.reshape(8 * 32, 128)

    def coarse4(part):
        rows = row_pairs(pair3_flat, 128).reshape(8, 16, 128)
        out = None
        for h in range(2):
            into = jnp.where(lane_c == 64 * h + lane_r // 2, 0.125 * part, 0.0)
            piece = spread(rows[4 * h : 4 * h + 4].reshape(64, 128), into)
            out = piece if out is None else out + piece
        return out.reshape(4, 16, 128)

    for i in range(8):
        pair3[i] = fk3[1, 1 + 2 * i] + fk3[1, 2 + 2 * i]
    k4 = coarse4(1.0)
    shape4 = (4, 16, 128)
    row4, lane4 = iota(shape4, 1), iota(shape4, 2)
    z4 = lane4 & 63

    def cat(parts):
        return jnp.concatenate(parts, axis=0)

    def x_below(v):
        return cat([rotate(v[3], 64, 1)[None], v[0:3]])

    def x_above(v):
        return cat([v[1:4], rotate(v[0], 64, 1)[None]])

    def roll3(v, shift, axis):
        flat = [rotate(v[i], shift, axis)[None] for i in range(4)]
        return cat(flat)

    plane4 = iota(shape4, 0)
    first_x = (plane4 == 0) & (lane4 < 64)
    last_x = (plane4 == 3) & (lane4 >= 64)
    hs4 = 0.5 * 0.25**4
    kxl, kxu = jnp.where(first_x, 0.0, x_below(k4)), jnp.where(last_x, 0.0, x_above(k4))
    kyl = jnp.where(row4 == 0, 0.0, roll3(k4, 1, 0))
    kyu = jnp.where(row4 == 15, 0.0, roll3(k4, -1, 0))
    kzl = jnp.where(z4 == 0, 0.0, roll3(k4, 1, 1))
    kzu = jnp.where(z4 == 63, 0.0, roll3(k4, -1, 1))
    w4 = s["w4"]
    inv4 = 1.0 / (hs4 * (6.0 * k4 + kxl + kxu + kyl + kyu + kzl + kzu))
    odd4 = (plane4 + row4 + lane4) & 1
    w4[0] = jnp.where(first_x, 0.0, hs4 * (k4 + kxl))
    w4[1] = jnp.where(last_x, 0.0, hs4 * (k4 + kxu))
    w4[2] = jnp.where(row4 == 0, 0.0, hs4 * (k4 + kyl))
    w4[3] = jnp.where(row4 == 15, 0.0, hs4 * (k4 + kyu))
    w4[4] = jnp.where(z4 == 0, 0.0, hs4 * (k4 + kzl))
    w4[5] = jnp.where(z4 == 63, 0.0, hs4 * (k4 + kzu))
    w4[6] = jnp.where(odd4 == 0, inv4, 0.0)
    w4[7] = jnp.where(odd4 == 1, inv4, 0.0)

    for _ in f_gather:
        pass
    unpack3(s["gf3"], fk3.at[0])
    l3.sources(1, 9)
    l3.half("b", l3.v["b"], 1, 9)
    l3.sweep(l3.v["b"], (1, 9), (1, 9))
    l3.residual(1, 9, (0, 32), pair3)
    f4 = coarse4(0.5)
    w4[8] = f4

    def around4(v):
        total = w4[0] * x_below(v) + w4[1] * x_above(v)
        total = total + (w4[2] * roll3(v, 1, 0) + w4[3] * roll3(v, -1, 0))
        return total + (w4[4] * roll3(v, 1, 1) + w4[5] * roll3(v, -1, 1))

    def bottom(i, carry):
        black = carry[1]
        red = w4[6] * (w4[8] + around4(black))
        black = w4[7] * (w4[8] + around4(red))
        return (red, black)

    zero4 = jnp.zeros(shape4, F32)
    red4, black4 = lax.fori_loop(0, BOTTOM, bottom, (zero4, zero4))
    u4 = red4 + black4

    for h in range(2):
        into = jnp.where(lane_r == 64 * h + lane_c // 2, 1.0, 0.0)
        wide4 = spread(u4.reshape(64, 128), into)
        pair3_flat[pl.ds(128 * h, 64, 2), :] = wide4
        pair3_flat[pl.ds(128 * h + 1, 64, 2), :] = wide4
    v3 = l3.v["b"]
    for j in range(1, 9):
        l3.correct(v3, j, pair3[j - 1])
    for _ in range(2):
        l3.sweep(v3, (1, 9), (1, 9))
    for j in range(1, 9):
        u3[2 + 2 * j], u3[3 + 2 * j] = l3.planes(v3, j)

    v2 = s["v2"]
    zoff = jnp.where(lane_c < 64, lane_c, lane_c - 128)
    source_lane = 16 * iz + ((zoff + 128) // 2 - 64)
    spread_z = jnp.where((lane_r == source_lane) & ((lane_c < 64) | (lane_c >= 96)), 1.0, 0.0)
    spread_y = jnp.where(iota((24, 32), 1) == 4 * iy - 4 + iota((24, 32), 0) // 2, 1.0, 0.0)
    stretched = spread(u3[pl.ds(2 * ix, 10)].reshape(320, 128), spread_z)
    side_by_side = jnp.concatenate([stretched[32 * j : 32 * j + 32] for j in range(10)], axis=1)
    corr2 = select_rows(spread_y, side_by_side)
    wait(recv, 9)
    for j in range(1, 11):
        b, q = divmod(j - 1, 2)
        for by in range(3):
            v2[j, 8 * by : 8 * by + 8, :] = unpack2(lambda i, j, k: ru2[i, j, k], b, q, by)
        l2.correct(v2, j, corr2[:, 128 * (j - 1) : 128 * j])
    l2.sweep(v2, (2, 10), (2, 10))
    l2.sweep(v2, (3, 9), (3, 9))

    spread1 = jnp.where(lane_r == jnp.where(lane_c >= 96, 64 + lane_c // 2, lane_c // 2), 1.0, 0.0)
    up1 = s["up1"]
    coarse = []
    for j in range(3, 9):
        coarse += list(l2.planes(v2, j))
    up1[...] = spread(jnp.concatenate(coarse[1:11], axis=0), spread1).reshape(10, 24, 128)
    tall1 = s["tall1"]
    wait(recv, 7)
    wait(recv, 8)
    v1 = s["v1"]
    for j in range(1, 11):
        v1[j] = jnp.where(lane32 < 64, v1[j], ghost(s["zru1"], (), j, 4, 4, 64))
        part = up1[j - 1, 4:20, :]
        tall1[j - 1, pl.ds(0, 16, 2), :] = part
        tall1[j - 1, pl.ds(1, 16, 2), :] = part
        l1.correct(v1, j, tall1[j - 1])
    l1.sweep(v1, (1, 11), (2, 10))
    l1.sweep(v1, (2, 10), (3, 9))

    spread0 = jnp.where(iota((128, 256), 0) == iota((128, 256), 1) // 2, 1.0, 0.0)
    up0 = s["up0"]
    coarse = []
    for j in range(3, 9):
        coarse += list(l1.planes(v1, j))
    wide0 = spread(jnp.concatenate(coarse, axis=0), spread0).reshape(12, 32, 256)
    up0[0], up0[1] = wide0[:, :, 0:128], wide0[:, :, 128:256]
    wait(recv, 17)
    wait(recv, 18)
    v0 = s["v0"]
    for j in range(1, 13):
        v0n[1, j] = ghost(s["zru0"], (), j, 3, 8, 0)
    for j in range(1, 13):
        tiles = []
        for t in range(2):
            rows = [up0[t, j - 1, pl.ds(4 + c, 8, 3), :] for c in range(3)]
            tiles.append(jnp.concatenate([rows[c // 2] for c in range(6)], axis=0))
        corr = jnp.concatenate(tiles, axis=1)
        v0[j] = jnp.where(l0.i["b"][j] > 0.0, l0.read(v0n, j) + corr, 0.0)
    l0.sweep(v0, (1, 13), (2, 12))
    l0.half("r", v0, 2, 12)
    outn = s["outn"]

    def last(j):
        black = l0.updated("b", l0.v["r"], j)
        red, even = l0.v["r"][j], l0.even()
        for n, plane in enumerate((jnp.where(even, red, black), jnp.where(even, black, red))):
            for t in range(6):
                outn[2 * j - 6 + n, pl.ds(t, 8, 6), :] = plane[8 * t : 8 * t + 8, 0:128]

    l0.loop(3, 11, last)
    out_ref[...] = outn[:, 8:40, :]
    for sem in sorted(sent):
        if sem not in (0, 2, 4):
            wait(send, sem)


def vmem(*shape):
    return pltpu.VMEM(shape, F32)


def scratch_shapes():
    shapes = {}
    sizes = [(26, 12, 48, 256), (22, 10, 32, 128), (22, 10, 24, 128), (18, 8, 32, 128)]
    for no, (planes, pairs, rows, lanes) in enumerate(sizes):
        shapes[f"fk{no}"] = vmem(2, 2, planes, rows, 128) if no == 0 else vmem(2, planes, rows, lanes)
        names = ["xin", "dr", "db"] + [n + c for n in ("v", "xo", "wy", "wz", "inv", "src") for c in "rb"]
        for name in names + (["v"] if no < 3 else []):
            shapes[f"{name}{no}"] = vmem(pairs + 2, rows, lanes)
    shapes["zp0"], shapes["zr0"] = vmem(2, 2, 32, 128), vmem(2, 3, 2, 48, 128)
    shapes["ze0"], shapes["zs0"] = vmem(2, 32, 128), vmem(2, 3, 48, 128)
    shapes["zpu0"], shapes["zru0"] = vmem(2, 32, 128), vmem(2, 3, 48, 128)
    for name in ("k1", "f1", "pu1"):
        shapes["z" + name] = vmem(2, 16, 128)
    for name in ("zrk1", "zrf1", "zru1"):
        shapes[name] = vmem(2, 3, 32, 128)
    for name in ("rf2", "ru2"):
        shapes[name] = vmem(5, 3, 3, 8, 128)
    shapes["rk2"] = vmem(3, 3, 5, 8, 128)
    for name in "kf":
        shapes[f"g{name}1"] = vmem(8, 8, 128)
        shapes[f"g{name}2"] = vmem(8, 8, 128)
        shapes[f"g{name}3"] = vmem(8, 2, 4, 8, 128)
    shapes["pair0"], shapes["pair1"] = vmem(8, 24, 128), vmem(4, 16, 128)
    shapes["pairk"], shapes["outn"] = vmem(8, 32, 128), vmem(16, 48, 128)
    shapes["vb0n"], shapes["v0n"] = vmem(14, 48, 128), vmem(2, 14, 48, 128)
    shapes["pair2"], shapes["pair3"] = vmem(2, 8, 128), vmem(8, 32, 128)
    shapes["w4"], shapes["u3"] = vmem(9, 4, 16, 128), vmem(24, 32, 128)
    shapes["up0"] = vmem(2, 12, 32, 128)
    shapes["up1"], shapes["tall1"] = vmem(10, 24, 128), vmem(10, 32, 128)
    shapes["dummy"] = vmem(256, 8, 128)
    shapes["send"] = pltpu.SemaphoreType.DMA((24,))
    shapes["recv"] = pltpu.SemaphoreType.DMA((24,))
    shapes["load"] = pltpu.SemaphoreType.DMA((2,))
    return shapes


SCRATCH = scratch_shapes()


def on_device(source_term, conductivity):
    return pl.pallas_call(
        kernel,
        out_shape=jax.ShapeDtypeStruct((16, 32, 128), F32),
        in_specs=[pl.BlockSpec(memory_space=pl.ANY)] * 2,
        out_specs=pl.BlockSpec(memory_space=pltpu.VMEM),
        scratch_shapes=list(SCRATCH.values()),
        compiler_params=pltpu.CompilerParams(
            collective_id=0, has_side_effects=True, vmem_limit_bytes=107 * 2**19
        ),
        name="vcycle",
    )(source_term, conductivity)


def solution(mesh):
    spec = P("gx", "gy", "gz")
    return jax.shard_map(
        on_device, mesh=mesh, in_specs=(spec, spec), out_specs=spec, check_vma=False
    )
```

```python
import functools

import jax
import jax.numpy as jnp
from jax import lax
from jax.experimental import pallas as pl
from jax.experimental.pallas import tpu as pltpu
from jax.sharding import PartitionSpec as P

MESH = pl.DeviceIdType.MESH
AXES = ("gx", "gy", "gz")
N = 8
BOTTOM = 16
F32 = jnp.float32


def iota(shape, axis):
    return lax.broadcasted_iota(jnp.int32, shape, axis)


def halves(a):
    high = a.astype(jnp.bfloat16)
    return high, (a - high.astype(F32)).astype(jnp.bfloat16)


def product(a, b):
    return lax.dot_general(a, b, (((1,), (0,)), ((), ())), preferred_element_type=F32)


def spread(a, b):
    high, low = halves(a)
    b = b.astype(jnp.bfloat16)
    return product(high, b) + product(low, b)


def select_rows(a, b):
    high, low = halves(b)
    a = a.astype(jnp.bfloat16)
    return product(a, high) + product(a, low)


def rotate(a, shift, axis):
    shift = shift % a.shape[axis]
    return a if shift == 0 else pltpu.roll(a, shift, axis)


class Level:
    def __init__(self, s, no, fk, scale, closed, block, steps=None):
        self.f, self.k = fk.at[0], fk.at[1]
        self.xin, self.dr, self.db = s[f"xin{no}"], s[f"dr{no}"], s[f"db{no}"]
        self.v = {"r": s[f"vr{no}"], "b": s[f"vb{no}"]}
        self.xo, self.y, self.z, self.i, self.g = (
            {c: s[f"{n}{c}{no}"] for c in "rb"} for n in ("xo", "wy", "wz", "inv", "src")
        )
        self.pairs, self.rows, self.lanes = self.xin.shape
        self.scale, self.closed, self.block, self.steps = (scale, closed, block, steps)

    def even(self):
        shape = (self.rows, self.lanes)
        row = iota(shape, 0) if self.steps is None else iota(shape, 0) // 8
        return (row + iota(shape, 1)) & 1 == 0

    def read(self, ref, p):
        if self.steps is None:
            return ref[p]
        tiles = []
        for t in range(0, self.lanes, 128):
            rows = [ref[t // 128, p, pl.ds(r, 8, self.steps), :] for r in range(self.steps)]
            tiles.append(jnp.concatenate(rows, axis=0))
        return jnp.concatenate(tiles, axis=1)

    def shift(self, a, way):
        if self.steps is None:
            return rotate(a, way, 0)
        if way == 1:
            return jnp.concatenate([rotate(a[self.rows - 8 :], 1, 0), a[: self.rows - 8]], axis=0)
        return jnp.concatenate([a[8:], rotate(a[:8], -1, 0)], axis=0)

    def loop(self, lo, hi, body):
        block = min(self.block, hi - lo)
        if block == hi - lo:
            for j in range(lo, hi):
                body(j)
            return

        def step(i, carry):
            for t in range(block):
                body(lo + i * block + t)
            return carry

        lax.fori_loop(0, (hi - lo) // block, step, 0)
        for j in range(lo + (hi - lo) // block * block, hi):
            body(j)

    def prepare(self, lo, hi):
        shape = (self.rows, self.lanes)
        hs = self.scale

        def times(a):
            return a if hs == 1.0 else hs * a

        def one(before, k, after):
            kyl, kyu = self.shift(k, 1), self.shift(k, -1)
            kzl, kzu = rotate(k, 1, 1), rotate(k, -1, 1)
            wy, wz = times(k + kyl), times(k + kzl)
            if self.closed:
                row, lane = iota(shape, 0), iota(shape, 1)
                kyl = jnp.where(row == 0, 0.0, kyl)
                kyu = jnp.where(row == self.rows - 1, 0.0, kyu)
                kzl = jnp.where(lane == 0, 0.0, kzl)
                kzu = jnp.where(lane == self.lanes - 1, 0.0, kzu)
                wy = jnp.where(row == 0, 0.0, wy)
                wz = jnp.where(lane == 0, 0.0, wz)
            diag = times(6.0 * k + before + after + kyl + kyu + kzl + kzu)
            inside = k > 0.0
            inv = jnp.where(inside, 1.0 / jnp.where(inside, diag, 1.0), 0.0)
            return wy, wz, inv, diag

        def body(j):
            even = self.even()
            k = [self.read(self.k, 2 * j - 2 + n) for n in range(4)]
            first, second = one(k[0], k[1], k[2]), one(k[1], k[2], k[3])
            below = times(k[0] + k[1])
            above = times(k[2] + k[3])
            self.xin[j] = times(k[1] + k[2])
            self.xo["r"][j] = jnp.where(even, below, above)
            self.xo["b"][j] = jnp.where(even, above, below)
            for ref, n in ((self.y, 0), (self.z, 1), (self.i, 2)):
                ref["r"][j] = jnp.where(even, first[n], second[n])
                ref["b"][j] = jnp.where(even, second[n], first[n])
            self.dr[j] = jnp.where(even, first[3], second[3])
            self.db[j] = jnp.where(even, second[3], first[3])

        self.loop(lo, hi, body)

    def sources(self, lo, hi):
        def body(j):
            even = self.even()
            a, b = self.read(self.f, 2 * j - 1), self.read(self.f, 2 * j)
            a, b = a + a, b + b
            red = jnp.where(even, a, b)
            self.g["r"][j] = red
            self.g["b"][j] = jnp.where(even, b, a)
            self.v["r"][j] = self.i["r"][j] * red

        self.loop(lo, hi, body)

    def around(self, colour, other, j):
        far = "b" if colour == "r" else "r"
        u, before, after = other[j], other[j - 1], other[j + 1]
        if colour == "b":
            before, after = after, before
        total = self.xin[j] * u + self.xo[colour][j] * jnp.where(self.even(), before, after)
        total = total + (self.y[colour][j] * self.shift(u, 1) + self.shift(self.y[far][j] * u, -1))
        return total + (self.z[colour][j] * rotate(u, 1, 1) + rotate(self.z[far][j] * u, -1, 1))

    def updated(self, colour, other, j):
        return self.i[colour][j] * (self.g[colour][j] + self.around(colour, other, j))

    def half(self, colour, black, lo, hi):
        target, other = (self.v["r"], black) if colour == "r" else (black, self.v["r"])

        def body(j):
            target[j] = self.updated(colour, other, j)

        self.loop(lo, hi, body)

    def sweep(self, black, red_range, black_range):
        self.half("r", black, *red_range)
        self.half("b", black, *black_range)

    def residual(self, lo, hi, rows, out):
        def body(j):
            r, b = self.v["r"], self.v["b"]
            red = self.g["r"][j] - (self.dr[j] * r[j] - self.around("r", b, j))
            black = self.g["b"][j] - (self.db[j] * b[j] - self.around("b", r, j))
            both = (red + black)[:, 0:128]
            if self.steps is None:
                out[j - lo] = both[rows[0] : rows[1]]
                return
            for t in range(0, self.steps, 2):
                two = both[8 * t : 8 * t + 8] + both[8 * t + 8 : 8 * t + 16]
                out[j - lo, pl.ds(t // 2, 8, self.steps // 2), :] = two

        self.loop(lo, hi, body)

    def correct(self, black, j, value):
        black[j] = jnp.where(self.i["b"][j] > 0.0, black[j] + value, 0.0)

    def planes(self, black, j):
        r, b, even = self.v["r"][j], black[j], self.even()
        return jnp.where(even, r, b), jnp.where(even, b, r)


def row_pairs(ref, count):
    return ref[pl.ds(0, count, 2), :] + ref[pl.ds(1, count, 2), :]


def kernel(f_hbm, k_hbm, out_ref, *scratch):
    names = list(SCRATCH)
    s = dict(zip(names, scratch))
    ix, iy, iz = (lax.axis_index(a) for a in AXES)
    me = (ix, iy, iz)

    def device(off):
        return tuple(lax.rem(me[a] + (off[a] + N), N) for a in range(3))

    send, recv, dummy = s["send"], s["recv"], s["dummy"]
    sent = {}

    def push(src, dst, sem, off):
        pltpu.make_async_remote_copy(
            src_ref=src, dst_ref=dst, send_sem=send.at[sem], recv_sem=recv.at[sem],
            device_id=device(off), device_id_type=MESH,
        ).start()
        size = 1
        for d in src.shape:
            size *= d
        sent[sem] = sent.get(sem, 0) + size // 1024

    def wait(sems, sem):
        view = dummy.at[pl.ds(0, sent[sem])]
        pltpu.make_async_copy(view, view, sems.at[sem]).wait()

    fk0, fk1, fk2, fk3 = s["fk0"], s["fk1"], s["fk2"], s["fk3"]

    l0, l1 = Level(s, 0, fk0, 1.0, False, 12, 6), Level(s, 1, fk1, 0.25, False, 12)
    l2, l3 = Level(s, 2, fk2, 0.25**2, False, 12), Level(s, 3, fk3, 0.25**3, True, 12)

    own0 = [fk0.at[a, 0, pl.ds(5, 16), pl.ds(8, 32)] for a in range(2)]
    loads = [pltpu.make_async_copy(r, own0[a], s["load"].at[a]) for a, r in enumerate((f_hbm, k_hbm))]
    loads[1].start()
    loads[0].start()
    near = [(a, b, c) for a in (-1, 0, 1) for b in (-1, 0, 1) for c in (-1, 0, 1) if (a, b, c) != (0, 0, 0)]
    wide = [(a, b, c) for a in (-2, -1, 0, 1, 2) for b in (-1, 0, 1) for c in (-1, 0, 1) if (a, b, c) != (0, 0, 0)]
    partners = near + [(d, 0, 0) for d in (-3, -2, 2, 3, 4)]
    barrier = pltpu.get_barrier_semaphore()
    for off in partners:
        pl.semaphore_signal(barrier, inc=1, device_id=device(off), device_id_type=MESH)
    loads[1].wait()
    pl.semaphore_wait(barrier, len(partners))

    def pack(own, zp, planes, length):
        left = right = None
        for p in range(planes):
            v = rotate(own(p), 8 * p, 1)
            group = iota(v.shape, 1) // 8
            left = v if p == 0 else jnp.where(group == p, v, left)
            right = v if p == 0 else jnp.where(group == (p + length // 8 - 1) % 16, v, right)
        zp[0], zp[1] = left, right

    def slabs(src, dst, start, nx, w, ny, lead, sem, corners=None):
        for sx in (-1, 0, 1):
            for sy in (-1, 0, 1):
                if (sx, sy) == (0, 0):
                    continue
                xs = {1: (start + nx - w, w, start - w), -1: (start, w, start + nx), 0: (start, nx, start)}[sx]
                ys = {1: (8 + ny - 8, 8, 0), -1: (8, 8, 8 + ny), 0: (8, ny, 8)}[sy]
                a = lead + (pl.ds(xs[0], xs[1]), pl.ds(ys[0], ys[1]), pl.ds(0, 128))
                b = lead + (pl.ds(xs[2], xs[1]), pl.ds(ys[2], ys[1]), pl.ds(0, 128))
                push(src.at[a], dst.at[b], sem, (sx, sy, 0))

    def edges(zp, zr, ny, lead, sem, columns=(-1, 0, 1)):
        for sz in (-1, 1):
            side = 1 if sz == 1 else 0
            for sx in columns:
                for sy in (-1, 0, 1):
                    ys = {1: (ny - 8, 8, 0), -1: (0, 8, 8 + ny), 0: (0, ny, 8)}[sy]
                    a = (side,) + lead + (pl.ds(ys[0], ys[1]),)
                    b = (1 - side, 1 - sx) + lead + (pl.ds(ys[2], ys[1]),)
                    push(zp.at[a], zr.at[b], sem, (sx, sy, sz))

    def place(right, left, at, base):
        lane = iota(right.shape, 1)
        both = rotate(jnp.where(lane // 8 == at, right, left), base - 8 * at, 1)
        return jnp.where((lane >= base) & (lane < base + 8) | (lane >= 120), both, 0.0)

    def slot(p, start, nx):
        return (0, p - start + nx) if p < start else (1, p - start) if p < start + nx else (2, p - start - nx)

    def ghost(zr, lead, p, start, nx, base):
        b, q = slot(p, start, nx)
        return place(zr[(1, b) + lead], zr[(0, b) + lead], q, base)

    def flag(condition):
        return jnp.where(condition, 1.0, 0.0)

    def inside_yz(rows, ny, own_lanes, right_end, lanes):
        row, lane = iota((rows, lanes), 0), iota((rows, lanes), 1)
        in_y = ((row >= 8) | (iy > 0)) & ((row < 8 + ny) | (iy < N - 1))
        in_z = (lane < own_lanes) | ((lane < right_end) & (iz < N - 1)) | ((lane >= right_end) & (iz > 0))
        return jnp.where(in_y & in_z, 1.0, 0.0)

    def inside_x(p, h, nx):
        return flag(ix > 0) if p < h else flag(ix < N - 1) if p >= h + nx else 1.0

    zp0, ze0, zr0, zs0 = s["zp0"], s["ze0"], s["zr0"], s["zs0"]
    slabs(fk0, fk0, 5, 16, 4, 32, (1, 0), 0)
    for sx, a, b in ((1, 16, 0), (-1, 9, 25)):
        push(fk0.at[1, 0, a, pl.ds(8, 32)], fk0.at[1, 0, b, pl.ds(8, 32)], 0, (sx, 0, 0))
    pack(lambda p: fk0[1, 0, 5 + p, 8:40, :], zp0.at[:, 1], 16, 128)
    edges(zp0, zr0, 32, (1,), 1, (0,))
    loads[0].wait()
    pack(lambda p: fk0[0, 0, 5 + p, 8:40, :], zp0.at[:, 0], 16, 128)
    lane32 = iota((32, 128), 1)
    for side in range(2):
        fs, ks = [rotate(zp0[side, a], 8 * side, 1) for a in range(2)]
        v = jnp.where(lane32 < 32, fs, rotate(fs, -64, 1))
        v = jnp.where(lane32 < 64, v, jnp.where(lane32 < 96, rotate(ks, 64, 1), ks))
        ze0[side] = rotate(v, -8 * side, 1)
    edges(ze0, zs0, 32, (), 1, (-1, 1))
    slabs(fk0, fk0, 5, 16, 4, 32, (0, 0), 20)
    edges(zp0, zr0, 32, (0,), 21, (0,))

    def ghost0(a, p):
        b, q = slot(p, 5, 16)
        if b == 1:
            return ghost(zr0, (a,), p, 5, 16, 0)
        if not 0 < p < 25:
            return jnp.zeros((48, 128), F32)
        return place(zs0[1, b], zs0[0, b], 8 * a + (q if b == 2 else 4 + q - 12), 0)

    lane_r, lane_c = iota((128, 128), 0), iota((128, 128), 1)
    halve1 = jnp.where((lane_r // 2 == lane_c), 0.125, 0.0)
    halve2 = jnp.where((lane_r // 2 == lane_c) & (lane_c < 32), 0.125, 0.0)

    pairk = s["pairk"]
    pair0, pair1, pair2, pair3 = s["pair0"], s["pair1"], s["pair2"], s["pair3"]

    def coarse1(rows, part):
        return spread(rows, part * halve1).reshape(8, 16, 128)

    def coarse2(part):
        flat = pair1.reshape(64, 128)
        return spread(row_pairs(flat, 32), part * halve2).reshape(4, 8, 128)

    def packed2(value):
        total = value[0]
        for q in range(1, 4):
            total = total + rotate(value[q], 32 * q, 1)
        return total

    row8, col8 = iota((8, 8), 0), iota((8, 8), 1)

    def coarse3(part):
        place_rows = jnp.where(row8 == 4 * (ix // 4) + col8 // 2, 1.0, 0.0)
        total = None
        for dx in range(2):
            group = lax.rem(2 * ix + dx, 8)
            into = jnp.where((lane_r < 32) & (lane_c == 16 * group + lane_r // 2), 0.125 * part, 0.0)
            piece = spread(select_rows(place_rows, pair2[dx]), into)
            total = piece if total is None else total + piece
        return total

    def gather(tile, g1, g2, g3, sem):
        g1[ix] = tile
        for d in range(1, N):
            push(g1.at[ix], g1.at[ix], sem, (d, 0, 0))
        yield
        wait(recv, sem)
        g2[iy] = (g1[0] + g1[1]) + (g1[2] + g1[3]) + ((g1[4] + g1[5]) + (g1[6] + g1[7]))
        for d in range(1, N):
            push(g2.at[iy], g2.at[iy], sem + 1, (0, d, 0))
        yield
        wait(recv, sem + 1)
        for o in range(4):
            a, b = g2[2 * o], g2[2 * o + 1]
            g3[iz, 0, o] = jnp.where(iota((8, 128), 0) < 4, a, rotate(b, 4, 0))
            g3[iz, 1, o] = jnp.where(iota((8, 128), 0) < 4, rotate(a, 4, 0), b)
        for d in range(1, N):
            push(g3.at[iz], g3.at[iz], sem + 2, (0, 0, d))
        yield
        wait(recv, sem + 2)

    def unpack3(g3, out):
        group = iota((32, 128), 1) // 16
        for h in range(2):
            blocks = [g3[j, h].reshape(32, 128) for j in range(8)]
            for bit in (4, 2, 1):
                low = group & bit == 0
                for j in range(8):
                    if j & bit:
                        continue
                    a, c = blocks[j], blocks[j + bit]
                    blocks[j] = jnp.where(low, a, rotate(c, 16 * bit, 1))
                    blocks[j + bit] = jnp.where(low, rotate(a, -16 * bit, 1), c)
            for g in range(8):
                out[1 + 8 * h + g] = blocks[g]

    for i in range(8):
        pairk[i] = fk0[1, 0, 5 + 2 * i, 8:40, :] + fk0[1, 0, 6 + 2 * i, 8:40, :]
    k1_own = coarse1(row_pairs(pairk.reshape(256, 128), 128), 1.0)
    fk1[1, 7:15, 8:24, :] = k1_own
    for i in range(4):
        pair1[i] = k1_own[2 * i] + k1_own[2 * i + 1]
    k2_own = coarse2(1.0)
    rk2 = s["rk2"]
    rk2[1, 1, 2] = packed2(k2_own)
    for i in range(2):
        pair2[i] = k2_own[2 * i] + k2_own[2 * i + 1]
    k_gather = gather(coarse3(1.0), s["gk1"], s["gk2"], s["gk3"], 10)
    pack(lambda p: fk1[1, 7 + p, 8:24, :], s["zk1"], 8, 64)

    for lev, last in ((l0, 13), (l1, 11), (l2, 11), (l3, 9)):
        for colour in "rb":
            for j in (0, last):
                lev.v[colour][j] = jnp.zeros((lev.rows, lev.lanes), F32)
    for j in (0, 13):
        s["v0"][j] = jnp.zeros((48, 256), F32)
    for j in (0, 11):
        s["v1"][j] = jnp.zeros((32, 128), F32)
        s["v2"][j] = jnp.zeros((24, 128), F32)
    for p in (0, 21):
        fk1[1, p] = jnp.zeros((32, 128), F32)
        fk2[1, p] = jnp.zeros((24, 128), F32)
    for j in (1, 2, 9, 10):
        l2.v["r"][j] = jnp.zeros((24, 128), F32)
    for p in (1, 20):
        fk1[0, p] = jnp.zeros((32, 128), F32)
    for p in (0, 17):
        fk3[1, p] = jnp.zeros((32, 128), F32)
    u3 = s["u3"]
    for p in (0, 1, 2, 3, 20, 21, 22, 23):
        u3[p] = jnp.zeros((32, 128), F32)

    wait(recv, 0)
    wait(recv, 1)
    wait(send, 0)
    next(k_gather)
    for sx in (-2, -1, 1, 2):
        push(rk2.at[1, 1, 2], rk2.at[1, 1, 2 - sx], 16, (sx, 0, 0))
    slabs(fk1, fk1, 7, 8, 6, 16, (1,), 2)
    edges(s["zk1"], s["zrk1"], 16, (), 3)
    myz0 = inside_yz(48, 32, 128, 192, 256)
    row48 = iota((48, 128), 0)
    for p in range(26):
        sx = inside_x(p, 5, 16)
        main = fk0[1, 0, p] * (myz0[:, 0:128] * sx)
        if not 0 < p < 25:
            main = jnp.where((row48 >= 8) & (row48 < 40), main, 0.0)
        fk0[1, 0, p] = main
        fk0[1, 1, p] = ghost0(1, p) * (myz0[:, 128:256] * sx)
    l0.prepare(1, 13)
    wait(recv, 20)
    wait(recv, 21)
    for p in range(1, 25):
        fk0[0, 1, p] = ghost0(0, p)
    l0.sources(1, 13)
    l0.half("b", l0.v["b"], 1, 13)
    l0.sweep(l0.v["b"], (2, 12), (2, 12))
    l0.residual(3, 11, (8, 40), pair0)
    f1_own = coarse1(pair0[:, 4:20, :].reshape(128, 128), 0.5)
    fk1[0, 7:15, 8:24, :] = f1_own

    slabs(fk1, fk1, 7, 8, 5, 16, (0,), 4)
    pack(lambda p: fk1[0, 7 + p, 8:24, :], s["zf1"], 8, 64)
    edges(s["zf1"], s["zrf1"], 16, (), 5)
    wait(recv, 16)
    for sy in (-1, 1):
        push(rk2.at[1, 1], rk2.at[1, 1 - sy], 22, (0, sy, 0))
    wait(recv, 2)
    wait(recv, 3)
    wait(send, 2)
    myz1 = inside_yz(32, 16, 64, 96, 128)
    for p in range(1, 21):
        v = jnp.where(lane32 < 64, fk1[1, p], ghost(s["zrk1"], (), p, 7, 8, 64))
        fk1[1, p] = v * (myz1 * inside_x(p, 7, 8))
    l1.prepare(1, 11)
    wait(recv, 22)
    for sz in (-1, 1):
        push(rk2.at[1], rk2.at[1 - sz], 23, (0, 0, sz))

    lane8 = iota((8, 128), 1)

    def unpack2(block, b, q, by):
        own = rotate(block(b, by, 1), -32 * q, 1)
        right = rotate(block(b, by, 2), 32 * (1 - q), 1)
        left = rotate(block(b, by, 0), 32 * (3 - q), 1)
        return jnp.where(lane8 < 32, own, jnp.where(lane8 < 64, right, jnp.where(lane8 >= 96, left, 0.0)))

    row24, lane24 = iota((24, 128), 0), iota((24, 128), 1)
    in_y = ((row24 >= 8) | (iy > 0)) & ((row24 < 16) | (iy < N - 1))
    in_z = (lane24 < 32) | ((lane24 < 64) & (iz < N - 1)) | ((lane24 >= 96) & (iz > 0))
    myz2 = jnp.where(in_y & in_z, 1.0, 0.0)
    wait(recv, 4)
    wait(recv, 5)
    wait(send, 4)
    for p in range(2, 20):
        fk1[0, p] = jnp.where(lane32 < 64, fk1[0, p], ghost(s["zrf1"], (), p, 7, 8, 64))
    l1.sources(1, 11)
    l1.half("b", l1.v["b"], 2, 10)
    l1.sweep(l1.v["b"], (3, 9), (3, 9))
    l1.residual(4, 8, (8, 24), pair1)
    rf2 = s["rf2"]
    rf2[2, 1, 1] = packed2(coarse2(0.5))

    far = [off for off in wide if off not in near]
    for sem, group in ((6, near), (19, far)):
        for off in group:
            push(rf2.at[2, 1, 1], rf2.at[2 - off[0], 1 - off[1], 1 - off[2]], sem, off)

    def source2(boxes):
        for b in boxes:
            for p in range(4 * b, 4 * b + 4):
                for by in range(3):
                    fk2[0, 1 + p, 8 * by : 8 * by + 8, :] = unpack2(lambda i, j, k: rf2[i, j, k], b, p % 4, by)
            l2.sources(1 + 2 * b, 3 + 2 * b)

    wait(recv, 23)
    for p in range(20):
        b, q = divmod(p, 4)
        sx = [flag(ix > 1), flag(ix > 0), 1.0, flag(ix < N - 1), flag(ix < N - 2)][b]
        for by in range(3):
            v = unpack2(lambda i, j, k: rk2[k, j, i], b, q, by)
            fk2[1, 1 + p, 8 * by : 8 * by + 8, :] = v * (myz2[8 * by : 8 * by + 8] * sx)
    l2.prepare(1, 11)

    wait(recv, 6)
    next(k_gather)
    source2((1, 2, 3))
    l2.half("b", l2.v["b"], 3, 9)
    l2.sweep(l2.v["b"], (4, 8), (4, 8))
    l2.residual(5, 7, (8, 16), pair2)
    f_gather = gather(coarse3(0.5), s["gf1"], s["gf2"], s["gf3"], 13)
    next(f_gather)
    ru2 = s["ru2"]
    total = jnp.where(lane8 < 32, l2.v["b"][5, 8:16, :], 0.0)
    ru2[1, 1, 2] = total + rotate(jnp.where(lane8 < 32, l2.v["b"][6, 8:16, :], 0.0), 32, 1)
    for sx in (-2, -1, 1, 2):
        push(ru2.at[1, 1, 2], ru2.at[1, 1, 2 - sx], 9, (sx, 0, 0))
    slabs(l1.v["b"], s["v1"], 4, 4, 3, 16, (), 7)
    pack(lambda p: l1.v["b"][4 + p, 8:24, :], s["zpu1"], 4, 64)
    edges(s["zpu1"], s["zru1"], 16, (), 8)
    s["v1"][4:8, 8:24, :] = l1.v["b"][4:8, 8:24, :]
    vb0n, v0n = s["vb0n"], s["v0n"]
    for j in range(3, 11):
        for t in range(6):
            vb0n[j, pl.ds(t, 8, 6), :] = l0.v["b"][j, 8 * t : 8 * t + 8, 0:128]
    pack(lambda p: vb0n[3 + p, 8:40, :], s["zpu0"], 8, 128)
    v0n[0, 3:11, 8:40, :] = vb0n[3:11, 8:40, :]
    next(f_gather)
    wait(recv, 9)
    for sy in (-1, 1):
        push(ru2.at[1, 1], ru2.at[1, 1 - sy], 24, (0, sy, 0))
    slabs(vb0n, v0n.at[0], 3, 8, 2, 32, (), 17)
    edges(s["zpu0"], s["zru0"], 32, (), 18)
    wait(recv, 19)
    source2((0, 4))
    next(k_gather)
    next(f_gather)
    wait(recv, 24)
    for sz in (-1, 1):
        push(ru2.at[1], ru2.at[1 - sz], 25, (0, 0, sz))
    for _ in k_gather:
        pass
    unpack3(s["gk3"], fk3.at[1])
    l3.prepare(1, 9)
    pair3_flat = pair3.reshape(8 * 32, 128)

    def coarse4(part):
        rows = row_pairs(pair3_flat, 128).reshape(8, 16, 128)
        out = None
        for h in range(2):
            into = jnp.where(lane_c == 64 * h + lane_r // 2, 0.125 * part, 0.0)
            piece = spread(rows[4 * h : 4 * h + 4].reshape(64, 128), into)
            out = piece if out is None else out + piece
        return out.reshape(4, 16, 128)

    for i in range(8):
        pair3[i] = fk3[1, 1 + 2 * i] + fk3[1, 2 + 2 * i]
    k4 = coarse4(1.0)
    shape4 = (4, 16, 128)
    row4, lane4 = iota(shape4, 1), iota(shape4, 2)
    z4 = lane4 & 63

    def cat(parts):
        return jnp.concatenate(parts, axis=0)

    def x_below(v):
        return cat([rotate(v[3], 64, 1)[None], v[0:3]])

    def x_above(v):
        return cat([v[1:4], rotate(v[0], 64, 1)[None]])

    def roll3(v, shift, axis):
        flat = [rotate(v[i], shift, axis)[None] for i in range(4)]
        return cat(flat)

    plane4 = iota(shape4, 0)
    first_x = (plane4 == 0) & (lane4 < 64)
    last_x = (plane4 == 3) & (lane4 >= 64)
    hs4 = 0.5 * 0.25**4
    kxl, kxu = jnp.where(first_x, 0.0, x_below(k4)), jnp.where(last_x, 0.0, x_above(k4))
    kyl = jnp.where(row4 == 0, 0.0, roll3(k4, 1, 0))
    kyu = jnp.where(row4 == 15, 0.0, roll3(k4, -1, 0))
    kzl = jnp.where(z4 == 0, 0.0, roll3(k4, 1, 1))
    kzu = jnp.where(z4 == 63, 0.0, roll3(k4, -1, 1))
    w4 = s["w4"]
    inv4 = 1.0 / (hs4 * (6.0 * k4 + kxl + kxu + kyl + kyu + kzl + kzu))
    odd4 = (plane4 + row4 + lane4) & 1
    w4[0] = jnp.where(first_x, 0.0, hs4 * (k4 + kxl))
    w4[1] = jnp.where(last_x, 0.0, hs4 * (k4 + kxu))
    w4[2] = jnp.where(row4 == 0, 0.0, hs4 * (k4 + kyl))
    w4[3] = jnp.where(row4 == 15, 0.0, hs4 * (k4 + kyu))
    w4[4] = jnp.where(z4 == 0, 0.0, hs4 * (k4 + kzl))
    w4[5] = jnp.where(z4 == 63, 0.0, hs4 * (k4 + kzu))
    w4[6] = jnp.where(odd4 == 0, inv4, 0.0)
    w4[7] = jnp.where(odd4 == 1, inv4, 0.0)

    wait(recv, 7)
    wait(recv, 8)
    v1 = s["v1"]
    for j in range(1, 11):
        v1[j] = jnp.where(lane32 < 64, v1[j], ghost(s["zru1"], (), j, 4, 4, 64))
    wait(recv, 17)
    wait(recv, 18)
    v0 = s["v0"]
    for j in range(1, 13):
        v0n[1, j] = ghost(s["zru0"], (), j, 3, 8, 0)
    for j in range(1, 13):
        v0[j] = l0.read(v0n, j)
    wait(recv, 25)
    v2 = s["v2"]
    for j in range(1, 11):
        b, q = divmod(j - 1, 2)
        for by in range(3):
            v2[j, 8 * by : 8 * by + 8, :] = unpack2(lambda i, j, k: ru2[k, j, i], b, q, by)
    for _ in f_gather:
        pass
    unpack3(s["gf3"], fk3.at[0])
    l3.sources(1, 9)
    l3.half("b", l3.v["b"], 1, 9)
    l3.sweep(l3.v["b"], (1, 9), (1, 9))
    l3.residual(1, 9, (0, 32), pair3)
    f4 = coarse4(0.5)
    w4[8] = f4

    def around4(v):
        total = w4[0] * x_below(v) + w4[1] * x_above(v)
        total = total + (w4[2] * roll3(v, 1, 0) + w4[3] * roll3(v, -1, 0))
        return total + (w4[4] * roll3(v, 1, 1) + w4[5] * roll3(v, -1, 1))

    def bottom(i, carry):
        black = carry[1]
        red = w4[6] * (w4[8] + around4(black))
        black = w4[7] * (w4[8] + around4(red))
        return (red, black)

    zero4 = jnp.zeros(shape4, F32)
    red4, black4 = lax.fori_loop(0, BOTTOM, bottom, (zero4, zero4))
    u4 = red4 + black4

    for h in range(2):
        into = jnp.where(lane_r == 64 * h + lane_c // 2, 1.0, 0.0)
        wide4 = spread(u4.reshape(64, 128), into)
        pair3_flat[pl.ds(128 * h, 64, 2), :] = wide4
        pair3_flat[pl.ds(128 * h + 1, 64, 2), :] = wide4
    v3 = l3.v["b"]
    for j in range(1, 9):
        l3.correct(v3, j, pair3[j - 1])
    for _ in range(2):
        l3.sweep(v3, (1, 9), (1, 9))
    for j in range(1, 9):
        u3[2 + 2 * j], u3[3 + 2 * j] = l3.planes(v3, j)

    zoff = jnp.where(lane_c < 64, lane_c, lane_c - 128)
    source_lane = 16 * iz + ((zoff + 128) // 2 - 64)
    spread_z = jnp.where((lane_r == source_lane) & ((lane_c < 64) | (lane_c >= 96)), 1.0, 0.0)
    spread_y = jnp.where(iota((24, 32), 1) == 4 * iy - 4 + iota((24, 32), 0) // 2, 1.0, 0.0)
    stretched = spread(u3[pl.ds(2 * ix, 10)].reshape(320, 128), spread_z)
    side_by_side = jnp.concatenate([stretched[32 * j : 32 * j + 32] for j in range(10)], axis=1)
    corr2 = select_rows(spread_y, side_by_side)
    for j in range(1, 11):
        l2.correct(v2, j, corr2[:, 128 * (j - 1) : 128 * j])
    l2.sweep(v2, (2, 10), (2, 10))
    l2.sweep(v2, (3, 9), (3, 9))

    spread1 = jnp.where(lane_r == jnp.where(lane_c >= 96, 64 + lane_c // 2, lane_c // 2), 1.0, 0.0)
    up1 = s["up1"]
    coarse = []
    for j in range(3, 9):
        coarse += list(l2.planes(v2, j))
    up1[...] = spread(jnp.concatenate(coarse[1:11], axis=0), spread1).reshape(10, 24, 128)
    tall1 = s["tall1"]
    for j in range(1, 11):
        part = up1[j - 1, 4:20, :]
        tall1[j - 1, pl.ds(0, 16, 2), :] = part
        tall1[j - 1, pl.ds(1, 16, 2), :] = part
        l1.correct(v1, j, tall1[j - 1])
    l1.sweep(v1, (1, 11), (2, 10))
    l1.sweep(v1, (2, 10), (3, 9))

    spread0 = jnp.where(iota((128, 256), 0) == iota((128, 256), 1) // 2, 1.0, 0.0)
    up0 = s["up0"]
    coarse = []
    for j in range(3, 9):
        coarse += list(l1.planes(v1, j))
    wide0 = spread(jnp.concatenate(coarse, axis=0), spread0).reshape(12, 32, 256)
    up0[0], up0[1] = wide0[:, :, 0:128], wide0[:, :, 128:256]
    for j in range(1, 13):
        tiles = []
        for t in range(2):
            rows = [up0[t, j - 1, pl.ds(4 + c, 8, 3), :] for c in range(3)]
            tiles.append(jnp.concatenate([rows[c // 2] for c in range(6)], axis=0))
        corr = jnp.concatenate(tiles, axis=1)
        v0[j] = jnp.where(l0.i["b"][j] > 0.0, v0[j] + corr, 0.0)
    l0.sweep(v0, (1, 13), (2, 12))
    l0.half("r", v0, 2, 12)
    outn = s["outn"]

    def last(j):
        black = l0.updated("b", l0.v["r"], j)
        red, even = l0.v["r"][j], l0.even()
        for n, plane in enumerate((jnp.where(even, red, black), jnp.where(even, black, red))):
            for t in range(6):
                outn[2 * j - 6 + n, pl.ds(t, 8, 6), :] = plane[8 * t : 8 * t + 8, 0:128]

    l0.loop(3, 11, last)
    out_ref[...] = outn[:, 8:40, :]
    for sem in sorted(sent):
        if sem not in (0, 2, 4):
            wait(send, sem)


def vmem(*shape):
    return pltpu.VMEM(shape, F32)


def scratch_shapes():
    shapes = {}
    sizes = [(26, 12, 48, 256), (22, 10, 32, 128), (22, 10, 24, 128), (18, 8, 32, 128)]
    for no, (planes, pairs, rows, lanes) in enumerate(sizes):
        shapes[f"fk{no}"] = vmem(2, 2, planes, rows, 128) if no == 0 else vmem(2, planes, rows, lanes)
        names = ["xin", "dr", "db"] + [n + c for n in ("v", "xo", "wy", "wz", "inv", "src") for c in "rb"]
        for name in names + (["v"] if no < 3 else []):
            shapes[f"{name}{no}"] = vmem(pairs + 2, rows, lanes)
    shapes["zp0"], shapes["zr0"] = vmem(2, 2, 32, 128), vmem(2, 3, 2, 48, 128)
    shapes["ze0"], shapes["zs0"] = vmem(2, 32, 128), vmem(2, 3, 48, 128)
    shapes["zpu0"], shapes["zru0"] = vmem(2, 32, 128), vmem(2, 3, 48, 128)
    for name in ("k1", "f1", "pu1"):
        shapes["z" + name] = vmem(2, 16, 128)
    for name in ("zrk1", "zrf1", "zru1"):
        shapes[name] = vmem(2, 3, 32, 128)
    shapes["rf2"] = vmem(5, 3, 3, 8, 128)
    for name in ("rk2", "ru2"):
        shapes[name] = vmem(3, 3, 5, 8, 128)
    for name in "kf":
        shapes[f"g{name}1"] = vmem(8, 8, 128)
        shapes[f"g{name}2"] = vmem(8, 8, 128)
        shapes[f"g{name}3"] = vmem(8, 2, 4, 8, 128)
    shapes["pair0"], shapes["pair1"] = vmem(8, 24, 128), vmem(4, 16, 128)
    shapes["pairk"], shapes["outn"] = vmem(8, 32, 128), vmem(16, 48, 128)
    shapes["vb0n"], shapes["v0n"] = vmem(14, 48, 128), vmem(2, 14, 48, 128)
    shapes["pair2"], shapes["pair3"] = vmem(2, 8, 128), vmem(8, 32, 128)
    shapes["w4"], shapes["u3"] = vmem(9, 4, 16, 128), vmem(24, 32, 128)
    shapes["up0"] = vmem(2, 12, 32, 128)
    shapes["up1"], shapes["tall1"] = vmem(10, 24, 128), vmem(10, 32, 128)
    shapes["dummy"] = vmem(256, 8, 128)
    shapes["send"] = pltpu.SemaphoreType.DMA((26,))
    shapes["recv"] = pltpu.SemaphoreType.DMA((26,))
    shapes["load"] = pltpu.SemaphoreType.DMA((2,))
    return shapes


SCRATCH = scratch_shapes()


def on_device(source_term, conductivity):
    return pl.pallas_call(
        kernel,
        out_shape=jax.ShapeDtypeStruct((16, 32, 128), F32),
        in_specs=[pl.BlockSpec(memory_space=pl.ANY)] * 2,
        out_specs=pl.BlockSpec(memory_space=pltpu.VMEM),
        scratch_shapes=list(SCRATCH.values()),
        compiler_params=pltpu.CompilerParams(
            collective_id=0, has_side_effects=True, vmem_limit_bytes=107 * 2**19
        ),
        name="vcycle",
    )(source_term, conductivity)


def solution(mesh):
    spec = P("gx", "gy", "gz")
    return jax.shard_map(
        on_device, mesh=mesh, in_specs=(spec, spec), out_specs=spec, check_vma=False
    )
```

```python
import functools

import jax
import jax.numpy as jnp
from jax import lax
from jax.experimental import pallas as pl
from jax.experimental.pallas import tpu as pltpu
from jax.sharding import PartitionSpec as P

MESH = pl.DeviceIdType.MESH
AXES = ("gx", "gy", "gz")
N = 8
BOTTOM = 16
F32 = jnp.float32


def iota(shape, axis):
    return lax.broadcasted_iota(jnp.int32, shape, axis)


def halves(a):
    high = a.astype(jnp.bfloat16)
    return high, (a - high.astype(F32)).astype(jnp.bfloat16)


def product(a, b):
    return lax.dot_general(a, b, (((1,), (0,)), ((), ())), preferred_element_type=F32)


def spread(a, b):
    high, low = halves(a)
    b = b.astype(jnp.bfloat16)
    return product(high, b) + product(low, b)


def select_rows(a, b):
    high, low = halves(b)
    a = a.astype(jnp.bfloat16)
    return product(a, high) + product(a, low)


def rotate(a, shift, axis):
    shift = shift % a.shape[axis]
    return a if shift == 0 else pltpu.roll(a, shift, axis)


class Level:
    def __init__(self, s, no, fk, scale, closed, block, steps=None):
        self.f, self.k = fk.at[0], fk.at[1]
        self.xin, self.dr, self.db = s[f"xin{no}"], s[f"dr{no}"], s[f"db{no}"]
        self.v = {"r": s[f"vr{no}"], "b": s[f"vb{no}"]}
        self.xo, self.y, self.z, self.i, self.g = (
            {c: s[f"{n}{c}{no}"] for c in "rb"} for n in ("xo", "wy", "wz", "inv", "src")
        )
        self.pairs, self.rows, self.lanes = self.xin.shape
        self.scale, self.closed, self.block, self.steps = (scale, closed, block, steps)

    def even(self):
        shape = (self.rows, self.lanes)
        row = iota(shape, 0) if self.steps is None else iota(shape, 0) // 8
        return (row + iota(shape, 1)) & 1 == 0

    def read(self, ref, p):
        if self.steps is None:
            return ref[p]
        tiles = []
        for t in range(0, self.lanes, 128):
            rows = [ref[t // 128, p, pl.ds(r, 8, self.steps), :] for r in range(self.steps)]
            tiles.append(jnp.concatenate(rows, axis=0))
        return jnp.concatenate(tiles, axis=1)

    def shift(self, a, way):
        if self.steps is None:
            return rotate(a, way, 0)
        if way == 1:
            return jnp.concatenate([rotate(a[self.rows - 8 :], 1, 0), a[: self.rows - 8]], axis=0)
        return jnp.concatenate([a[8:], rotate(a[:8], -1, 0)], axis=0)

    def loop(self, lo, hi, body):
        block = min(self.block, hi - lo)
        if block == hi - lo:
            for j in range(lo, hi):
                body(j)
            return

        def step(i, carry):
            for t in range(block):
                body(lo + i * block + t)
            return carry

        lax.fori_loop(0, (hi - lo) // block, step, 0)
        for j in range(lo + (hi - lo) // block * block, hi):
            body(j)

    def prepare(self, lo, hi):
        shape = (self.rows, self.lanes)
        hs = self.scale

        def times(a):
            return a if hs == 1.0 else hs * a

        def one(before, k, after):
            kyl, kyu = self.shift(k, 1), self.shift(k, -1)
            kzl, kzu = rotate(k, 1, 1), rotate(k, -1, 1)
            wy, wz = times(k + kyl), times(k + kzl)
            if self.closed:
                row, lane = iota(shape, 0), iota(shape, 1)
                kyl = jnp.where(row == 0, 0.0, kyl)
                kyu = jnp.where(row == self.rows - 1, 0.0, kyu)
                kzl = jnp.where(lane == 0, 0.0, kzl)
                kzu = jnp.where(lane == self.lanes - 1, 0.0, kzu)
                wy = jnp.where(row == 0, 0.0, wy)
                wz = jnp.where(lane == 0, 0.0, wz)
            diag = times(6.0 * k + before + after + kyl + kyu + kzl + kzu)
            inside = k > 0.0
            inv = jnp.where(inside, 1.0 / jnp.where(inside, diag, 1.0), 0.0)
            return wy, wz, inv, diag

        def body(j):
            even = self.even()
            k = [self.read(self.k, 2 * j - 2 + n) for n in range(4)]
            first, second = one(k[0], k[1], k[2]), one(k[1], k[2], k[3])
            below = times(k[0] + k[1])
            above = times(k[2] + k[3])
            self.xin[j] = times(k[1] + k[2])
            self.xo["r"][j] = jnp.where(even, below, above)
            self.xo["b"][j] = jnp.where(even, above, below)
            for ref, n in ((self.y, 0), (self.z, 1), (self.i, 2)):
                ref["r"][j] = jnp.where(even, first[n], second[n])
                ref["b"][j] = jnp.where(even, second[n], first[n])
            self.dr[j] = jnp.where(even, first[3], second[3])
            self.db[j] = jnp.where(even, second[3], first[3])

        self.loop(lo, hi, body)

    def sources(self, lo, hi):
        def body(j):
            even = self.even()
            a, b = self.read(self.f, 2 * j - 1), self.read(self.f, 2 * j)
            a, b = a + a, b + b
            red = jnp.where(even, a, b)
            self.g["r"][j] = red
            self.g["b"][j] = jnp.where(even, b, a)
            self.v["r"][j] = self.i["r"][j] * red

        self.loop(lo, hi, body)

    def around(self, colour, other, j):
        far = "b" if colour == "r" else "r"
        u, before, after = other[j], other[j - 1], other[j + 1]
        if colour == "b":
            before, after = after, before
        total = self.xin[j] * u + self.xo[colour][j] * jnp.where(self.even(), before, after)
        total = total + (self.y[colour][j] * self.shift(u, 1) + self.shift(self.y[far][j] * u, -1))
        return total + (self.z[colour][j] * rotate(u, 1, 1) + rotate(self.z[far][j] * u, -1, 1))

    def updated(self, colour, other, j):
        return self.i[colour][j] * (self.g[colour][j] + self.around(colour, other, j))

    def half(self, colour, black, lo, hi):
        target, other = (self.v["r"], black) if colour == "r" else (black, self.v["r"])

        def body(j):
            target[j] = self.updated(colour, other, j)

        self.loop(lo, hi, body)

    def sweep(self, black, red_range, black_range):
        self.half("r", black, *red_range)
        self.half("b", black, *black_range)

    def residual(self, lo, hi, rows, out):
        def body(j):
            r, b = self.v["r"], self.v["b"]
            red = self.g["r"][j] - (self.dr[j] * r[j] - self.around("r", b, j))
            black = self.g["b"][j] - (self.db[j] * b[j] - self.around("b", r, j))
            both = (red + black)[:, 0:128]
            if self.steps is None:
                out[j - lo] = both[rows[0] : rows[1]]
                return
            for t in range(0, self.steps, 2):
                two = both[8 * t : 8 * t + 8] + both[8 * t + 8 : 8 * t + 16]
                out[j - lo, pl.ds(t // 2, 8, self.steps // 2), :] = two

        self.loop(lo, hi, body)

    def correct(self, black, j, value):
        black[j] = jnp.where(self.i["b"][j] > 0.0, black[j] + value, 0.0)

    def planes(self, black, j):
        r, b, even = self.v["r"][j], black[j], self.even()
        return jnp.where(even, r, b), jnp.where(even, b, r)


def row_pairs(ref, count):
    return ref[pl.ds(0, count, 2), :] + ref[pl.ds(1, count, 2), :]


def kernel(f_hbm, k_hbm, out_ref, *scratch):
    names = list(SCRATCH)
    s = dict(zip(names, scratch))
    ix, iy, iz = (lax.axis_index(a) for a in AXES)
    me = (ix, iy, iz)

    def device(off):
        return tuple(lax.rem(me[a] + (off[a] + N), N) for a in range(3))

    send, recv, dummy = s["send"], s["recv"], s["dummy"]
    sent = {}

    def push(src, dst, sem, off):
        pltpu.make_async_remote_copy(
            src_ref=src, dst_ref=dst, send_sem=send.at[sem], recv_sem=recv.at[sem],
            device_id=device(off), device_id_type=MESH,
        ).start()
        size = 1
        for d in src.shape:
            size *= d
        sent[sem] = sent.get(sem, 0) + size // 1024

    def wait(sems, sem):
        view = dummy.at[pl.ds(0, sent[sem])]
        pltpu.make_async_copy(view, view, sems.at[sem]).wait()

    fk0, fk1, fk2, fk3 = s["fk0"], s["fk1"], s["fk2"], s["fk3"]

    l0, l1 = Level(s, 0, fk0, 1.0, False, 12, 6), Level(s, 1, fk1, 0.25, False, 12)
    l2, l3 = Level(s, 2, fk2, 0.25**2, False, 12), Level(s, 3, fk3, 0.25**3, True, 12)

    own0 = [fk0.at[a, 0, pl.ds(5, 16), pl.ds(8, 32)] for a in range(2)]
    loads = [pltpu.make_async_copy(r, own0[a], s["load"].at[a]) for a, r in enumerate((f_hbm, k_hbm))]
    loads[1].start()
    loads[0].start()
    near = [(a, b, c) for a in (-1, 0, 1) for b in (-1, 0, 1) for c in (-1, 0, 1) if (a, b, c) != (0, 0, 0)]
    wide = [(a, b, c) for a in (-2, -1, 0, 1, 2) for b in (-1, 0, 1) for c in (-1, 0, 1) if (a, b, c) != (0, 0, 0)]
    partners = near + [(d, 0, 0) for d in (-3, -2, 2, 3, 4)]
    barrier = pltpu.get_barrier_semaphore()
    for off in partners:
        pl.semaphore_signal(barrier, inc=1, device_id=device(off), device_id_type=MESH)
    loads[1].wait()
    pl.semaphore_wait(barrier, len(partners))

    def pack(own, zp, planes, length):
        left = right = None
        for p in range(planes):
            v = rotate(own(p), 8 * p, 1)
            group = iota(v.shape, 1) // 8
            left = v if p == 0 else jnp.where(group == p, v, left)
            right = v if p == 0 else jnp.where(group == (p + length // 8 - 1) % 16, v, right)
        zp[0], zp[1] = left, right

    def slabs(src, dst, start, nx, w, ny, lead, sem, corners=None):
        for sx in (-1, 0, 1):
            for sy in (-1, 0, 1):
                if (sx, sy) == (0, 0):
                    continue
                xs = {1: (start + nx - w, w, start - w), -1: (start, w, start + nx), 0: (start, nx, start)}[sx]
                ys = {1: (8 + ny - 8, 8, 0), -1: (8, 8, 8 + ny), 0: (8, ny, 8)}[sy]
                a = lead + (pl.ds(xs[0], xs[1]), pl.ds(ys[0], ys[1]), pl.ds(0, 128))
                b = lead + (pl.ds(xs[2], xs[1]), pl.ds(ys[2], ys[1]), pl.ds(0, 128))
                push(src.at[a], dst.at[b], sem, (sx, sy, 0))

    def edges(zp, zr, ny, lead, sem, columns=(-1, 0, 1)):
        for sz in (-1, 1):
            side = 1 if sz == 1 else 0
            for sx in columns:
                for sy in (-1, 0, 1):
                    ys = {1: (ny - 8, 8, 0), -1: (0, 8, 8 + ny), 0: (0, ny, 8)}[sy]
                    a = (side,) + lead + (pl.ds(ys[0], ys[1]),)
                    b = (1 - side, 1 - sx) + lead + (pl.ds(ys[2], ys[1]),)
                    push(zp.at[a], zr.at[b], sem, (sx, sy, sz))

    def place(right, left, at, base):
        lane = iota(right.shape, 1)
        both = rotate(jnp.where(lane // 8 == at, right, left), base - 8 * at, 1)
        return jnp.where((lane >= base) & (lane < base + 8) | (lane >= 120), both, 0.0)

    def slot(p, start, nx):
        return (0, p - start + nx) if p < start else (1, p - start) if p < start + nx else (2, p - start - nx)

    def ghost(zr, lead, p, start, nx, base):
        b, q = slot(p, start, nx)
        return place(zr[(1, b) + lead], zr[(0, b) + lead], q, base)

    def flag(condition):
        return jnp.where(condition, 1.0, 0.0)

    def inside_yz(rows, ny, own_lanes, right_end, lanes):
        row, lane = iota((rows, lanes), 0), iota((rows, lanes), 1)
        in_y = ((row >= 8) | (iy > 0)) & ((row < 8 + ny) | (iy < N - 1))
        in_z = (lane < own_lanes) | ((lane < right_end) & (iz < N - 1)) | ((lane >= right_end) & (iz > 0))
        return jnp.where(in_y & in_z, 1.0, 0.0)

    def inside_x(p, h, nx):
        return flag(ix > 0) if p < h else flag(ix < N - 1) if p >= h + nx else 1.0

    zp0, ze0, zr0, zs0 = s["zp0"], s["ze0"], s["zr0"], s["zs0"]
    slabs(fk0, fk0, 5, 16, 4, 32, (1, 0), 0)
    for sx, a, b in ((1, 16, 0), (-1, 9, 25)):
        push(fk0.at[1, 0, a, pl.ds(8, 32)], fk0.at[1, 0, b, pl.ds(8, 32)], 0, (sx, 0, 0))
    pack(lambda p: fk0[1, 0, 5 + p, 8:40, :], zp0.at[:, 1], 16, 128)
    edges(zp0, zr0, 32, (1,), 1, (0,))
    loads[0].wait()
    pack(lambda p: fk0[0, 0, 5 + p, 8:40, :], zp0.at[:, 0], 16, 128)
    lane32 = iota((32, 128), 1)
    for side in range(2):
        fs, ks = [rotate(zp0[side, a], 8 * side, 1) for a in range(2)]
        v = jnp.where(lane32 < 32, fs, rotate(fs, -64, 1))
        v = jnp.where(lane32 < 64, v, jnp.where(lane32 < 96, rotate(ks, 64, 1), ks))
        ze0[side] = rotate(v, -8 * side, 1)
    edges(ze0, zs0, 32, (), 1, (-1, 1))
    slabs(fk0, fk0, 5, 16, 4, 32, (0, 0), 20)
    edges(zp0, zr0, 32, (0,), 21, (0,))

    def ghost0(a, p):
        b, q = slot(p, 5, 16)
        if b == 1:
            return ghost(zr0, (a,), p, 5, 16, 0)
        if not 0 < p < 25:
            return jnp.zeros((48, 128), F32)
        return place(zs0[1, b], zs0[0, b], 8 * a + (q if b == 2 else 4 + q - 12), 0)

    lane_r, lane_c = iota((128, 128), 0), iota((128, 128), 1)
    halve1 = jnp.where((lane_r // 2 == lane_c), 0.125, 0.0)
    halve2 = jnp.where((lane_r // 2 == lane_c) & (lane_c < 32), 0.125, 0.0)

    pairk = s["pairk"]
    pair0, pair1, pair2, pair3 = s["pair0"], s["pair1"], s["pair2"], s["pair3"]

    def coarse1(rows, part):
        return spread(rows, part * halve1).reshape(8, 16, 128)

    def coarse2(part):
        flat = pair1.reshape(64, 128)
        return spread(row_pairs(flat, 32), part * halve2).reshape(4, 8, 128)

    def packed2(value):
        total = value[0]
        for q in range(1, 4):
            total = total + rotate(value[q], 32 * q, 1)
        return total

    row8, col8 = iota((8, 8), 0), iota((8, 8), 1)

    def coarse3(part):
        place_rows = jnp.where(row8 == 4 * (ix // 4) + col8 // 2, 1.0, 0.0)
        total = None
        for dx in range(2):
            group = lax.rem(2 * ix + dx, 8)
            into = jnp.where((lane_r < 32) & (lane_c == 16 * group + lane_r // 2), 0.125 * part, 0.0)
            piece = spread(select_rows(place_rows, pair2[dx]), into)
            total = piece if total is None else total + piece
        return total

    def gather(tile, g1, g2, g3, sem):
        g1[ix] = tile
        for d in range(1, N):
            push(g1.at[ix], g1.at[ix], sem, (d, 0, 0))
        yield
        wait(recv, sem)
        g2[iy] = (g1[0] + g1[1]) + (g1[2] + g1[3]) + ((g1[4] + g1[5]) + (g1[6] + g1[7]))
        for d in range(1, N):
            push(g2.at[iy], g2.at[iy], sem + 1, (0, d, 0))
        yield
        wait(recv, sem + 1)
        for o in range(4):
            a, b = g2[2 * o], g2[2 * o + 1]
            g3[iz, 0, o] = jnp.where(iota((8, 128), 0) < 4, a, rotate(b, 4, 0))
            g3[iz, 1, o] = jnp.where(iota((8, 128), 0) < 4, rotate(a, 4, 0), b)
        for d in range(1, N):
            push(g3.at[iz], g3.at[iz], sem + 2, (0, 0, d))
        yield
        wait(recv, sem + 2)

    def unpack3(g3, out):
        group = iota((32, 128), 1) // 16
        for h in range(2):
            blocks = [g3[j, h].reshape(32, 128) for j in range(8)]
            for bit in (4, 2, 1):
                low = group & bit == 0
                for j in range(8):
                    if j & bit:
                        continue
                    a, c = blocks[j], blocks[j + bit]
                    blocks[j] = jnp.where(low, a, rotate(c, 16 * bit, 1))
                    blocks[j + bit] = jnp.where(low, rotate(a, -16 * bit, 1), c)
            for g in range(8):
                out[1 + 8 * h + g] = blocks[g]

    for i in range(8):
        pairk[i] = fk0[1, 0, 5 + 2 * i, 8:40, :] + fk0[1, 0, 6 + 2 * i, 8:40, :]
    k1_own = coarse1(row_pairs(pairk.reshape(256, 128), 128), 1.0)
    fk1[1, 7:15, 8:24, :] = k1_own
    for i in range(4):
        pair1[i] = k1_own[2 * i] + k1_own[2 * i + 1]
    k2_own = coarse2(1.0)
    rk2 = s["rk2"]
    rk2[1, 1, 2] = packed2(k2_own)
    for i in range(2):
        pair2[i] = k2_own[2 * i] + k2_own[2 * i + 1]
    k_gather = gather(coarse3(1.0), s["gk1"], s["gk2"], s["gk3"], 10)
    pack(lambda p: fk1[1, 7 + p, 8:24, :], s["zk1"], 8, 64)

    for lev, last in ((l0, 13), (l1, 11), (l2, 11), (l3, 9)):
        for colour in "rb":
            for j in (0, last):
                lev.v[colour][j] = jnp.zeros((lev.rows, lev.lanes), F32)
    for j in (0, 13):
        s["v0"][j] = jnp.zeros((48, 256), F32)
    for j in (0, 11):
        s["v1"][j] = jnp.zeros((32, 128), F32)
        s["v2"][j] = jnp.zeros((24, 128), F32)
    for p in (0, 21):
        fk1[1, p] = jnp.zeros((32, 128), F32)
        fk2[1, p] = jnp.zeros((24, 128), F32)
    for j in (1, 2, 9, 10):
        l2.v["r"][j] = jnp.zeros((24, 128), F32)
    for p in (1, 20):
        fk1[0, p] = jnp.zeros((32, 128), F32)
    for p in (0, 17):
        fk3[1, p] = jnp.zeros((32, 128), F32)
    u3 = s["u3"]
    for p in (0, 1, 2, 3, 20, 21, 22, 23):
        u3[p] = jnp.zeros((32, 128), F32)

    wait(recv, 0)
    wait(recv, 1)
    wait(send, 0)
    next(k_gather)
    for sx in (-2, -1, 1, 2):
        push(rk2.at[1, 1, 2], rk2.at[1, 1, 2 - sx], 16, (sx, 0, 0))
    slabs(fk1, fk1, 7, 8, 6, 16, (1,), 2)
    edges(s["zk1"], s["zrk1"], 16, (), 3)
    myz0 = inside_yz(48, 32, 128, 192, 256)
    row48 = iota((48, 128), 0)
    for p in range(26):
        sx = inside_x(p, 5, 16)
        main = fk0[1, 0, p] * (myz0[:, 0:128] * sx)
        if not 0 < p < 25:
            main = jnp.where((row48 >= 8) & (row48 < 40), main, 0.0)
        fk0[1, 0, p] = main
        fk0[1, 1, p] = ghost0(1, p) * (myz0[:, 128:256] * sx)
    l0.prepare(1, 13)
    wait(recv, 20)
    wait(recv, 21)
    for p in range(1, 25):
        fk0[0, 1, p] = ghost0(0, p)
    l0.sources(1, 13)
    l0.half("b", l0.v["b"], 1, 13)
    l0.sweep(l0.v["b"], (2, 12), (2, 12))
    l0.residual(3, 11, (8, 40), pair0)
    f1_own = coarse1(pair0[:, 4:20, :].reshape(128, 128), 0.5)
    fk1[0, 7:15, 8:24, :] = f1_own

    slabs(fk1, fk1, 7, 8, 5, 16, (0,), 4)
    pack(lambda p: fk1[0, 7 + p, 8:24, :], s["zf1"], 8, 64)
    edges(s["zf1"], s["zrf1"], 16, (), 5)
    wait(recv, 16)
    for sy in (-1, 1):
        push(rk2.at[1, 1], rk2.at[1, 1 - sy], 22, (0, sy, 0))
    wait(recv, 2)
    wait(recv, 3)
    wait(send, 2)
    myz1 = inside_yz(32, 16, 64, 96, 128)
    for p in range(1, 21):
        v = jnp.where(lane32 < 64, fk1[1, p], ghost(s["zrk1"], (), p, 7, 8, 64))
        fk1[1, p] = v * (myz1 * inside_x(p, 7, 8))
    l1.prepare(1, 11)
    wait(recv, 22)
    for sz in (-1, 1):
        push(rk2.at[1], rk2.at[1 - sz], 23, (0, 0, sz))

    lane8 = iota((8, 128), 1)

    def unpack2(block, b, q, by):
        own = rotate(block(b, by, 1), -32 * q, 1)
        right = rotate(block(b, by, 2), 32 * (1 - q), 1)
        left = rotate(block(b, by, 0), 32 * (3 - q), 1)
        return jnp.where(lane8 < 32, own, jnp.where(lane8 < 64, right, jnp.where(lane8 >= 96, left, 0.0)))

    row24, lane24 = iota((24, 128), 0), iota((24, 128), 1)
    in_y = ((row24 >= 8) | (iy > 0)) & ((row24 < 16) | (iy < N - 1))
    in_z = (lane24 < 32) | ((lane24 < 64) & (iz < N - 1)) | ((lane24 >= 96) & (iz > 0))
    myz2 = jnp.where(in_y & in_z, 1.0, 0.0)
    wait(recv, 4)
    wait(recv, 5)
    wait(send, 4)
    for p in range(2, 20):
        fk1[0, p] = jnp.where(lane32 < 64, fk1[0, p], ghost(s["zrf1"], (), p, 7, 8, 64))
    l1.sources(1, 11)
    l1.half("b", l1.v["b"], 2, 10)
    l1.sweep(l1.v["b"], (3, 9), (3, 9))
    l1.residual(4, 8, (8, 24), pair1)
    rf2 = s["rf2"]
    rf2[2, 1, 1] = packed2(coarse2(0.5))

    far = [off for off in wide if off not in near]
    for sem, group in ((6, near), (19, far)):
        for off in group:
            push(rf2.at[2, 1, 1], rf2.at[2 - off[0], 1 - off[1], 1 - off[2]], sem, off)

    def source2(boxes):
        for b in boxes:
            for p in range(4 * b, 4 * b + 4):
                for by in range(3):
                    fk2[0, 1 + p, 8 * by : 8 * by + 8, :] = unpack2(lambda i, j, k: rf2[i, j, k], b, p % 4, by)
            l2.sources(1 + 2 * b, 3 + 2 * b)

    wait(recv, 23)
    for p in range(20):
        b, q = divmod(p, 4)
        sx = [flag(ix > 1), flag(ix > 0), 1.0, flag(ix < N - 1), flag(ix < N - 2)][b]
        for by in range(3):
            v = unpack2(lambda i, j, k: rk2[k, j, i], b, q, by)
            fk2[1, 1 + p, 8 * by : 8 * by + 8, :] = v * (myz2[8 * by : 8 * by + 8] * sx)
    l2.prepare(1, 11)

    wait(recv, 6)
    next(k_gather)
    source2((1, 2, 3))
    l2.half("b", l2.v["b"], 3, 9)
    l2.sweep(l2.v["b"], (4, 8), (4, 8))
    l2.residual(5, 7, (8, 16), pair2)
    f_gather = gather(coarse3(0.5), s["gf1"], s["gf2"], s["gf3"], 13)
    next(f_gather)
    ru2 = s["ru2"]
    total = jnp.where(lane8 < 32, l2.v["b"][5, 8:16, :], 0.0)
    ru2[1, 1, 2] = total + rotate(jnp.where(lane8 < 32, l2.v["b"][6, 8:16, :], 0.0), 32, 1)
    for sx in (-2, -1, 1, 2):
        push(ru2.at[1, 1, 2], ru2.at[1, 1, 2 - sx], 9, (sx, 0, 0))
    slabs(l1.v["b"], s["v1"], 4, 4, 3, 16, (), 7)
    pack(lambda p: l1.v["b"][4 + p, 8:24, :], s["zpu1"], 4, 64)
    edges(s["zpu1"], s["zru1"], 16, (), 8)
    s["v1"][4:8, 8:24, :] = l1.v["b"][4:8, 8:24, :]
    vb0n, v0n = s["vb0n"], s["v0n"]
    for j in range(3, 11):
        for t in range(6):
            vb0n[j, pl.ds(t, 8, 6), :] = l0.v["b"][j, 8 * t : 8 * t + 8, 0:128]
    pack(lambda p: vb0n[3 + p, 8:40, :], s["zpu0"], 8, 128)
    v0n[0, 3:11, 8:40, :] = vb0n[3:11, 8:40, :]
    next(f_gather)
    wait(recv, 9)
    for sy in (-1, 1):
        push(ru2.at[1, 1], ru2.at[1, 1 - sy], 24, (0, sy, 0))
    slabs(vb0n, v0n.at[0], 3, 8, 2, 32, (), 17)
    edges(s["zpu0"], s["zru0"], 32, (), 18)
    wait(recv, 19)
    source2((0, 4))
    next(k_gather)
    next(f_gather)
    wait(recv, 24)
    for sz in (-1, 1):
        push(ru2.at[1], ru2.at[1 - sz], 25, (0, 0, sz))
    for _ in k_gather:
        pass
    unpack3(s["gk3"], fk3.at[1])
    l3.prepare(1, 9)
    pair3_flat = pair3.reshape(8 * 32, 128)

    def coarse4(part):
        rows = row_pairs(pair3_flat, 128).reshape(8, 16, 128)
        out = None
        for h in range(2):
            into = jnp.where(lane_c == 64 * h + lane_r // 2, 0.125 * part, 0.0)
            piece = spread(rows[4 * h : 4 * h + 4].reshape(64, 128), into)
            out = piece if out is None else out + piece
        return out.reshape(4, 16, 128)

    for i in range(8):
        pair3[i] = fk3[1, 1 + 2 * i] + fk3[1, 2 + 2 * i]
    k4 = coarse4(1.0)
    shape4 = (4, 16, 128)
    row4, lane4 = iota(shape4, 1), iota(shape4, 2)
    z4 = lane4 & 63

    def cat(parts):
        return jnp.concatenate(parts, axis=0)

    def x_below(v):
        return cat([rotate(v[3], 64, 1)[None], v[0:3]])

    def x_above(v):
        return cat([v[1:4], rotate(v[0], 64, 1)[None]])

    def roll3(v, shift, axis):
        flat = [rotate(v[i], shift, axis)[None] for i in range(4)]
        return cat(flat)

    plane4 = iota(shape4, 0)
    first_x = (plane4 == 0) & (lane4 < 64)
    last_x = (plane4 == 3) & (lane4 >= 64)
    hs4 = 0.5 * 0.25**4
    kxl, kxu = jnp.where(first_x, 0.0, x_below(k4)), jnp.where(last_x, 0.0, x_above(k4))
    kyl = jnp.where(row4 == 0, 0.0, roll3(k4, 1, 0))
    kyu = jnp.where(row4 == 15, 0.0, roll3(k4, -1, 0))
    kzl = jnp.where(z4 == 0, 0.0, roll3(k4, 1, 1))
    kzu = jnp.where(z4 == 63, 0.0, roll3(k4, -1, 1))
    w4 = s["w4"]
    inv4 = 1.0 / (hs4 * (6.0 * k4 + kxl + kxu + kyl + kyu + kzl + kzu))
    odd4 = (plane4 + row4 + lane4) & 1
    w4[0] = jnp.where(first_x, 0.0, hs4 * (k4 + kxl))
    w4[1] = jnp.where(last_x, 0.0, hs4 * (k4 + kxu))
    w4[2] = jnp.where(row4 == 0, 0.0, hs4 * (k4 + kyl))
    w4[3] = jnp.where(row4 == 15, 0.0, hs4 * (k4 + kyu))
    w4[4] = jnp.where(z4 == 0, 0.0, hs4 * (k4 + kzl))
    w4[5] = jnp.where(z4 == 63, 0.0, hs4 * (k4 + kzu))
    w4[6] = jnp.where(odd4 == 0, inv4, 0.0)
    w4[7] = jnp.where(odd4 == 1, inv4, 0.0)

    wait(recv, 7)
    wait(recv, 8)
    v1 = s["v1"]
    for j in range(1, 11):
        v1[j] = jnp.where(lane32 < 64, v1[j], ghost(s["zru1"], (), j, 4, 4, 64))
    wait(recv, 17)
    wait(recv, 18)
    v0 = s["v0"]
    for j in range(1, 13):
        v0n[1, j] = ghost(s["zru0"], (), j, 3, 8, 0)
    for j in range(1, 13):
        v0[j] = l0.read(v0n, j)
    for _ in f_gather:
        pass
    unpack3(s["gf3"], fk3.at[0])
    l3.sources(1, 9)
    l3.half("b", l3.v["b"], 1, 9)
    l3.sweep(l3.v["b"], (1, 9), (1, 9))
    l3.residual(1, 9, (0, 32), pair3)
    f4 = coarse4(0.5)
    w4[8] = f4

    def around4(v):
        total = w4[0] * x_below(v) + w4[1] * x_above(v)
        total = total + (w4[2] * roll3(v, 1, 0) + w4[3] * roll3(v, -1, 0))
        return total + (w4[4] * roll3(v, 1, 1) + w4[5] * roll3(v, -1, 1))

    def bottom(i, carry):
        black = carry[1]
        red = w4[6] * (w4[8] + around4(black))
        black = w4[7] * (w4[8] + around4(red))
        return (red, black)

    zero4 = jnp.zeros(shape4, F32)
    red4, black4 = lax.fori_loop(0, BOTTOM, bottom, (zero4, zero4))
    u4 = red4 + black4

    for h in range(2):
        into = jnp.where(lane_r == 64 * h + lane_c // 2, 1.0, 0.0)
        wide4 = spread(u4.reshape(64, 128), into)
        pair3_flat[pl.ds(128 * h, 64, 2), :] = wide4
        pair3_flat[pl.ds(128 * h + 1, 64, 2), :] = wide4
    v3 = l3.v["b"]
    for j in range(1, 9):
        l3.correct(v3, j, pair3[j - 1])
    for _ in range(2):
        l3.sweep(v3, (1, 9), (1, 9))
    for j in range(1, 9):
        u3[2 + 2 * j], u3[3 + 2 * j] = l3.planes(v3, j)

    wait(recv, 25)
    v2 = s["v2"]
    for j in range(1, 11):
        b, q = divmod(j - 1, 2)
        for by in range(3):
            v2[j, 8 * by : 8 * by + 8, :] = unpack2(lambda i, j, k: ru2[k, j, i], b, q, by)
    zoff = jnp.where(lane_c < 64, lane_c, lane_c - 128)
    source_lane = 16 * iz + ((zoff + 128) // 2 - 64)
    spread_z = jnp.where((lane_r == source_lane) & ((lane_c < 64) | (lane_c >= 96)), 1.0, 0.0)
    spread_y = jnp.where(iota((24, 32), 1) == 4 * iy - 4 + iota((24, 32), 0) // 2, 1.0, 0.0)
    stretched = spread(u3[pl.ds(2 * ix, 10)].reshape(320, 128), spread_z)
    side_by_side = jnp.concatenate([stretched[32 * j : 32 * j + 32] for j in range(10)], axis=1)
    corr2 = select_rows(spread_y, side_by_side)
    for j in range(1, 11):
        l2.correct(v2, j, corr2[:, 128 * (j - 1) : 128 * j])
    l2.sweep(v2, (2, 10), (2, 10))
    l2.sweep(v2, (3, 9), (3, 9))

    spread1 = jnp.where(lane_r == jnp.where(lane_c >= 96, 64 + lane_c // 2, lane_c // 2), 1.0, 0.0)
    up1 = s["up1"]
    coarse = []
    for j in range(3, 9):
        coarse += list(l2.planes(v2, j))
    up1[...] = spread(jnp.concatenate(coarse[1:11], axis=0), spread1).reshape(10, 24, 128)
    tall1 = s["tall1"]
    for j in range(1, 11):
        part = up1[j - 1, 4:20, :]
        tall1[j - 1, pl.ds(0, 16, 2), :] = part
        tall1[j - 1, pl.ds(1, 16, 2), :] = part
        l1.correct(v1, j, tall1[j - 1])
    l1.sweep(v1, (1, 11), (2, 10))
    l1.sweep(v1, (2, 10), (3, 9))

    spread0 = jnp.where(iota((128, 256), 0) == iota((128, 256), 1) // 2, 1.0, 0.0)
    up0 = s["up0"]
    coarse = []
    for j in range(3, 9):
        coarse += list(l1.planes(v1, j))
    wide0 = spread(jnp.concatenate(coarse, axis=0), spread0).reshape(12, 32, 256)
    up0[0], up0[1] = wide0[:, :, 0:128], wide0[:, :, 128:256]
    for j in range(1, 13):
        tiles = []
        for t in range(2):
            rows = [up0[t, j - 1, pl.ds(4 + c, 8, 3), :] for c in range(3)]
            tiles.append(jnp.concatenate([rows[c // 2] for c in range(6)], axis=0))
        corr = jnp.concatenate(tiles, axis=1)
        v0[j] = jnp.where(l0.i["b"][j] > 0.0, v0[j] + corr, 0.0)
    l0.sweep(v0, (1, 13), (2, 12))
    l0.half("r", v0, 2, 12)
    outn = s["outn"]

    def last(j):
        black = l0.updated("b", l0.v["r"], j)
        red, even = l0.v["r"][j], l0.even()
        for n, plane in enumerate((jnp.where(even, red, black), jnp.where(even, black, red))):
            for t in range(6):
                outn[2 * j - 6 + n, pl.ds(t, 8, 6), :] = plane[8 * t : 8 * t + 8, 0:128]

    l0.loop(3, 11, last)
    out_ref[...] = outn[:, 8:40, :]
    for sem in sorted(sent):
        if sem not in (0, 2, 4):
            wait(send, sem)


def vmem(*shape):
    return pltpu.VMEM(shape, F32)


def scratch_shapes():
    shapes = {}
    sizes = [(26, 12, 48, 256), (22, 10, 32, 128), (22, 10, 24, 128), (18, 8, 32, 128)]
    for no, (planes, pairs, rows, lanes) in enumerate(sizes):
        shapes[f"fk{no}"] = vmem(2, 2, planes, rows, 128) if no == 0 else vmem(2, planes, rows, lanes)
        names = ["xin", "dr", "db"] + [n + c for n in ("v", "xo", "wy", "wz", "inv", "src") for c in "rb"]
        for name in names + (["v"] if no < 3 else []):
            shapes[f"{name}{no}"] = vmem(pairs + 2, rows, lanes)
    shapes["zp0"], shapes["zr0"] = vmem(2, 2, 32, 128), vmem(2, 3, 2, 48, 128)
    shapes["ze0"], shapes["zs0"] = vmem(2, 32, 128), vmem(2, 3, 48, 128)
    shapes["zpu0"], shapes["zru0"] = vmem(2, 32, 128), vmem(2, 3, 48, 128)
    for name in ("k1", "f1", "pu1"):
        shapes["z" + name] = vmem(2, 16, 128)
    for name in ("zrk1", "zrf1", "zru1"):
        shapes[name] = vmem(2, 3, 32, 128)
    shapes["rf2"] = vmem(5, 3, 3, 8, 128)
    for name in ("rk2", "ru2"):
        shapes[name] = vmem(3, 3, 5, 8, 128)
    for name in "kf":
        shapes[f"g{name}1"] = vmem(8, 8, 128)
        shapes[f"g{name}2"] = vmem(8, 8, 128)
        shapes[f"g{name}3"] = vmem(8, 2, 4, 8, 128)
    shapes["pair0"], shapes["pair1"] = vmem(8, 24, 128), vmem(4, 16, 128)
    shapes["pairk"], shapes["outn"] = vmem(8, 32, 128), vmem(16, 48, 128)
    shapes["vb0n"], shapes["v0n"] = vmem(14, 48, 128), vmem(2, 14, 48, 128)
    shapes["pair2"], shapes["pair3"] = vmem(2, 8, 128), vmem(8, 32, 128)
    shapes["w4"], shapes["u3"] = vmem(9, 4, 16, 128), vmem(24, 32, 128)
    shapes["up0"] = vmem(2, 12, 32, 128)
    shapes["up1"], shapes["tall1"] = vmem(10, 24, 128), vmem(10, 32, 128)
    shapes["dummy"] = vmem(256, 8, 128)
    shapes["send"] = pltpu.SemaphoreType.DMA((26,))
    shapes["recv"] = pltpu.SemaphoreType.DMA((26,))
    shapes["load"] = pltpu.SemaphoreType.DMA((2,))
    return shapes


SCRATCH = scratch_shapes()


def on_device(source_term, conductivity):
    return pl.pallas_call(
        kernel,
        out_shape=jax.ShapeDtypeStruct((16, 32, 128), F32),
        in_specs=[pl.BlockSpec(memory_space=pl.ANY)] * 2,
        out_specs=pl.BlockSpec(memory_space=pltpu.VMEM),
        scratch_shapes=list(SCRATCH.values()),
        compiler_params=pltpu.CompilerParams(
            collective_id=0, has_side_effects=True, vmem_limit_bytes=107 * 2**19
        ),
        name="vcycle",
    )(source_term, conductivity)


def solution(mesh):
    spec = P("gx", "gy", "gz")
    return jax.shard_map(
        on_device, mesh=mesh, in_specs=(spec, spec), out_specs=spec, check_vma=False
    )
```

```python
import functools

import jax
import jax.numpy as jnp
from jax import lax
from jax.experimental import pallas as pl
from jax.experimental.pallas import tpu as pltpu
from jax.sharding import PartitionSpec as P

MESH = pl.DeviceIdType.MESH
AXES = ("gx", "gy", "gz")
N = 8
BOTTOM = 16
F32 = jnp.float32


def iota(shape, axis):
    return lax.broadcasted_iota(jnp.int32, shape, axis)


def halves(a):
    high = a.astype(jnp.bfloat16)
    return high, (a - high.astype(F32)).astype(jnp.bfloat16)


def product(a, b):
    return lax.dot_general(a, b, (((1,), (0,)), ((), ())), preferred_element_type=F32)


def spread(a, b):
    high, low = halves(a)
    b = b.astype(jnp.bfloat16)
    return product(high, b) + product(low, b)


def select_rows(a, b):
    high, low = halves(b)
    a = a.astype(jnp.bfloat16)
    return product(a, high) + product(a, low)


def rotate(a, shift, axis):
    shift = shift % a.shape[axis]
    return a if shift == 0 else pltpu.roll(a, shift, axis)


class Level:
    def __init__(self, s, no, fk, scale, closed, block, steps=None):
        self.f, self.k = fk.at[0], fk.at[1]
        self.xin, self.dr, self.db = s[f"xin{no}"], s[f"dr{no}"], s[f"db{no}"]
        self.v = {"r": s[f"vr{no}"], "b": s[f"vb{no}"]}
        self.xo, self.y, self.z, self.i, self.g = (
            {c: s[f"{n}{c}{no}"] for c in "rb"} for n in ("xo", "wy", "wz", "inv", "src")
        )
        self.pairs, self.rows, self.lanes = self.xin.shape
        self.scale, self.closed, self.block, self.steps = (scale, closed, block, steps)

    def even(self):
        shape = (self.rows, self.lanes)
        row = iota(shape, 0) if self.steps is None else iota(shape, 0) // 8
        return (row + iota(shape, 1)) & 1 == 0

    def read(self, ref, p):
        if self.steps is None:
            return ref[p]
        tiles = []
        for t in range(0, self.lanes, 128):
            rows = [ref[t // 128, p, pl.ds(r, 8, self.steps), :] for r in range(self.steps)]
            tiles.append(jnp.concatenate(rows, axis=0))
        return jnp.concatenate(tiles, axis=1)

    def shift(self, a, way):
        if self.steps is None:
            return rotate(a, way, 0)
        if way == 1:
            return jnp.concatenate([rotate(a[self.rows - 8 :], 1, 0), a[: self.rows - 8]], axis=0)
        return jnp.concatenate([a[8:], rotate(a[:8], -1, 0)], axis=0)

    def loop(self, lo, hi, body):
        block = min(self.block, hi - lo)
        if block == hi - lo:
            for j in range(lo, hi):
                body(j)
            return

        def step(i, carry):
            for t in range(block):
                body(lo + i * block + t)
            return carry

        lax.fori_loop(0, (hi - lo) // block, step, 0)
        for j in range(lo + (hi - lo) // block * block, hi):
            body(j)

    def prepare(self, lo, hi):
        shape = (self.rows, self.lanes)
        hs = self.scale

        def times(a):
            return a if hs == 1.0 else hs * a

        def one(before, k, after):
            kyl, kyu = self.shift(k, 1), self.shift(k, -1)
            kzl, kzu = rotate(k, 1, 1), rotate(k, -1, 1)
            wy, wz = times(k + kyl), times(k + kzl)
            if self.closed:
                row, lane = iota(shape, 0), iota(shape, 1)
                kyl = jnp.where(row == 0, 0.0, kyl)
                kyu = jnp.where(row == self.rows - 1, 0.0, kyu)
                kzl = jnp.where(lane == 0, 0.0, kzl)
                kzu = jnp.where(lane == self.lanes - 1, 0.0, kzu)
                wy = jnp.where(row == 0, 0.0, wy)
                wz = jnp.where(lane == 0, 0.0, wz)
            diag = times(6.0 * k + before + after + kyl + kyu + kzl + kzu)
            inside = k > 0.0
            inv = jnp.where(inside, 1.0 / jnp.where(inside, diag, 1.0), 0.0)
            return wy, wz, inv, diag

        def body(j):
            even = self.even()
            k = [self.read(self.k, 2 * j - 2 + n) for n in range(4)]
            first, second = one(k[0], k[1], k[2]), one(k[1], k[2], k[3])
            below = times(k[0] + k[1])
            above = times(k[2] + k[3])
            self.xin[j] = times(k[1] + k[2])
            self.xo["r"][j] = jnp.where(even, below, above)
            self.xo["b"][j] = jnp.where(even, above, below)
            for ref, n in ((self.y, 0), (self.z, 1), (self.i, 2)):
                ref["r"][j] = jnp.where(even, first[n], second[n])
                ref["b"][j] = jnp.where(even, second[n], first[n])
            self.dr[j] = jnp.where(even, first[3], second[3])
            self.db[j] = jnp.where(even, second[3], first[3])

        self.loop(lo, hi, body)

    def sources(self, lo, hi):
        def body(j):
            even = self.even()
            a, b = self.read(self.f, 2 * j - 1), self.read(self.f, 2 * j)
            a, b = a + a, b + b
            red = jnp.where(even, a, b)
            self.g["r"][j] = red
            self.g["b"][j] = jnp.where(even, b, a)
            self.v["r"][j] = self.i["r"][j] * red

        self.loop(lo, hi, body)

    def around(self, colour, other, j):
        far = "b" if colour == "r" else "r"
        u, before, after = other[j], other[j - 1], other[j + 1]
        if colour == "b":
            before, after = after, before
        total = self.xin[j] * u + self.xo[colour][j] * jnp.where(self.even(), before, after)
        total = total + (self.y[colour][j] * self.shift(u, 1) + self.shift(self.y[far][j] * u, -1))
        return total + (self.z[colour][j] * rotate(u, 1, 1) + rotate(self.z[far][j] * u, -1, 1))

    def updated(self, colour, other, j):
        return self.i[colour][j] * (self.g[colour][j] + self.around(colour, other, j))

    def half(self, colour, black, lo, hi):
        target, other = (self.v["r"], black) if colour == "r" else (black, self.v["r"])

        def body(j):
            target[j] = self.updated(colour, other, j)

        self.loop(lo, hi, body)

    def sweep(self, black, red_range, black_range):
        self.half("r", black, *red_range)
        self.half("b", black, *black_range)

    def residual(self, lo, hi, rows, out):
        def body(j):
            r, b = self.v["r"], self.v["b"]
            red = self.g["r"][j] - (self.dr[j] * r[j] - self.around("r", b, j))
            black = self.g["b"][j] - (self.db[j] * b[j] - self.around("b", r, j))
            both = (red + black)[:, 0:128]
            if self.steps is None:
                out[j - lo] = both[rows[0] : rows[1]]
                return
            for t in range(0, self.steps, 2):
                two = both[8 * t : 8 * t + 8] + both[8 * t + 8 : 8 * t + 16]
                out[j - lo, pl.ds(t // 2, 8, self.steps // 2), :] = two

        self.loop(lo, hi, body)

    def correct(self, black, j, value):
        black[j] = jnp.where(self.i["b"][j] > 0.0, black[j] + value, 0.0)

    def planes(self, black, j):
        r, b, even = self.v["r"][j], black[j], self.even()
        return jnp.where(even, r, b), jnp.where(even, b, r)


def row_pairs(ref, count):
    return ref[pl.ds(0, count, 2), :] + ref[pl.ds(1, count, 2), :]


def kernel(f_hbm, k_hbm, out_ref, *scratch):
    names = list(SCRATCH)
    s = dict(zip(names, scratch))
    ix, iy, iz = (lax.axis_index(a) for a in AXES)
    me = (ix, iy, iz)

    def device(off):
        return tuple(lax.rem(me[a] + (off[a] + N), N) for a in range(3))

    send, recv, dummy = s["send"], s["recv"], s["dummy"]
    sent = {}

    def push(src, dst, sem, off):
        pltpu.make_async_remote_copy(
            src_ref=src, dst_ref=dst, send_sem=send.at[sem], recv_sem=recv.at[sem],
            device_id=device(off), device_id_type=MESH,
        ).start()
        size = 1
        for d in src.shape:
            size *= d
        sent[sem] = sent.get(sem, 0) + size // 1024

    def wait(sems, sem):
        view = dummy.at[pl.ds(0, sent[sem])]
        pltpu.make_async_copy(view, view, sems.at[sem]).wait()

    fk0, fk1, fk2, fk3 = s["fk0"], s["fk1"], s["fk2"], s["fk3"]

    l0, l1 = Level(s, 0, fk0, 1.0, False, 12, 6), Level(s, 1, fk1, 0.25, False, 12)
    l2, l3 = Level(s, 2, fk2, 0.25**2, False, 12), Level(s, 3, fk3, 0.25**3, True, 12)

    own0 = [fk0.at[a, 0, pl.ds(5, 16), pl.ds(8, 32)] for a in range(2)]
    loads = [pltpu.make_async_copy(r, own0[a], s["load"].at[a]) for a, r in enumerate((f_hbm, k_hbm))]
    loads[1].start()
    loads[0].start()
    near = [(a, b, c) for a in (-1, 0, 1) for b in (-1, 0, 1) for c in (-1, 0, 1) if (a, b, c) != (0, 0, 0)]
    wide = [(a, b, c) for a in (-2, -1, 0, 1, 2) for b in (-1, 0, 1) for c in (-1, 0, 1) if (a, b, c) != (0, 0, 0)]
    partners = near + [(d, 0, 0) for d in (-3, -2, 2, 3, 4)]
    barrier = pltpu.get_barrier_semaphore()
    for off in partners:
        pl.semaphore_signal(barrier, inc=1, device_id=device(off), device_id_type=MESH)
    loads[1].wait()
    pl.semaphore_wait(barrier, len(partners))

    def pack(own, zp, planes, length):
        left = right = None
        for p in range(planes):
            v = rotate(own(p), 8 * p, 1)
            group = iota(v.shape, 1) // 8
            left = v if p == 0 else jnp.where(group == p, v, left)
            right = v if p == 0 else jnp.where(group == (p + length // 8 - 1) % 16, v, right)
        zp[0], zp[1] = left, right

    def slabs(src, dst, start, nx, w, ny, lead, sem, corners=None):
        for sx in (-1, 0, 1):
            for sy in (-1, 0, 1):
                if (sx, sy) == (0, 0):
                    continue
                xs = {1: (start + nx - w, w, start - w), -1: (start, w, start + nx), 0: (start, nx, start)}[sx]
                ys = {1: (8 + ny - 8, 8, 0), -1: (8, 8, 8 + ny), 0: (8, ny, 8)}[sy]
                a = lead + (pl.ds(xs[0], xs[1]), pl.ds(ys[0], ys[1]), pl.ds(0, 128))
                b = lead + (pl.ds(xs[2], xs[1]), pl.ds(ys[2], ys[1]), pl.ds(0, 128))
                push(src.at[a], dst.at[b], sem, (sx, sy, 0))

    def edges(zp, zr, ny, lead, sem, columns=(-1, 0, 1)):
        for sz in (-1, 1):
            side = 1 if sz == 1 else 0
            for sx in columns:
                for sy in (-1, 0, 1):
                    ys = {1: (ny - 8, 8, 0), -1: (0, 8, 8 + ny), 0: (0, ny, 8)}[sy]
                    a = (side,) + lead + (pl.ds(ys[0], ys[1]),)
                    b = (1 - side, 1 - sx) + lead + (pl.ds(ys[2], ys[1]),)
                    push(zp.at[a], zr.at[b], sem, (sx, sy, sz))

    def place(right, left, at, base):
        lane = iota(right.shape, 1)
        both = rotate(jnp.where(lane // 8 == at, right, left), base - 8 * at, 1)
        return jnp.where((lane >= base) & (lane < base + 8) | (lane >= 120), both, 0.0)

    def slot(p, start, nx):
        return (0, p - start + nx) if p < start else (1, p - start) if p < start + nx else (2, p - start - nx)

    def ghost(zr, lead, p, start, nx, base):
        b, q = slot(p, start, nx)
        return place(zr[(1, b) + lead], zr[(0, b) + lead], q, base)

    def flag(condition):
        return jnp.where(condition, 1.0, 0.0)

    def inside_yz(rows, ny, own_lanes, right_end, lanes):
        row, lane = iota((rows, lanes), 0), iota((rows, lanes), 1)
        in_y = ((row >= 8) | (iy > 0)) & ((row < 8 + ny) | (iy < N - 1))
        in_z = (lane < own_lanes) | ((lane < right_end) & (iz < N - 1)) | ((lane >= right_end) & (iz > 0))
        return jnp.where(in_y & in_z, 1.0, 0.0)

    def inside_x(p, h, nx):
        return flag(ix > 0) if p < h else flag(ix < N - 1) if p >= h + nx else 1.0

    zp0, ze0, zr0, zs0 = s["zp0"], s["ze0"], s["zr0"], s["zs0"]
    slabs(fk0, fk0, 5, 16, 4, 32, (1, 0), 0)
    for sx, a, b in ((1, 16, 0), (-1, 9, 25)):
        push(fk0.at[1, 0, a, pl.ds(8, 32)], fk0.at[1, 0, b, pl.ds(8, 32)], 0, (sx, 0, 0))
    pack(lambda p: fk0[1, 0, 5 + p, 8:40, :], zp0.at[:, 1], 16, 128)
    edges(zp0, zr0, 32, (1,), 1, (0,))
    loads[0].wait()
    pack(lambda p: fk0[0, 0, 5 + p, 8:40, :], zp0.at[:, 0], 16, 128)
    lane32 = iota((32, 128), 1)
    for side in range(2):
        fs, ks = [rotate(zp0[side, a], 8 * side, 1) for a in range(2)]
        v = jnp.where(lane32 < 32, fs, rotate(fs, -64, 1))
        v = jnp.where(lane32 < 64, v, jnp.where(lane32 < 96, rotate(ks, 64, 1), ks))
        ze0[side] = rotate(v, -8 * side, 1)
    edges(ze0, zs0, 32, (), 1, (-1, 1))
    slabs(fk0, fk0, 5, 16, 4, 32, (0, 0), 20)
    edges(zp0, zr0, 32, (0,), 21, (0,))

    def ghost0(a, p):
        b, q = slot(p, 5, 16)
        if b == 1:
            return ghost(zr0, (a,), p, 5, 16, 0)
        if not 0 < p < 25:
            return jnp.zeros((48, 128), F32)
        return place(zs0[1, b], zs0[0, b], 8 * a + (q if b == 2 else 4 + q - 12), 0)

    lane_r, lane_c = iota((128, 128), 0), iota((128, 128), 1)
    halve1 = jnp.where((lane_r // 2 == lane_c), 0.125, 0.0)
    halve2 = jnp.where((lane_r // 2 == lane_c) & (lane_c < 32), 0.125, 0.0)

    pairk = s["pairk"]
    pair0, pair1, pair2, pair3 = s["pair0"], s["pair1"], s["pair2"], s["pair3"]

    def coarse1(rows, part):
        return spread(rows, part * halve1).reshape(8, 16, 128)

    def coarse2(part):
        flat = pair1.reshape(64, 128)
        return spread(row_pairs(flat, 32), part * halve2).reshape(4, 8, 128)

    def packed2(value):
        total = value[0]
        for q in range(1, 4):
            total = total + rotate(value[q], 32 * q, 1)
        return total

    row8, col8 = iota((8, 8), 0), iota((8, 8), 1)

    def coarse3(part):
        place_rows = jnp.where(row8 == 4 * (ix // 4) + col8 // 2, 1.0, 0.0)
        total = None
        for dx in range(2):
            group = lax.rem(2 * ix + dx, 8)
            into = jnp.where((lane_r < 32) & (lane_c == 16 * group + lane_r // 2), 0.125 * part, 0.0)
            piece = spread(select_rows(place_rows, pair2[dx]), into)
            total = piece if total is None else total + piece
        return total

    def gather(tile, g1, g2, g3, sem):
        g1[ix] = tile
        for d in range(1, N):
            push(g1.at[ix], g1.at[ix], sem, (d, 0, 0))
        yield
        wait(recv, sem)
        g2[iy] = (g1[0] + g1[1]) + (g1[2] + g1[3]) + ((g1[4] + g1[5]) + (g1[6] + g1[7]))
        for d in range(1, N):
            push(g2.at[iy], g2.at[iy], sem + 1, (0, d, 0))
        yield
        wait(recv, sem + 1)
        for o in range(4):
            a, b = g2[2 * o], g2[2 * o + 1]
            g3[iz, 0, o] = jnp.where(iota((8, 128), 0) < 4, a, rotate(b, 4, 0))
            g3[iz, 1, o] = jnp.where(iota((8, 128), 0) < 4, rotate(a, 4, 0), b)
        for d in range(1, N):
            push(g3.at[iz], g3.at[iz], sem + 2, (0, 0, d))
        yield
        wait(recv, sem + 2)

    def unpack3(g3, out):
        group = iota((32, 128), 1) // 16
        for h in range(2):
            blocks = [g3[j, h].reshape(32, 128) for j in range(8)]
            for bit in (4, 2, 1):
                low = group & bit == 0
                for j in range(8):
                    if j & bit:
                        continue
                    a, c = blocks[j], blocks[j + bit]
                    blocks[j] = jnp.where(low, a, rotate(c, 16 * bit, 1))
                    blocks[j + bit] = jnp.where(low, rotate(a, -16 * bit, 1), c)
            for g in range(8):
                out[1 + 8 * h + g] = blocks[g]

    for i in range(8):
        pairk[i] = fk0[1, 0, 5 + 2 * i, 8:40, :] + fk0[1, 0, 6 + 2 * i, 8:40, :]
    k1_own = coarse1(row_pairs(pairk.reshape(256, 128), 128), 1.0)
    fk1[1, 7:15, 8:24, :] = k1_own
    for i in range(4):
        pair1[i] = k1_own[2 * i] + k1_own[2 * i + 1]
    k2_own = coarse2(1.0)
    rk2 = s["rk2"]
    rk2[1, 1, 2] = packed2(k2_own)
    for i in range(2):
        pair2[i] = k2_own[2 * i] + k2_own[2 * i + 1]
    k_gather = gather(coarse3(1.0), s["gk1"], s["gk2"], s["gk3"], 10)
    pack(lambda p: fk1[1, 7 + p, 8:24, :], s["zk1"], 8, 64)

    for lev, last in ((l0, 13), (l1, 11), (l2, 11), (l3, 9)):
        for colour in "rb":
            for j in (0, last):
                lev.v[colour][j] = jnp.zeros((lev.rows, lev.lanes), F32)
    for j in (0, 13):
        s["v0"][j] = jnp.zeros((48, 256), F32)
    for j in (0, 11):
        s["v1"][j] = jnp.zeros((32, 128), F32)
        s["v2"][j] = jnp.zeros((24, 128), F32)
    for p in (0, 21):
        fk1[1, p] = jnp.zeros((32, 128), F32)
        fk2[1, p] = jnp.zeros((24, 128), F32)
    for j in (1, 2, 9, 10):
        l2.v["r"][j] = jnp.zeros((24, 128), F32)
    for p in (1, 20):
        fk1[0, p] = jnp.zeros((32, 128), F32)
    for p in (0, 17):
        fk3[1, p] = jnp.zeros((32, 128), F32)
    u3 = s["u3"]
    for p in (0, 1, 2, 3, 20, 21, 22, 23):
        u3[p] = jnp.zeros((32, 128), F32)

    wait(recv, 0)
    wait(recv, 1)
    wait(send, 0)
    next(k_gather)
    for sx in (-2, -1, 1, 2):
        push(rk2.at[1, 1, 2], rk2.at[1, 1, 2 - sx], 16, (sx, 0, 0))
    slabs(fk1, fk1, 7, 8, 6, 16, (1,), 2)
    edges(s["zk1"], s["zrk1"], 16, (), 3)
    myz0 = inside_yz(48, 32, 128, 192, 256)
    row48 = iota((48, 128), 0)
    for p in range(26):
        sx = inside_x(p, 5, 16)
        main = fk0[1, 0, p] * (myz0[:, 0:128] * sx)
        if not 0 < p < 25:
            main = jnp.where((row48 >= 8) & (row48 < 40), main, 0.0)
        fk0[1, 0, p] = main
        fk0[1, 1, p] = ghost0(1, p) * (myz0[:, 128:256] * sx)
    l0.prepare(1, 13)
    wait(recv, 20)
    wait(recv, 21)
    for p in range(1, 25):
        fk0[0, 1, p] = ghost0(0, p)
    l0.sources(1, 13)
    l0.half("b", l0.v["b"], 1, 13)
    l0.sweep(l0.v["b"], (2, 12), (2, 12))
    l0.residual(3, 11, (8, 40), pair0)
    f1_own = coarse1(pair0[:, 4:20, :].reshape(128, 128), 0.5)
    fk1[0, 7:15, 8:24, :] = f1_own

    slabs(fk1, fk1, 7, 8, 5, 16, (0,), 4)
    pack(lambda p: fk1[0, 7 + p, 8:24, :], s["zf1"], 8, 64)
    edges(s["zf1"], s["zrf1"], 16, (), 5)
    wait(recv, 16)
    for sy in (-1, 1):
        push(rk2.at[1, 1], rk2.at[1, 1 - sy], 22, (0, sy, 0))
    wait(recv, 2)
    wait(recv, 3)
    wait(send, 2)
    myz1 = inside_yz(32, 16, 64, 96, 128)
    for p in range(1, 21):
        v = jnp.where(lane32 < 64, fk1[1, p], ghost(s["zrk1"], (), p, 7, 8, 64))
        fk1[1, p] = v * (myz1 * inside_x(p, 7, 8))
    l1.prepare(1, 11)
    wait(recv, 22)
    for sz in (-1, 1):
        push(rk2.at[1], rk2.at[1 - sz], 23, (0, 0, sz))

    lane8 = iota((8, 128), 1)

    def unpack2(block, b, q, by):
        own = rotate(block(b, by, 1), -32 * q, 1)
        right = rotate(block(b, by, 2), 32 * (1 - q), 1)
        left = rotate(block(b, by, 0), 32 * (3 - q), 1)
        return jnp.where(lane8 < 32, own, jnp.where(lane8 < 64, right, jnp.where(lane8 >= 96, left, 0.0)))

    row24, lane24 = iota((24, 128), 0), iota((24, 128), 1)
    in_y = ((row24 >= 8) | (iy > 0)) & ((row24 < 16) | (iy < N - 1))
    in_z = (lane24 < 32) | ((lane24 < 64) & (iz < N - 1)) | ((lane24 >= 96) & (iz > 0))
    myz2 = jnp.where(in_y & in_z, 1.0, 0.0)
    wait(recv, 4)
    wait(recv, 5)
    wait(send, 4)
    for p in range(2, 20):
        fk1[0, p] = jnp.where(lane32 < 64, fk1[0, p], ghost(s["zrf1"], (), p, 7, 8, 64))
    l1.sources(1, 11)
    l1.half("b", l1.v["b"], 2, 10)
    l1.sweep(l1.v["b"], (3, 9), (3, 9))
    l1.residual(4, 8, (8, 24), pair1)
    rf2 = s["rf2"]
    rf2[2, 1, 1] = packed2(coarse2(0.5))

    far = [off for off in wide if off not in near]
    for sem, group in ((6, near), (19, far)):
        for off in group:
            push(rf2.at[2, 1, 1], rf2.at[2 - off[0], 1 - off[1], 1 - off[2]], sem, off)

    def source2(boxes):
        for b in boxes:
            for p in range(4 * b, 4 * b + 4):
                for by in range(3):
                    fk2[0, 1 + p, 8 * by : 8 * by + 8, :] = unpack2(lambda i, j, k: rf2[i, j, k], b, p % 4, by)
            l2.sources(1 + 2 * b, 3 + 2 * b)

    wait(recv, 23)
    for p in range(20):
        b, q = divmod(p, 4)
        sx = [flag(ix > 1), flag(ix > 0), 1.0, flag(ix < N - 1), flag(ix < N - 2)][b]
        for by in range(3):
            v = unpack2(lambda i, j, k: rk2[k, j, i], b, q, by)
            fk2[1, 1 + p, 8 * by : 8 * by + 8, :] = v * (myz2[8 * by : 8 * by + 8] * sx)
    l2.prepare(1, 11)

    wait(recv, 6)
    next(k_gather)
    source2((1, 2, 3))
    l2.half("b", l2.v["b"], 3, 9)
    l2.sweep(l2.v["b"], (4, 8), (4, 8))
    l2.residual(5, 7, (8, 16), pair2)
    f_gather = gather(coarse3(0.5), s["gf1"], s["gf2"], s["gf3"], 13)
    next(f_gather)
    ru2 = s["ru2"]
    total = jnp.where(lane8 < 32, l2.v["b"][5, 8:16, :], 0.0)
    ru2[1, 1, 2] = total + rotate(jnp.where(lane8 < 32, l2.v["b"][6, 8:16, :], 0.0), 32, 1)
    for sx in (-2, -1, 1, 2):
        push(ru2.at[1, 1, 2], ru2.at[1, 1, 2 - sx], 9, (sx, 0, 0))
    slabs(l1.v["b"], s["v1"], 4, 4, 3, 16, (), 7)
    pack(lambda p: l1.v["b"][4 + p, 8:24, :], s["zpu1"], 4, 64)
    edges(s["zpu1"], s["zru1"], 16, (), 8)
    s["v1"][4:8, 8:24, :] = l1.v["b"][4:8, 8:24, :]
    vb0n, v0n = s["vb0n"], s["v0n"]
    for j in range(3, 11):
        for t in range(6):
            vb0n[j, pl.ds(t, 8, 6), :] = l0.v["b"][j, 8 * t : 8 * t + 8, 0:128]
    pack(lambda p: vb0n[3 + p, 8:40, :], s["zpu0"], 8, 128)
    v0n[0, 3:11, 8:40, :] = vb0n[3:11, 8:40, :]
    next(f_gather)
    next(k_gather)
    wait(recv, 9)
    for sy in (-1, 1):
        push(ru2.at[1, 1], ru2.at[1, 1 - sy], 24, (0, sy, 0))
    slabs(vb0n, v0n.at[0], 3, 8, 2, 32, (), 17)
    edges(s["zpu0"], s["zru0"], 32, (), 18)
    wait(recv, 19)
    source2((0, 4))
    next(f_gather)
    wait(recv, 24)
    for sz in (-1, 1):
        push(ru2.at[1], ru2.at[1 - sz], 25, (0, 0, sz))
    for _ in k_gather:
        pass
    unpack3(s["gk3"], fk3.at[1])
    l3.prepare(1, 9)
    pair3_flat = pair3.reshape(8 * 32, 128)

    def coarse4(part):
        rows = row_pairs(pair3_flat, 128).reshape(8, 16, 128)
        out = None
        for h in range(2):
            into = jnp.where(lane_c == 64 * h + lane_r // 2, 0.125 * part, 0.0)
            piece = spread(rows[4 * h : 4 * h + 4].reshape(64, 128), into)
            out = piece if out is None else out + piece
        return out.reshape(4, 16, 128)

    for i in range(8):
        pair3[i] = fk3[1, 1 + 2 * i] + fk3[1, 2 + 2 * i]
    k4 = coarse4(1.0)
    shape4 = (4, 16, 128)
    row4, lane4 = iota(shape4, 1), iota(shape4, 2)
    z4 = lane4 & 63

    def cat(parts):
        return jnp.concatenate(parts, axis=0)

    def x_below(v):
        return cat([rotate(v[3], 64, 1)[None], v[0:3]])

    def x_above(v):
        return cat([v[1:4], rotate(v[0], 64, 1)[None]])

    def roll3(v, shift, axis):
        flat = [rotate(v[i], shift, axis)[None] for i in range(4)]
        return cat(flat)

    plane4 = iota(shape4, 0)
    first_x = (plane4 == 0) & (lane4 < 64)
    last_x = (plane4 == 3) & (lane4 >= 64)
    hs4 = 0.5 * 0.25**4
    kxl, kxu = jnp.where(first_x, 0.0, x_below(k4)), jnp.where(last_x, 0.0, x_above(k4))
    kyl = jnp.where(row4 == 0, 0.0, roll3(k4, 1, 0))
    kyu = jnp.where(row4 == 15, 0.0, roll3(k4, -1, 0))
    kzl = jnp.where(z4 == 0, 0.0, roll3(k4, 1, 1))
    kzu = jnp.where(z4 == 63, 0.0, roll3(k4, -1, 1))
    w4 = s["w4"]
    inv4 = 1.0 / (hs4 * (6.0 * k4 + kxl + kxu + kyl + kyu + kzl + kzu))
    odd4 = (plane4 + row4 + lane4) & 1
    w4[0] = jnp.where(first_x, 0.0, hs4 * (k4 + kxl))
    w4[1] = jnp.where(last_x, 0.0, hs4 * (k4 + kxu))
    w4[2] = jnp.where(row4 == 0, 0.0, hs4 * (k4 + kyl))
    w4[3] = jnp.where(row4 == 15, 0.0, hs4 * (k4 + kyu))
    w4[4] = jnp.where(z4 == 0, 0.0, hs4 * (k4 + kzl))
    w4[5] = jnp.where(z4 == 63, 0.0, hs4 * (k4 + kzu))
    w4[6] = jnp.where(odd4 == 0, inv4, 0.0)
    w4[7] = jnp.where(odd4 == 1, inv4, 0.0)

    wait(recv, 7)
    wait(recv, 8)
    v1 = s["v1"]
    for j in range(1, 11):
        v1[j] = jnp.where(lane32 < 64, v1[j], ghost(s["zru1"], (), j, 4, 4, 64))
    wait(recv, 17)
    wait(recv, 18)
    v0 = s["v0"]
    for j in range(1, 13):
        v0n[1, j] = ghost(s["zru0"], (), j, 3, 8, 0)
    for j in range(1, 13):
        v0[j] = l0.read(v0n, j)
    wait(recv, 25)
    v2 = s["v2"]
    for j in range(1, 11):
        b, q = divmod(j - 1, 2)
        for by in range(3):
            v2[j, 8 * by : 8 * by + 8, :] = unpack2(lambda i, j, k: ru2[k, j, i], b, q, by)
    for _ in f_gather:
        pass
    unpack3(s["gf3"], fk3.at[0])
    l3.sources(1, 9)
    l3.half("b", l3.v["b"], 1, 9)
    l3.sweep(l3.v["b"], (1, 9), (1, 9))
    l3.residual(1, 9, (0, 32), pair3)
    f4 = coarse4(0.5)
    w4[8] = f4

    def around4(v):
        total = w4[0] * x_below(v) + w4[1] * x_above(v)
        total = total + (w4[2] * roll3(v, 1, 0) + w4[3] * roll3(v, -1, 0))
        return total + (w4[4] * roll3(v, 1, 1) + w4[5] * roll3(v, -1, 1))

    def bottom(i, carry):
        black = carry[1]
        red = w4[6] * (w4[8] + around4(black))
        black = w4[7] * (w4[8] + around4(red))
        return (red, black)

    zero4 = jnp.zeros(shape4, F32)
    red4, black4 = lax.fori_loop(0, BOTTOM, bottom, (zero4, zero4))
    u4 = red4 + black4

    for h in range(2):
        into = jnp.where(lane_r == 64 * h + lane_c // 2, 1.0, 0.0)
        wide4 = spread(u4.reshape(64, 128), into)
        pair3_flat[pl.ds(128 * h, 64, 2), :] = wide4
        pair3_flat[pl.ds(128 * h + 1, 64, 2), :] = wide4
    v3 = l3.v["b"]
    for j in range(1, 9):
        l3.correct(v3, j, pair3[j - 1])
    for _ in range(2):
        l3.sweep(v3, (1, 9), (1, 9))
    for j in range(1, 9):
        u3[2 + 2 * j], u3[3 + 2 * j] = l3.planes(v3, j)

    zoff = jnp.where(lane_c < 64, lane_c, lane_c - 128)
    source_lane = 16 * iz + ((zoff + 128) // 2 - 64)
    spread_z = jnp.where((lane_r == source_lane) & ((lane_c < 64) | (lane_c >= 96)), 1.0, 0.0)
    spread_y = jnp.where(iota((24, 32), 1) == 4 * iy - 4 + iota((24, 32), 0) // 2, 1.0, 0.0)
    stretched = spread(u3[pl.ds(2 * ix, 10)].reshape(320, 128), spread_z)
    side_by_side = jnp.concatenate([stretched[32 * j : 32 * j + 32] for j in range(10)], axis=1)
    corr2 = select_rows(spread_y, side_by_side)
    for j in range(1, 11):
        l2.correct(v2, j, corr2[:, 128 * (j - 1) : 128 * j])
    l2.sweep(v2, (2, 10), (2, 10))
    l2.sweep(v2, (3, 9), (3, 9))

    spread1 = jnp.where(lane_r == jnp.where(lane_c >= 96, 64 + lane_c // 2, lane_c // 2), 1.0, 0.0)
    up1 = s["up1"]
    coarse = []
    for j in range(3, 9):
        coarse += list(l2.planes(v2, j))
    up1[...] = spread(jnp.concatenate(coarse[1:11], axis=0), spread1).reshape(10, 24, 128)
    tall1 = s["tall1"]
    for j in range(1, 11):
        part = up1[j - 1, 4:20, :]
        tall1[j - 1, pl.ds(0, 16, 2), :] = part
        tall1[j - 1, pl.ds(1, 16, 2), :] = part
        l1.correct(v1, j, tall1[j - 1])
    l1.sweep(v1, (1, 11), (2, 10))
    l1.sweep(v1, (2, 10), (3, 9))

    spread0 = jnp.where(iota((128, 256), 0) == iota((128, 256), 1) // 2, 1.0, 0.0)
    up0 = s["up0"]
    coarse = []
    for j in range(3, 9):
        coarse += list(l1.planes(v1, j))
    wide0 = spread(jnp.concatenate(coarse, axis=0), spread0).reshape(12, 32, 256)
    up0[0], up0[1] = wide0[:, :, 0:128], wide0[:, :, 128:256]
    for j in range(1, 13):
        tiles = []
        for t in range(2):
            rows = [up0[t, j - 1, pl.ds(4 + c, 8, 3), :] for c in range(3)]
            tiles.append(jnp.concatenate([rows[c // 2] for c in range(6)], axis=0))
        corr = jnp.concatenate(tiles, axis=1)
        v0[j] = jnp.where(l0.i["b"][j] > 0.0, v0[j] + corr, 0.0)
    l0.sweep(v0, (1, 13), (2, 12))
    l0.half("r", v0, 2, 12)
    outn = s["outn"]

    def last(j):
        black = l0.updated("b", l0.v["r"], j)
        red, even = l0.v["r"][j], l0.even()
        for n, plane in enumerate((jnp.where(even, red, black), jnp.where(even, black, red))):
            for t in range(6):
                outn[2 * j - 6 + n, pl.ds(t, 8, 6), :] = plane[8 * t : 8 * t + 8, 0:128]

    l0.loop(3, 11, last)
    out_ref[...] = outn[:, 8:40, :]
    for sem in sorted(sent):
        if sem not in (0, 2, 4):
            wait(send, sem)


def vmem(*shape):
    return pltpu.VMEM(shape, F32)


def scratch_shapes():
    shapes = {}
    sizes = [(26, 12, 48, 256), (22, 10, 32, 128), (22, 10, 24, 128), (18, 8, 32, 128)]
    for no, (planes, pairs, rows, lanes) in enumerate(sizes):
        shapes[f"fk{no}"] = vmem(2, 2, planes, rows, 128) if no == 0 else vmem(2, planes, rows, lanes)
        names = ["xin", "dr", "db"] + [n + c for n in ("v", "xo", "wy", "wz", "inv", "src") for c in "rb"]
        for name in names + (["v"] if no < 3 else []):
            shapes[f"{name}{no}"] = vmem(pairs + 2, rows, lanes)
    shapes["zp0"], shapes["zr0"] = vmem(2, 2, 32, 128), vmem(2, 3, 2, 48, 128)
    shapes["ze0"], shapes["zs0"] = vmem(2, 32, 128), vmem(2, 3, 48, 128)
    shapes["zpu0"], shapes["zru0"] = vmem(2, 32, 128), vmem(2, 3, 48, 128)
    for name in ("k1", "f1", "pu1"):
        shapes["z" + name] = vmem(2, 16, 128)
    for name in ("zrk1", "zrf1", "zru1"):
        shapes[name] = vmem(2, 3, 32, 128)
    shapes["rf2"] = vmem(5, 3, 3, 8, 128)
    for name in ("rk2", "ru2"):
        shapes[name] = vmem(3, 3, 5, 8, 128)
    for name in "kf":
        shapes[f"g{name}1"] = vmem(8, 8, 128)
        shapes[f"g{name}2"] = vmem(8, 8, 128)
        shapes[f"g{name}3"] = vmem(8, 2, 4, 8, 128)
    shapes["pair0"], shapes["pair1"] = vmem(8, 24, 128), vmem(4, 16, 128)
    shapes["pairk"], shapes["outn"] = vmem(8, 32, 128), vmem(16, 48, 128)
    shapes["vb0n"], shapes["v0n"] = vmem(14, 48, 128), vmem(2, 14, 48, 128)
    shapes["pair2"], shapes["pair3"] = vmem(2, 8, 128), vmem(8, 32, 128)
    shapes["w4"], shapes["u3"] = vmem(9, 4, 16, 128), vmem(24, 32, 128)
    shapes["up0"] = vmem(2, 12, 32, 128)
    shapes["up1"], shapes["tall1"] = vmem(10, 24, 128), vmem(10, 32, 128)
    shapes["dummy"] = vmem(256, 8, 128)
    shapes["send"] = pltpu.SemaphoreType.DMA((26,))
    shapes["recv"] = pltpu.SemaphoreType.DMA((26,))
    shapes["load"] = pltpu.SemaphoreType.DMA((2,))
    return shapes


SCRATCH = scratch_shapes()


def on_device(source_term, conductivity):
    return pl.pallas_call(
        kernel,
        out_shape=jax.ShapeDtypeStruct((16, 32, 128), F32),
        in_specs=[pl.BlockSpec(memory_space=pl.ANY)] * 2,
        out_specs=pl.BlockSpec(memory_space=pltpu.VMEM),
        scratch_shapes=list(SCRATCH.values()),
        compiler_params=pltpu.CompilerParams(
            collective_id=0, has_side_effects=True, vmem_limit_bytes=107 * 2**19
        ),
        name="vcycle",
    )(source_term, conductivity)


def solution(mesh):
    spec = P("gx", "gy", "gz")
    return jax.shard_map(
        on_device, mesh=mesh, in_specs=(spec, spec), out_specs=spec, check_vma=False
    )
```
